32 devices in a mesh: dp: 16 (over z, y, x), blk: 2 (over core).
Axes of the slice: x: 2, y: 2, z: 4, core: 2. Of those that a mesh axis runs over, the one named last changes fastest.
Arguments:
- tokens: bfloat16 [32, 1252, 768], P('dp', 'blk'), may hold values from -6 to 6
- counts: int32 [32], P('dp'), may hold values from 10 to 104, as said below
- attend_gain: bfloat16 [768], P(('dp', 'blk')), may hold values from 0.099609375 to 1.8984375
- attend_shift: bfloat16 [768], P(('dp', 'blk')), may hold values from -2.5 to 2.5
- merged_weight: bfloat16 [768, 2304], P(('dp', 'blk')), may hold values from -0.21875 to 0.21875
- query_bias: bfloat16 [768], P(('dp', 'blk')), may hold values from -3 to 3
- value_bias: bfloat16 [768], P(('dp', 'blk')), may hold values from -3 to 3
- output_weight: bfloat16 [768, 768], P(('dp', 'blk')), may hold values from -0.875 to 0.875
- output_bias: bfloat16 [768], P(('dp', 'blk')), may hold values from -2.5 to 2.5
- feed_gain: bfloat16 [768], P(('dp', 'blk')), may hold values from 0.099609375 to 1.8984375
- feed_shift: bfloat16 [768], P(('dp', 'blk')), may hold values from -2.5 to 2.5
- expand_weight: bfloat16 [768, 3072], P(('dp', 'blk')), may hold values from -0.21875 to 0.21875
- expand_bias: bfloat16 [3072], P(('dp', 'blk')), may hold values from -2.5 to 2.5
- shrink_weight: bfloat16 [3072, 768], P(('dp', 'blk')), may hold values from -0.21875 to 0.21875
- shrink_bias: bfloat16 [768], P(('dp', 'blk')), may hold values from -2.5 to 2.5
- cotangent: bfloat16 [32, 1252, 768], P('dp', 'blk'), may hold values from -6 to 6
Outputs:
- result: bfloat16 [32, 1252, 768], P('dp', 'blk')
- tokens_grad: bfloat16 [32, 1252, 768], P('dp', 'blk')
- attend_gain_grad: float32 [768], P(('dp', 'blk'))
- attend_shift_grad: float32 [768], P(('dp', 'blk'))
- merged_weight_grad: float32 [768, 2304], P(('dp', 'blk'))
- query_bias_grad: float32 [768], P(('dp', 'blk'))
- value_bias_grad: float32 [768], P(('dp', 'blk'))
- output_weight_grad: float32 [768, 768], P(('dp', 'blk'))
- output_bias_grad: float32 [768], P(('dp', 'blk'))
- feed_gain_grad: float32 [768], P(('dp', 'blk'))
- feed_shift_grad: float32 [768], P(('dp', 'blk'))
- expand_weight_grad: float32 [768, 3072], P(('dp', 'blk'))
- expand_bias_grad: float32 [3072], P(('dp', 'blk'))
- shrink_weight_grad: float32 [3072, 768], P(('dp', 'blk'))
- shrink_bias_grad: float32 [768], P(('dp', 'blk'))
The draws below stay inside these ranges and needn't reach their ends.
Inputs may be any that keep to these rules, and one draw needn't show every extreme that they name: `counts`: in every run of 2 clips that share an index of dp, one clip drawn from the seed has more than 52 columns; in the first run that clip has all 104.
All inputs are finite; a program needn't handle non-finite values.
Results may differ from the reference program's by a relative error of at most 0.017.
Values may be sent and summed in bfloat16 or wider, within the bound.
No kernel may reach another device: no remote copies, remote signals or barrier semaphores. Data moves between devices by JAX's collectives and lax.ppermute only.
A program may use at most 320 MiB of HBM per device.

```python
import jax
import jax.numpy as jnp
from jax import lax

D = 768
HEADS = 12
HEAD_DIM = 64
MLP = 3072
FREQ = 12
COLS = 104
COLS_DEV = 52
ROWS_DEV = 626
SEQ = 1252
CLIPS_GRP = 2
CLIPS = 32


def draw_counts(key, part):
    key = jax.random.fold_in(key, 7)
    length_key, pick_key, reach_key = jax.random.split(key, 3)
    lowest = max(1, COLS // 10)
    groups = CLIPS // CLIPS_GRP
    lengths = jax.random.randint(length_key, (CLIPS,), lowest, COLS + 1)
    picked = jax.random.randint(pick_key, (groups,), 0, CLIPS_GRP)
    reaching = jax.random.randint(reach_key, (groups,), COLS - COLS_DEV + 1, COLS + 1)
    reaching = jnp.where(jnp.arange(groups) == 0, COLS, reaching)
    places = jnp.arange(CLIPS) % CLIPS_GRP
    chosen = jnp.repeat(picked, CLIPS_GRP)
    longest = jnp.repeat(reaching, CLIPS_GRP)
    return jnp.where(places == chosen, longest, lengths).astype(jnp.int32)


def block_levels(rng, dims, cuts, smallest, high):
    loudness, own = 1.0, jax.random.fold_in(rng, 6)
    for position, blocks in cuts:
        heights = jnp.exp(jax.random.uniform(jax.random.fold_in(own, position), (blocks,), jnp.float32, smallest / len(cuts), high / len(cuts)))
        loudness = loudness * jnp.repeat(heights, dims[position] // blocks).reshape([-1 if axis == position else 1 for axis in range(len(dims))])
    return loudness


def bell_draw(own_key, dims, scale, most, cuts=(), held_as=jnp.bfloat16):
    drawn = scale * jax.random.normal(own_key, dims, jnp.float32)
    if cuts:
        drawn = drawn * block_levels(own_key, dims, cuts, -0.22, 0.18)
    return jnp.clip(drawn, -most, most).astype(held_as)


def setup_inputs(seed: int = 0) -> dict:
    key_of = jax.random.split(jax.random.key(seed), 17)
    tokens = bell_draw(key_of[0], (CLIPS, SEQ, D), 1.0, 6.0, ((0, 16), (1, 2)))
    counts = draw_counts(jax.random.fold_in(key_of[16], 71), 0)
    attend_gain = jnp.clip(1.0 + 0.18 * jax.random.normal(key_of[2], (D,), jnp.float32), 0.099609375, 1.8984375).astype(jnp.bfloat16)
    attend_shift = bell_draw(key_of[3], (D,), 0.3, 2.5, ((0, 32),))
    merged_weight = bell_draw(key_of[4], (D, 3 * D), D ** -0.5, 0.21875, ((0, 32),))
    query_bias = bell_draw(key_of[5], (D,), 0.5, 3.0, ((0, 32),))
    value_bias = bell_draw(key_of[6], (D,), 0.5, 3.0, ((0, 32),))
    output_weight = bell_draw(key_of[7], (D, D), (D // 16) ** -0.5, 0.875, ((0, 32),))
    output_bias = bell_draw(key_of[8], (D,), 0.3, 2.5, ((0, 32),))
    feed_gain = jnp.clip(1.0 + 0.18 * jax.random.normal(key_of[9], (D,), jnp.float32), 0.099609375, 1.8984375).astype(jnp.bfloat16)
    feed_shift = bell_draw(key_of[10], (D,), 0.3, 2.5, ((0, 32),))
    expand_weight = bell_draw(key_of[11], (D, MLP), D ** -0.5, 0.21875, ((0, 32),))
    expand_bias = bell_draw(key_of[12], (MLP,), 0.3, 2.5, ((0, 32),))
    shrink_weight = bell_draw(key_of[13], (MLP, D), (MLP // 4) ** -0.5, 0.21875, ((0, 32),))
    shrink_bias = bell_draw(key_of[14], (D,), 0.3, 2.5, ((0, 32),))
    cotangent = bell_draw(key_of[15], (CLIPS, SEQ, D), 1.0, 6.0, ((0, 16), (1, 2)))
    return dict(tokens=tokens, counts=counts, attend_gain=attend_gain, attend_shift=attend_shift, merged_weight=merged_weight, query_bias=query_bias, value_bias=value_bias, output_weight=output_weight, output_bias=output_bias, feed_gain=feed_gain, feed_shift=feed_shift, expand_weight=expand_weight, expand_bias=expand_bias, shrink_weight=shrink_weight, shrink_bias=shrink_bias, cotangent=cotangent)


@jax.custom_vjp
def low(v):
    return lax.optimization_barrier(v.astype(jnp.bfloat16)).astype(jnp.float32)

@jax.custom_vjp
def low_back(v):
    return v

def low_keep(v):
    return (low(v), None)

def low_pass(kept, grad):
    return (grad,)

def back_keep(v):
    return (v, None)

def back_low(kept, grad):
    return (low(grad),)
low.defvjp(low_keep, low_pass)
low_back.defvjp(back_keep, back_low)
EPSILON = 1e-06

def layer_norm(values, scale_row, shift_row):
    mean_row = lax.optimization_barrier(jnp.mean(values, axis=-1, keepdims=True))
    centered = values - mean_row
    spread = lax.optimization_barrier(jnp.mean(centered * centered, axis=-1, keepdims=True))
    return centered * lax.rsqrt(spread + EPSILON) * scale_row + shift_row

def highest(left_side, right_side):
    return jnp.dot(left_side, right_side, precision=lax.Precision.HIGHEST)

def valid_keys(clip_count):
    positions = jnp.arange(SEQ, dtype=jnp.int32)
    owner_block = positions // ROWS_DEV
    offset = positions % ROWS_DEV
    column = owner_block * COLS_DEV + (offset - 2) // FREQ
    return jnp.where(offset < 2, owner_block == 0, column < clip_count)

def clip_forward(params, clip_rows, clip_count):
    attend_gain, attend_shift, merged_weight, query_bias, value_bias, output_weight, output_bias, feed_gain, feed_shift, expand_weight, expand_bias, shrink_weight, shrink_bias = params
    attend_input = low(layer_norm(clip_rows, attend_gain, attend_shift))
    merged_rows = highest(attend_input, merged_weight)
    query_rows = low(low_back(merged_rows[:, :D] + query_bias))
    key_rows = low(low_back(merged_rows[:, D:2 * D]))
    value_rows = low(low_back(merged_rows[:, 2 * D:] + value_bias))
    query_heads = query_rows.reshape(SEQ, HEADS, HEAD_DIM)
    key_heads = key_rows.reshape(SEQ, HEADS, HEAD_DIM)
    value_heads = value_rows.reshape(SEQ, HEADS, HEAD_DIM)
    scores = jnp.einsum('qhd,khd->hqk', query_heads, key_heads, precision=lax.Precision.HIGHEST) * HEAD_DIM ** (-0.5)
    scores = low_back(scores)
    visible = valid_keys(clip_count)[None, None, :]
    masked = jnp.where(visible, scores, -1e+30)
    row_top = lax.optimization_barrier(jnp.max(masked, axis=-1, keepdims=True))
    raised = jnp.where(visible, jnp.exp(masked - row_top), 0.0)
    attention = raised / lax.optimization_barrier(jnp.sum(raised, axis=-1, keepdims=True))
    mixture = jnp.einsum('hqk,khd->qhd', low(attention), value_heads, precision=lax.Precision.HIGHEST).reshape(SEQ, D)
    attended = low(low_back(mixture))
    branch = low_back(highest(attended, output_weight) + output_bias)
    middle = clip_rows + branch
    feed_input = low(layer_norm(middle, feed_gain, feed_shift))
    preact = low_back(highest(feed_input, expand_weight) + expand_bias)
    hidden = low(jax.nn.gelu(preact, approximate=False))
    return middle + low_back(highest(hidden, shrink_weight) + shrink_bias)

def forward(tokens_float, counts, params):

    def one_clip(item):
        return jax.checkpoint(clip_forward)(params, item[0], item[1])
    return lax.map(one_clip, (tokens_float, counts))

def reference(tokens, counts, attend_gain, attend_shift, merged_weight, query_bias, value_bias, output_weight, output_bias, feed_gain, feed_shift, expand_weight, expand_bias, shrink_weight, shrink_bias, cotangent):
    weights_in = tuple((weight_item.astype(jnp.float32) for weight_item in (attend_gain, attend_shift, merged_weight, query_bias, value_bias, output_weight, output_bias, feed_gain, feed_shift, expand_weight, expand_bias, shrink_weight, shrink_bias)))

    def whole(inputs, *weight_list):
        return forward(inputs, counts, weight_list)
    result, pull = jax.vjp(whole, tokens.astype(jnp.float32), *weights_in)
    grads = pull(cotangent.astype(jnp.float32))
    return (result.astype(jnp.bfloat16), grads[0].astype(jnp.bfloat16), grads[1], grads[2], grads[3], grads[4], grads[5], grads[6], grads[7], grads[8], grads[9], grads[10], grads[11], grads[12], grads[13])
```

```python
from functools import partial

import jax
import jax.numpy as jnp
from jax import lax
from jax.experimental import pallas as pl
from jax.experimental.pallas import tpu as pltpu
from jax.sharding import PartitionSpec as P

HEADS = 12
HEAD_DIM = 64
FREQ = 12
EPSILON = 1e-06
NEGATIVE = -1e30
LOG2E = 1.4426950408889634
PAIRS = HEADS // 2
LANES = 2 * HEAD_DIM
ROW_GROUP = 8
VMEM_BYTES = 60 * 1024 * 1024

BF = jnp.bfloat16
F32 = jnp.float32

NN = (((1,), (0,)), ((), ()))
NT = (((1,), (1,)), ((), ()))
TN = (((0,), (0,)), ((), ()))


def dot(left, right, dims=NN):
    return lax.dot_general(left, right, dims, preferred_element_type=F32)


def params(count):
    return pltpu.CompilerParams(
        dimension_semantics=("arbitrary",) * count, vmem_limit_bytes=VMEM_BYTES
    )


def whole(shape):
    return pl.BlockSpec(shape, lambda *_: (0,) * len(shape), pipeline_mode=pl.Buffered(1))


def cost(flops, bytes_accessed, transcendentals=0):
    return pl.CostEstimate(
        flops=int(flops), bytes_accessed=int(bytes_accessed), transcendentals=int(transcendentals)
    )


def normed(values):
    mean_row = jnp.mean(values, axis=-1, keepdims=True)
    centered = values - mean_row
    spread = jnp.mean(centered * centered, axis=-1, keepdims=True)
    scale = lax.rsqrt(spread + EPSILON)
    return centered * scale, scale


def norm_back(upstream, gain_row, z, scale):
    w = upstream * gain_row
    return scale * (
        w - jnp.mean(w, axis=-1, keepdims=True) - z * jnp.mean(w * z, axis=-1, keepdims=True)
    )


def fold_rows(values):
    rows, width = values.shape
    return jnp.sum(values.reshape(rows // ROW_GROUP, ROW_GROUP, width), axis=0)


def row_tile(rows):
    return 256 if rows % 256 == 0 else rows


BITS_FIRST = (3, 2, 0, 1)
BITS_SECOND = (3, 2, 1, 0)


def quick_mesh(sizes):
    return sizes["dp"] == 16 and sizes["blk"] == 2


def swap_bit(block, bit):
    return lax.ppermute(block, "dp", [(i, i ^ (1 << bit)) for i in range(lax.axis_size("dp"))])


def sibling(block):
    return lax.ppermute(block, "blk", [(0, 1), (1, 0)])


def spread(block, bits):
    held = block[None]
    for bit in bits:
        held = jnp.concatenate([held, swap_bit(held, bit)], axis=0)
    return held


def relative(slot, bits):
    return sum(((slot >> k) & 1) << bit for k, bit in enumerate(bits))


def slot_of(offset, bits):
    return sum(((offset >> bit) & 1) << k for k, bit in enumerate(bits))


class Gathered:
    def __init__(self, shape, parts):
        self.shape = shape
        self.parts = parts

    @property
    def arrays(self):
        return [part[0] for part in self.parts]

    @property
    def copies(self):
        return sum(1 if bits is None else array.shape[0] for array, bits, _ in self.parts)

    def start(self, refs, target, sems):
        count = 0
        chip = lax.axis_index("dp")
        core = lax.axis_index("blk")
        for ref, (array, bits, place) in zip(refs, self.parts):
            if bits is None:
                pltpu.make_async_copy(ref, target, sems.at[count]).start()
                count += 1
                continue
            slots, rows, cols = array.shape
            for slot in range(slots):
                owner = lax.bitwise_xor(chip, jnp.int32(relative(slot, bits)))
                first_row, first_col = place(owner, core)
                spot = target.at[
                    pl.ds(pl.multiple_of(first_row, 16), rows),
                    pl.ds(pl.multiple_of(first_col, 128), cols),
                ]
                pltpu.make_async_copy(ref.at[slot], spot, sems.at[count]).start()
                count += 1

    def wait(self, refs, target, sems):
        count = 0
        for ref, (array, bits, _) in zip(refs, self.parts):
            if bits is None:
                pltpu.make_async_copy(ref, target, sems.at[count]).wait()
                count += 1
                continue
            slots, rows, cols = array.shape
            for slot in range(slots):
                spot = target.at[pl.ds(0, rows), pl.ds(0, cols)]
                pltpu.make_async_copy(ref.at[slot], spot, sems.at[count]).wait()
                count += 1


def gather_halves(block, cuts):
    rows, cols = block.shape
    half = cols // 2
    core = lax.axis_index("blk")
    mine = lax.dynamic_slice_in_dim(block, core * half, half, axis=1)
    other = sibling(lax.dynamic_slice_in_dim(block, (1 - core) * half, half, axis=1))
    chip_rows = jnp.where(
        core == 0,
        jnp.concatenate([mine, other], axis=0),
        jnp.concatenate([other, mine], axis=0),
    )
    parts = []
    start = 0
    for width, bits in cuts:
        held = spread(chip_rows[:, start : start + width], bits)

        def place(owner, which, start=start, flip=0):
            return owner * (2 * rows), (which ^ flip) * half + start

        parts.append((held, bits, place))
        parts.append((sibling(held), bits, partial(place, flip=1)))
        start += width
    return Gathered((32 * rows, cols), parts)


def gather_rows(block, bits):
    rows, cols = block.shape
    held = spread(block, bits)

    def place(owner, which, flip=0):
        return (owner * 2 + (which ^ flip)) * rows, 0

    parts = [(held, bits, place), (sibling(held), bits, partial(place, flip=1))]
    return Gathered((32 * rows, cols), parts)


def gather_plain(block):
    full = lax.all_gather(block, ("dp", "blk"), axis=0, tiled=True)
    return Gathered(full.shape, [(full, None, None)])


ANYWHERE = pl.BlockSpec(memory_space=pl.ANY)


VEC_COLS = 256


def project_body(*refs, weight):
    count = len(weight.parts)
    x_ref = refs[0]
    sources = refs[1 : 1 + count]
    a_ref, m_ref, w_ref, vec_ref, sems = refs[1 + count :]
    width = x_ref.shape[1]
    first = pl.program_id(0) == 0

    @pl.when(first)
    def _():
        weight.start(sources, w_ref, sems)

    z, _ = normed(x_ref[...].astype(F32))

    @pl.when(first)
    def _():
        weight.wait(sources, w_ref, sems)
        turned = jnp.transpose(w_ref[:, 3 * width : 3 * width + 128].astype(F32))
        vec_ref[...] = turned[:16]

    a = (z * vec_ref[0:1, :] + vec_ref[1:2, :]).astype(BF)
    a_ref[...] = a
    merged = dot(a, w_ref[:, : 3 * width])
    query = (merged[:, :width] + vec_ref[2:3, :]) * (LOG2E * HEAD_DIM**-0.5)
    m_ref[:, :width] = query.astype(BF)
    m_ref[:, width : 2 * width] = merged[:, width : 2 * width].astype(BF)
    m_ref[:, 2 * width :] = (merged[:, 2 * width :] + vec_ref[3:4, :]).astype(BF)


def project(x, weight):
    rows, width = x.shape
    tile = row_tile(rows)
    row = lambda cols: pl.BlockSpec((tile, cols), lambda i: (i, 0))
    return pl.pallas_call(
        partial(project_body, weight=weight),
        grid=(rows // tile,),
        in_specs=[row(width)] + [ANYWHERE] * len(weight.parts),
        out_specs=[row(width), row(3 * width), whole(weight.shape), whole((16, width))],
        out_shape=[
            jax.ShapeDtypeStruct((rows, width), BF),
            jax.ShapeDtypeStruct((rows, 3 * width), BF),
            jax.ShapeDtypeStruct(weight.shape, BF),
            jax.ShapeDtypeStruct((16, width), F32),
        ],
        scratch_shapes=[pltpu.SemaphoreType.DMA((weight.copies,))],
        compiler_params=params(1),
        cost_estimate=cost(6 * rows * width * width, 2 * rows * width * 5 + 6 * width * width),
        name="project",
    )(x, *weight.arrays)


def half_lanes(shape, head):
    return (lax.broadcasted_iota(jnp.int32, shape, 1) < HEAD_DIM) == (head == 0)


def only_head(values, head):
    return jnp.where(half_lanes(values.shape, head), values, jnp.zeros_like(values))


def ones_lane(rows):
    first = lax.broadcasted_iota(jnp.int32, (rows, LANES), 1) == 0
    return jnp.where(first, 1.0, 0.0).astype(BF)


def attend_body(q_ref, k_ref, v_ref, mask_ref, o_ref, sum_ref, *, tile):
    keys = k_ref.shape[1]
    queries = q_ref.shape[1]
    ka = jnp.concatenate([k_ref[0], mask_ref[0]], axis=1)
    v_turned = jnp.transpose(v_ref[0])
    ones = jnp.ones((16, keys), BF)
    va = [
        jnp.concatenate([v_turned[:HEAD_DIM], ones], axis=0),
        jnp.concatenate([v_turned[HEAD_DIM:], ones], axis=0),
    ]
    one = ones_lane(tile)
    for start in range(0, queries, tile):
        q = q_ref[0, start : start + tile, :]
        parts = []
        for head in range(2):
            qa = jnp.concatenate([only_head(q, head), one], axis=1)
            s = dot(ka, qa, NT)
            top = jnp.max(s, axis=0, keepdims=True)
            p = jnp.exp2(s - top).astype(BF)
            mix = dot(va[head], p)
            total = mix[HEAD_DIM : HEAD_DIM + 1]
            parts.append(mix[:HEAD_DIM] / total)
            sum_ref[0, head : head + 1, start : start + tile] = top + jnp.log2(total)
        o_ref[0, start : start + tile, :] = jnp.transpose(jnp.concatenate(parts, axis=0))


def attend(merged, key_merged, key_base, mask, first=0, count=PAIRS):
    clips, queries, _ = merged.shape
    keys = key_merged.shape[1]
    tile = row_tile(queries)
    lanes = lambda rows, base: pl.BlockSpec((1, rows, LANES), lambda c, h: (c, 0, base + h))
    return pl.pallas_call(
        partial(attend_body, tile=tile),
        grid=(clips, count),
        in_specs=[
            lanes(queries, first),
            lanes(keys, key_base + first),
            lanes(keys, key_base + PAIRS + first),
            pl.BlockSpec((1, keys, LANES), lambda c, h: (c, 0, 0)),
        ],
        out_specs=[
            lanes(queries, 0),
            pl.BlockSpec((1, ROW_GROUP, queries), lambda c, h: (c, h, 0)),
        ],
        out_shape=[
            jax.ShapeDtypeStruct((clips, queries, count * LANES), F32),
            jax.ShapeDtypeStruct((clips, count * ROW_GROUP, queries), F32),
        ],
        compiler_params=params(2),
        cost_estimate=cost(
            clips * count * queries * keys * 2 * 4 * 256,
            clips * count * LANES * (2 * queries + 4 * keys + 4 * queries),
            clips * count * queries * keys * 2,
        ),
        name="attend",
    )(merged, key_merged, key_merged, mask)


def attend_back_body(
    q_ref, k_ref, v_ref, do_ref, mask_ref, sum_ref, delta_ref, dq_ref, dk_ref, dv_ref,
    dk_acc, dv_acc, *, tile
):
    queries = q_ref.shape[1]
    k = k_ref[0]
    v = v_ref[0]
    ka = jnp.concatenate([k, mask_ref[0]], axis=1)
    k_turned = jnp.transpose(k)
    one = ones_lane(tile)
    for start in range(0, queries, tile):
        rows = slice(start, start + tile)
        q = q_ref[0, rows, :]
        do = do_ref[0, rows, :]
        q_parts, do_parts, p_parts, ds_parts, dq_parts = [], [], [], [], []
        for head in range(2):
            qm = only_head(q, head)
            dom = only_head(do, head)
            s = dot(ka, jnp.concatenate([qm, one], axis=1), NT)
            p = jnp.exp2(s - sum_ref[0, head : head + 1, rows])
            dp = dot(v, dom, NT)
            ds = (p * (dp - delta_ref[0, head : head + 1, rows])).astype(BF)
            q_parts.append(qm)
            do_parts.append(dom)
            p_parts.append(p.astype(BF))
            ds_parts.append(ds)
            dq_parts.append(dot(k_turned[head * HEAD_DIM : (head + 1) * HEAD_DIM], ds))
        dq = jnp.transpose(jnp.concatenate(dq_parts, axis=0)) * (HEAD_DIM**-0.5)
        dq_ref[0, rows, :] = dq.astype(BF)
        dk = dot(jnp.concatenate(ds_parts, axis=1), jnp.concatenate(q_parts, axis=0))
        dv = dot(jnp.concatenate(p_parts, axis=1), jnp.concatenate(do_parts, axis=0))
        if start == 0:
            dk_acc[...] = dk
            dv_acc[...] = dv
        else:
            dk_acc[...] += dk
            dv_acc[...] += dv
    dk_ref[0] = (dk_acc[...] * (1.0 / LOG2E)).astype(BF)
    dv_ref[0] = dv_acc[...].astype(BF)


def attend_back(merged, key_merged, key_base, grad_out, mask, sums, delta, first=0, count=PAIRS):
    clips, queries, _ = merged.shape
    keys = key_merged.shape[1]
    tile = row_tile(queries)
    lanes = lambda rows, base: pl.BlockSpec((1, rows, LANES), lambda c, h: (c, 0, base + h))
    stat = lambda base: pl.BlockSpec((1, ROW_GROUP, queries), lambda c, h: (c, base + h, 0))
    return pl.pallas_call(
        partial(attend_back_body, tile=tile),
        grid=(clips, count),
        in_specs=[
            lanes(queries, first),
            lanes(keys, key_base + first),
            lanes(keys, key_base + PAIRS + first),
            lanes(queries, first),
            pl.BlockSpec((1, keys, LANES), lambda c, h: (c, 0, 0)),
            stat(0),
            stat(first),
        ],
        out_specs=[lanes(queries, 0), lanes(keys, 0), lanes(keys, 0)],
        out_shape=[
            jax.ShapeDtypeStruct((clips, queries, count * LANES), BF),
            jax.ShapeDtypeStruct((clips, keys, count * LANES), BF),
            jax.ShapeDtypeStruct((clips, keys, count * LANES), BF),
        ],
        scratch_shapes=[pltpu.VMEM((keys, LANES), F32), pltpu.VMEM((keys, LANES), F32)],
        compiler_params=params(2),
        cost_estimate=cost(
            clips * count * queries * keys * 2 * 9 * 256,
            clips * count * LANES * 2 * (3 * queries + 4 * keys),
            clips * count * queries * keys * 2,
        ),
        name="attend_back",
    )(merged, key_merged, key_merged, grad_out, mask, sums, delta)


ERF = (0.254829592, -0.284496736, 1.421413741, -1.453152027, 1.061405429)
ERF_P = 0.3275911


def gelu_both(u):
    bell = jnp.exp2(u * u * (-0.5 * LOG2E))
    t = 1.0 / (1.0 + (ERF_P * 0.5**0.5) * jnp.abs(u))
    series = ERF[4] * 0.5
    for term in ERF[3::-1]:
        series = series * t + term * 0.5
    tail = series * t * bell
    chance = jnp.where(u >= 0, 1.0 - tail, tail)
    return u * chance, chance + u * bell * 0.3989422804014327


def feed_body(*refs, chunk, mixes, wide, tall):
    x_ref, g_ref = refs[:2]
    o_refs = refs[2 : 2 + mixes]
    at = 2 + mixes
    wide_refs = refs[at : at + len(wide.parts)]
    at += len(wide.parts)
    tall_refs = refs[at : at + len(tall.parts)]
    at += len(tall.parts)
    (
        vecs_ref, be_ref, sel_ref,
        result_ref, h_ref, gp_ref, gm_ref, att_ref, gb_ref, fi_ref, ga_ref, delta_ref, vec_ref,
        ebg_ref, wide_w, tall_w, wide_sems, tall_sems,
    ) = refs[at:]
    width = x_ref.shape[1]
    hidden_width = be_ref.shape[1]
    we_ref = wide_w.at[:, :hidden_width]
    wo_ref = wide_w.at[:, hidden_width:]
    ws_ref = tall_w

    @pl.when(pl.program_id(0) == 0)
    def _():
        wide.start(wide_refs, wide_w, wide_sems)
        tall.start(tall_refs, tall_w, tall_sems)
        vec_ref[...] = jnp.zeros_like(vec_ref)
        ebg_ref[...] = jnp.zeros_like(ebg_ref)
        wide.wait(wide_refs, wide_w, wide_sems)
        tall.wait(tall_refs, tall_w, tall_sems)

    o = jnp.concatenate([ref[...] for ref in o_refs], axis=1)
    att = o.astype(BF)
    att_ref[...] = att
    middle = x_ref[...].astype(F32) + dot(att, wo_ref[...]) + vecs_ref[4:5, :]
    z, scale = normed(middle)
    gain = vecs_ref[5:6, :]
    fi = (z * gain + vecs_ref[6:7, :]).astype(BF)
    fi_ref[...] = fi
    g = g_ref[...]
    out = middle + vecs_ref[7:8, :]
    u = jnp.zeros_like(middle)
    for start in range(0, hidden_width, chunk):
        cols = slice(start, start + chunk)
        pre = dot(fi, we_ref[:, cols]) + be_ref[:, cols]
        gh = dot(g, ws_ref[cols, :], NT)
        act, slope = gelu_both(pre)
        act = act.astype(BF)
        gp = (gh * slope).astype(BF)
        h_ref[:, cols] = act
        gp_ref[:, cols] = gp
        ebg_ref[:, cols] += fold_rows(gp.astype(F32))
        out += dot(act, ws_ref[cols, :])
        u += dot(gp, we_ref[:, cols], NT)
    result_ref[...] = out.astype(BF)
    gf = g.astype(F32)
    gm = gf + norm_back(u, gain, z, scale)
    gm_ref[...] = gm
    gb = gm.astype(BF)
    gb_ref[...] = gb
    ga = dot(gb, wo_ref[...], NT).astype(BF)
    ga_ref[...] = ga
    prod = ga.astype(F32) * o
    high = prod.astype(BF)
    low = (prod - high.astype(F32)).astype(BF)
    sel = sel_ref[...]
    delta_ref[...] = dot(sel, high, NT) + dot(sel, low, NT)
    vec_ref[:, :width] += fold_rows(u * z)
    vec_ref[:, width : 2 * width] += fold_rows(u)
    vec_ref[:, 2 * width : 3 * width] += fold_rows(gb.astype(F32))
    vec_ref[:, 3 * width :] += fold_rows(gf)


def feed(x, g, mixtures, wide, tall, vecs, be):
    rows, width = x.shape
    hidden_width = be.shape[1]
    tile = row_tile(rows)
    lane_head = jnp.arange(width)[None, :] // HEAD_DIM
    stat_row = jnp.arange(PAIRS * ROW_GROUP)[:, None]
    chosen = (stat_row // ROW_GROUP * 2 + stat_row % ROW_GROUP == lane_head) & (
        stat_row % ROW_GROUP < 2
    )
    select = chosen.astype(BF)
    row = lambda cols: pl.BlockSpec((tile, cols), lambda i: (i, 0))
    keep = lambda cols: pl.BlockSpec((ROW_GROUP, cols), lambda i: (0, 0))
    shape = jax.ShapeDtypeStruct
    return pl.pallas_call(
        partial(feed_body, chunk=512, mixes=len(mixtures), wide=wide, tall=tall),
        grid=(rows // tile,),
        in_specs=[
            row(width), row(width), *[row(mixture.shape[1]) for mixture in mixtures],
            *[ANYWHERE] * (len(wide.parts) + len(tall.parts)),
            whole(vecs.shape), whole((1, hidden_width)), whole(select.shape),
        ],
        out_specs=[
            row(width), row(hidden_width), row(hidden_width), row(width), row(width), row(width),
            row(width), row(width),
            pl.BlockSpec((PAIRS * ROW_GROUP, tile), lambda i: (0, i)),
            keep(4 * width), keep(hidden_width),
        ],
        out_shape=[
            shape((rows, width), BF), shape((rows, hidden_width), BF),
            shape((rows, hidden_width), BF), shape((rows, width), F32), shape((rows, width), BF),
            shape((rows, width), BF), shape((rows, width), BF), shape((rows, width), BF),
            shape((PAIRS * ROW_GROUP, rows), F32),
            shape((ROW_GROUP, 4 * width), F32), shape((ROW_GROUP, hidden_width), F32),
        ],
        scratch_shapes=[
            pltpu.VMEM(wide.shape, BF), pltpu.VMEM(tall.shape, BF),
            pltpu.SemaphoreType.DMA((wide.copies,)), pltpu.SemaphoreType.DMA((tall.copies,)),
        ],
        compiler_params=params(1),
        cost_estimate=cost(
            rows * width * (4 * width + 8 * hidden_width),
            rows * (width * 20 + hidden_width * 4) + 2 * width * (width + 2 * hidden_width),
            rows * hidden_width * 2,
        ),
        name="feed",
    )(x, g, *mixtures, *wide.arrays, *tall.arrays, vecs, be, select)


def lay_out(value, first_device, keep_ref, send_ref, rows, bits):
    chip = lax.axis_index("dp")
    core = lax.axis_index("blk")
    for index in range(value.shape[0] // rows):
        device = first_device + index
        slot = slot_of(lax.bitwise_xor(chip, device // 2), bits)
        block = value[index * rows : (index + 1) * rows].astype(keep_ref.dtype)

        @pl.when(core == index % 2)
        def _():
            keep_ref[slot] = block

        @pl.when(core != index % 2)
        def _():
            send_ref[slot] = block


def outer_tall_body(left_ref, right_ref, *outs, rows, bits):
    value = dot(left_ref[...], right_ref[...], TN)
    if bits is None:
        outs[0][...] = value.astype(outs[0].dtype)
    else:
        first = pl.program_id(0) * (value.shape[0] // rows)
        lay_out(value, first, outs[0], outs[1], rows, bits)


def outer_tall(left, right, rows, bits, dtype=BF):
    length, many = left.shape
    few = right.shape[1]
    chunk = 384
    if bits is None:
        out_specs = [pl.BlockSpec((chunk, few), lambda i: (i, 0))]
        out_shape = [jax.ShapeDtypeStruct((many, few), dtype)]
    else:
        shape = (many // (2 * rows), rows, few)
        out_specs = [pl.BlockSpec(shape, lambda i: (0, 0, 0))] * 2
        out_shape = [jax.ShapeDtypeStruct(shape, dtype)] * 2
    return pl.pallas_call(
        partial(outer_tall_body, rows=rows, bits=bits),
        grid=(many // chunk,),
        in_specs=[pl.BlockSpec((length, chunk), lambda i: (0, i)), whole((length, few))],
        out_specs=out_specs,
        out_shape=out_shape,
        compiler_params=params(1),
        cost_estimate=cost(2 * length * many * few, 2 * length * (many + few) + 2 * many * few),
        name="outer_tall",
    )(left, right)


def outer_wide_body(left_ref, *refs, pieces, rows, bits):
    right_refs = refs[:pieces]
    outs = refs[pieces:-1]
    turned = refs[-1]

    @pl.when(pl.program_id(0) == 0)
    def _():
        turned[...] = jnp.transpose(left_ref[...])

    if pieces == 1:
        right = right_refs[0][...]
    else:
        right = jnp.concatenate([ref[...] for ref in right_refs], axis=1)
    value = dot(turned[...], right)
    if bits is None:
        outs[0][...] = value.astype(outs[0].dtype)
    else:
        lay_out(value, 0, outs[0], outs[1], rows, bits)


def outer_wide(left, rights, rows, bits, dtype=BF):
    length, few = left.shape
    many = sum(right.shape[1] for right in rights)
    pieces = len(rights)
    chunk = 512 if pieces == 1 and many % 512 == 0 else many
    if bits is None:
        out_specs = [pl.BlockSpec((few, chunk), lambda i: (0, i))]
        out_shape = [jax.ShapeDtypeStruct((few, many), dtype)]
    else:
        slots = few // (2 * rows)
        out_specs = [pl.BlockSpec((slots, rows, chunk), lambda i: (0, 0, i))] * 2
        out_shape = [jax.ShapeDtypeStruct((slots, rows, many), dtype)] * 2
    return pl.pallas_call(
        partial(outer_wide_body, pieces=pieces, rows=rows, bits=bits),
        grid=(many // chunk,),
        in_specs=[whole((length, few))]
        + [
            pl.BlockSpec((length, chunk if pieces == 1 else right.shape[1]), lambda i: (0, i))
            for right in rights
        ],
        out_specs=out_specs,
        out_shape=out_shape,
        scratch_shapes=[pltpu.VMEM((few, length), BF)],
        compiler_params=params(1),
        cost_estimate=cost(2 * length * many * few, 2 * length * (many + few) + 2 * many * few),
        name="outer_wide",
    )(left, *rights)


def collect(grads, bits):
    if bits is None:
        return lax.psum_scatter(
            grads[0].astype(F32), ("dp", "blk"), scatter_dimension=0, tiled=True
        )
    held, sent = grads
    arrived = sibling(sent)
    for k in range(len(bits))[::-1]:
        half = 1 << k
        away = (held[half:].astype(F32) + arrived[half:].astype(F32)).astype(BF)
        held = (held[:half].astype(F32) + arrived[:half].astype(F32)).astype(BF)
        arrived = swap_bit(away, bits[k])
    return (held.astype(F32) + arrived.astype(F32))[0]


def collect_small(table):
    sizes = {"dp": lax.axis_size("dp"), "blk": lax.axis_size("blk")}
    if not quick_mesh(sizes):
        return lax.psum_scatter(table, ("dp", "blk"), scatter_dimension=0, tiled=True)[0]
    chip = lax.axis_index("dp")
    core = lax.axis_index("blk")
    held = table
    for bit in (3, 2, 1, 0):
        pairs = held.reshape(2, held.shape[0] // 2, held.shape[1])
        mine = (chip >> bit) & 1
        keep = jnp.where(mine == 0, pairs[0], pairs[1])
        away = jnp.where(mine == 0, pairs[1], pairs[0])
        held = keep + swap_bit(away, bit)
    keep = jnp.where(core == 0, held[0], held[1])
    away = jnp.where(core == 0, held[1], held[0])
    return keep + sibling(away)


def unproject_body(*refs, pieces):
    parts = [[ref[...] for ref in refs[pieces * k : pieces * (k + 1)]] for k in range(3)]
    w_ref, x_ref, vecs_ref, gm_ref, tg_ref, vec_ref = refs[3 * pieces :]
    width = x_ref.shape[1]

    @pl.when(pl.program_id(0) == 0)
    def _():
        vec_ref[...] = jnp.zeros_like(vec_ref)

    grads = [part[0] if pieces == 1 else jnp.concatenate(part, axis=1) for part in parts]
    u = dot(jnp.concatenate(grads, axis=1), w_ref[:, : 3 * width], NT)
    z, scale = normed(x_ref[...].astype(F32))
    back = norm_back(u, vecs_ref[0:1, :], z, scale)
    tg_ref[...] = (gm_ref[...] + back).astype(BF)
    vec_ref[:, :width] += fold_rows(u * z)
    vec_ref[:, width : 2 * width] += fold_rows(u)
    vec_ref[:, 2 * width : 3 * width] += fold_rows(grads[0].astype(F32))
    vec_ref[:, 3 * width :] += fold_rows(grads[2].astype(F32))


def unproject(dq, dk, dv, weight, x, vecs, gm):
    rows, width = x.shape
    tile = row_tile(rows)
    row = lambda cols: pl.BlockSpec((tile, cols), lambda i: (i, 0))
    grads = [*dq, *dk, *dv]
    return pl.pallas_call(
        partial(unproject_body, pieces=len(dq)),
        grid=(rows // tile,),
        in_specs=[row(grad.shape[1]) for grad in grads]
        + [whole(weight.shape), row(width), whole(vecs.shape), row(width)],
        out_specs=[row(width), pl.BlockSpec((ROW_GROUP, 4 * width), lambda i: (0, 0))],
        out_shape=[
            jax.ShapeDtypeStruct((rows, width), BF),
            jax.ShapeDtypeStruct((ROW_GROUP, 4 * width), F32),
        ],
        compiler_params=params(1),
        cost_estimate=cost(6 * rows * width * width, 2 * rows * width * 8 + 6 * width * width),
        name="unproject",
    )(*grads, weight, x, vecs, gm)


def pad_rows(values, rows):
    return jnp.pad(values, ((0, 0), (0, rows - values.shape[1]), (0, 0)))


def trade_clips(values):
    if lax.axis_size("blk") != 2:
        return lax.all_to_all(values, "blk", 0, 1, tiled=True)
    clips, rows, width = values.shape
    core = lax.axis_index("blk")
    pairs = values.reshape(2, clips // 2, rows, width)
    low, high = pairs[0], pairs[1]
    mine = jnp.where(core == 0, low, high)
    other = sibling(jnp.where(core == 0, high, low))
    return jnp.concatenate(
        [jnp.where(core == 0, mine, other), jnp.where(core == 0, other, mine)], axis=1
    )


def trade_back(values):
    if lax.axis_size("blk") != 2:
        return lax.all_to_all(values, "blk", 1, 0, tiled=True)
    clips, rows, width = values.shape
    core = lax.axis_index("blk")
    low, high = values[:, : rows // 2], values[:, rows // 2 :]
    mine = jnp.where(core == 0, low, high)
    other = sibling(jnp.where(core == 0, high, low))
    return jnp.concatenate(
        [jnp.where(core == 0, mine, other), jnp.where(core == 0, other, mine)], axis=0
    )


def key_mask(counts, cycle, rows_dev, rows_pad):
    position = jnp.arange(cycle * rows_pad, dtype=jnp.int32)
    block = position // rows_pad
    offset = position % rows_pad
    column = block * ((rows_dev - 2) // FREQ) + (offset - 2) // FREQ
    seen = jnp.where(
        (offset < 2)[None, :], (block == 0)[None, :], column[None, :] < counts[:, None]
    ) & (offset < rows_dev)[None, :]
    lane = jnp.arange(LANES, dtype=jnp.int32)
    return jnp.where(seen[:, :, None] | (lane > 0)[None, None, :], 0.0, NEGATIVE).astype(BF)


GROUPS = ((0, 2), (2, 2), (4, 2))


def local(
    tokens, counts, attend_gain, attend_shift, merged_weight, query_bias, value_bias,
    output_weight, output_bias, feed_gain, feed_shift, expand_weight, expand_bias,
    shrink_weight, shrink_bias, cotangent,
):
    clips, rows_dev, width = tokens.shape
    chips, cycle = lax.axis_size("dp"), lax.axis_size("blk")
    quick = quick_mesh({"dp": chips, "blk": cycle})
    rows_pad = -(-rows_dev // 16) * 16
    traded = clips % cycle == 0
    weight_rows = merged_weight.shape[0]
    tall_rows = shrink_weight.shape[0]
    hidden_width = expand_weight.shape[1]

    bias_cols = expand_bias.reshape(weight_rows, -1)
    vec_cols = jnp.stack(
        [
            attend_gain, attend_shift, query_bias, value_bias,
            output_bias, feed_gain, feed_shift, shrink_bias,
        ],
        axis=1,
    )
    extra = jnp.concatenate([vec_cols, bias_cols], axis=1)
    extra = jnp.pad(extra, ((0, 0), (0, VEC_COLS - extra.shape[1])))
    first_pack = jnp.concatenate([merged_weight, extra], axis=1)
    wide_pack = jnp.concatenate([expand_weight, output_weight], axis=1)
    if quick:
        cut = first_pack.shape[1] // 4
        merged_full = gather_halves(first_pack, ((cut, BITS_FIRST), (cut, BITS_SECOND)))
        wide = gather_halves(wide_pack, ((wide_pack.shape[1] // 2, BITS_FIRST),))
        tall = gather_rows(shrink_weight, BITS_SECOND)
    else:
        merged_full = gather_plain(first_pack)
        wide = gather_plain(wide_pack)
        tall = gather_plain(shrink_weight)

    x = pad_rows(tokens, rows_pad)
    g = pad_rows(cotangent, rows_pad)
    if traded:
        x = trade_clips(x)
        g = trade_clips(g)
        held = clips // cycle
        own_counts = lax.dynamic_slice_in_dim(counts, lax.axis_index("blk") * held, held)
    else:
        held = clips
        own_counts = counts
    queries = x.shape[1]
    total = held * queries
    x = x.reshape(total, width)
    g = g.reshape(total, width)
    mask = key_mask(own_counts, cycle, rows_dev, rows_pad)

    attend_input, merged, weight_flat, vecs = project(x, merged_full)
    bias_row = vecs[8 : 8 + bias_cols.shape[1]].T.reshape(1, hidden_width)
    merged = merged.reshape(held, queries, 3 * width)
    if traded:
        keys, key_base = merged, PAIRS
    else:
        keys = lax.all_gather(merged[:, :, width:], "blk", axis=1, tiled=True)
        key_base = 0
    mixtures, sums = [], []
    for first, count in GROUPS:
        mixture, log_total = attend(merged, keys, key_base, mask, first, count)
        mixtures.append(mixture.reshape(total, count * LANES))
        sums.append(log_total)
    (
        result, hidden, grad_preact, grad_middle, attended, grad_branch, feed_input, grad_attended,
        delta, feed_vec, expand_vec,
    ) = feed(x, g, mixtures, wide, tall, vecs, bias_row)

    first_bits, second_bits = (BITS_FIRST, BITS_SECOND) if quick else (None, None)
    shrink_grad = collect(outer_tall(hidden, g, tall_rows, second_bits), second_bits)
    expand_grad = collect(outer_wide(feed_input, [grad_preact], weight_rows, first_bits), first_bits)
    output_grad = collect(outer_wide(attended, [grad_branch], weight_rows, second_bits), second_bits)
    delta = delta.reshape(PAIRS * ROW_GROUP, held, queries).transpose(1, 0, 2)
    grad_heads = grad_attended.reshape(held, queries, width)
    dq, dk, dv = [], [], []
    for (first, count), log_total in zip(GROUPS, sums):
        parts = attend_back(merged, keys, key_base, grad_heads, mask, log_total, delta, first, count)
        if not traded:
            parts = (
                parts[0],
                lax.psum_scatter(parts[1], "blk", scatter_dimension=1, tiled=True),
                lax.psum_scatter(parts[2], "blk", scatter_dimension=1, tiled=True),
            )
        for into, part in zip((dq, dk, dv), parts):
            into.append(part.reshape(total, count * LANES))
    query_grad = collect(outer_wide(attend_input, dq, weight_rows, first_bits), first_bits)
    key_grad = collect(outer_wide(attend_input, dk, weight_rows, second_bits), second_bits)
    value_grad = collect(outer_wide(attend_input, dv, weight_rows, first_bits), first_bits)
    tokens_grad, attend_vec = unproject(dq, dk, dv, weight_flat, x, vecs, grad_middle)

    devices = chips * cycle
    rows_of = lambda values: jnp.sum(values, axis=0).reshape(-1, devices, weight_rows)
    small = jnp.concatenate([rows_of(attend_vec), rows_of(feed_vec)], axis=0)
    small = small.transpose(1, 0, 2).reshape(devices, 8 * weight_rows)
    small = jnp.concatenate([small, jnp.sum(expand_vec, axis=0).reshape(devices, -1)], axis=1)
    small = collect_small(small)
    vec = lambda k: small[k * weight_rows : (k + 1) * weight_rows]

    def home(values):
        values = values.reshape(held, queries, width)
        if traded:
            values = trade_back(values)
        return values[:, :rows_dev]

    return (
        home(result),
        home(tokens_grad),
        vec(0),
        vec(1),
        jnp.concatenate([query_grad, key_grad, value_grad], axis=1),
        vec(2),
        vec(3),
        output_grad,
        vec(6),
        vec(4),
        vec(5),
        expand_grad,
        small[8 * weight_rows :],
        shrink_grad,
        vec(7),
    )


def solution(mesh):
    rows = P("dp", "blk", None)
    vector = P(("dp", "blk"))
    matrix = P(("dp", "blk"), None)
    in_specs = (
        rows, P("dp"), vector, vector, matrix, vector, vector, matrix, vector, vector, vector,
        matrix, vector, matrix, vector, rows,
    )
    out_specs = (
        rows, rows, vector, vector, matrix, vector, vector, matrix, vector, vector, vector,
        matrix, vector, matrix, vector,
    )
    return jax.shard_map(local, mesh=mesh, in_specs=in_specs, out_specs=out_specs, check_vma=False)
```

```python
from functools import partial

import jax
import jax.numpy as jnp
from jax import lax
from jax.experimental import pallas as pl
from jax.experimental.pallas import tpu as pltpu
from jax.sharding import PartitionSpec as P

HEADS = 12
HEAD_DIM = 64
FREQ = 12
EPSILON = 1e-06
NEGATIVE = -1e30
LOG2E = 1.4426950408889634
PAIRS = HEADS // 2
LANES = 2 * HEAD_DIM
ROW_GROUP = 8
VMEM_BYTES = 60 * 1024 * 1024

BF = jnp.bfloat16
F32 = jnp.float32

NN = (((1,), (0,)), ((), ()))
NT = (((1,), (1,)), ((), ()))
TN = (((0,), (0,)), ((), ()))


def dot(left, right, dims=NN):
    return lax.dot_general(left, right, dims, preferred_element_type=F32)


def params(count):
    return pltpu.CompilerParams(
        dimension_semantics=("arbitrary",) * count, vmem_limit_bytes=VMEM_BYTES
    )


def whole(shape):
    return pl.BlockSpec(shape, lambda *_: (0,) * len(shape), pipeline_mode=pl.Buffered(1))


def cost(flops, bytes_accessed, transcendentals=0):
    return pl.CostEstimate(
        flops=int(flops), bytes_accessed=int(bytes_accessed), transcendentals=int(transcendentals)
    )


def normed(values):
    mean_row = jnp.mean(values, axis=-1, keepdims=True)
    centered = values - mean_row
    spread = jnp.mean(centered * centered, axis=-1, keepdims=True)
    scale = lax.rsqrt(spread + EPSILON)
    return centered * scale, scale


def norm_back(upstream, gain_row, z, scale):
    w = upstream * gain_row
    return scale * (
        w - jnp.mean(w, axis=-1, keepdims=True) - z * jnp.mean(w * z, axis=-1, keepdims=True)
    )


def fold_rows(values):
    rows, width = values.shape
    return jnp.sum(values.reshape(rows // ROW_GROUP, ROW_GROUP, width), axis=0)


def row_tile(rows):
    return 256 if rows % 256 == 0 else rows


BITS_FIRST = (3, 2, 0, 1)
BITS_SECOND = (3, 2, 1, 0)


def after(value, *others):
    return lax.optimization_barrier((value, *others))[0]


def quick_mesh(sizes):
    return sizes["dp"] == 16 and sizes["blk"] == 2


def swap_bit(block, bit):
    return lax.ppermute(block, "dp", [(i, i ^ (1 << bit)) for i in range(lax.axis_size("dp"))])


def sibling(block):
    return lax.ppermute(block, "blk", [(0, 1), (1, 0)])


def grow(held, bit, *others):
    return jnp.concatenate([held, after(swap_bit(held, bit), *others)], axis=0)


def relative(slot, bits):
    return sum(((slot >> k) & 1) << bit for k, bit in enumerate(bits))


def slot_of(offset, bits):
    return sum(((offset >> bit) & 1) << k for k, bit in enumerate(bits))


def beside(moves, kernel, operand):
    came = [route(array) for array, route in moves]
    results = kernel(after(operand, *[array for array, _ in moves]))
    joined = lax.optimization_barrier((*came, *results))
    return joined[: len(came)], joined[len(came) :]


def over(bit):
    return partial(swap_bit, bit=bit)


class Gathered:
    def __init__(self, arrays, shape, blocked, moves):
        self.arrays = arrays
        self.shape = shape
        self.blocked = blocked
        self.moves = moves

    @property
    def count(self):
        return len(self.arrays)

    def start(self, refs, target, sems):
        for index, (source, spot) in enumerate(self.moves(refs, target)):
            pltpu.make_async_copy(source, spot, sems.at[index]).start()

    def wait(self, refs, target, sems):
        for index, (source, spot) in enumerate(self.moves(refs, target)):
            pltpu.make_async_copy(source, spot, sems.at[index]).wait()

    def columns(self, ref, cols):
        if not self.blocked:
            return ref[:, cols]
        block = ref[:, :, cols]
        return block.reshape(block.shape[0] * block.shape[1], block.shape[2])

    def rows(self, ref, cols):
        if not self.blocked:
            return ref[cols, :]
        of_device = ref.shape[1] * ref.shape[2]
        block = ref[cols.start // of_device : cols.stop // of_device]
        return block.reshape(cols.stop - cols.start, block.shape[3])


def plain(array):
    return Gathered([array], array.shape, False, lambda refs, target: [(refs[0], target)])


def gathered_first(one, two, rows):
    slots, _, cols = one.shape
    arrays = [one, sibling(one), two, sibling(two)]

    def moves(refs, target):
        chip = lax.axis_index("dp")
        core = lax.axis_index("blk")
        pairs = []
        for index, ref in enumerate(refs):
            bits = BITS_FIRST if index < 2 else BITS_SECOND
            which = core if index % 2 == 0 else 1 - core
            place = pl.ds(index // 2 * cols, cols)
            for slot in range(slots):
                owner = lax.bitwise_xor(chip, jnp.int32(relative(slot, bits)))
                pairs.append((ref.at[slot], target.at[owner * 2 + which, :, place]))
        return pairs

    return Gathered(arrays, (2 * slots, rows, 2 * cols), True, moves)


ANYWHERE = pl.BlockSpec(memory_space=pl.ANY)


VEC_COLS = 256


def project_body(*refs, weight):
    count = weight.count
    x_ref = refs[0]
    sources = refs[1 : 1 + count]
    zt_ref, m_ref, w_ref, vec_ref, sems = refs[1 + count :]
    width = x_ref.shape[1]
    first = pl.program_id(0) == 0

    @pl.when(first)
    def _():
        weight.start(sources, w_ref, sems)

    z, _ = normed(x_ref[...].astype(F32))
    zt_ref[...] = jnp.transpose(z.astype(BF))

    @pl.when(first)
    def _():
        weight.wait(sources, w_ref, sems)
        extra = weight.columns(w_ref, slice(3 * width, 3 * width + 128))
        turned = jnp.transpose(extra.astype(F32))
        vec_ref[...] = turned[:16]

    a = (z * vec_ref[0:1, :] + vec_ref[1:2, :]).astype(BF)
    merged = dot(a, weight.columns(w_ref, slice(0, 3 * width)))
    query = (merged[:, :width] + vec_ref[2:3, :]) * (LOG2E * HEAD_DIM**-0.5)
    m_ref[:, :width] = query.astype(BF)
    m_ref[:, width : 2 * width] = merged[:, width : 2 * width].astype(BF)
    m_ref[:, 2 * width :] = (merged[:, 2 * width :] + vec_ref[3:4, :]).astype(BF)


def project(x, weight):
    rows, width = x.shape
    tile = row_tile(rows)
    row = lambda cols: pl.BlockSpec((tile, cols), lambda i: (i, 0))
    return pl.pallas_call(
        partial(project_body, weight=weight),
        grid=(rows // tile,),
        in_specs=[row(width)] + [ANYWHERE] * weight.count,
        out_specs=[
            pl.BlockSpec((width, tile), lambda i: (0, i)),
            row(3 * width), whole(weight.shape), whole((16, width)),
        ],
        out_shape=[
            jax.ShapeDtypeStruct((width, rows), BF),
            jax.ShapeDtypeStruct((rows, 3 * width), BF),
            jax.ShapeDtypeStruct(weight.shape, BF),
            jax.ShapeDtypeStruct((16, width), F32),
        ],
        scratch_shapes=[pltpu.SemaphoreType.DMA((64,))],
        compiler_params=params(1),
        cost_estimate=cost(6 * rows * width * width, 2 * rows * width * 5 + 6 * width * width),
        name="project",
    )(x, *weight.arrays)


def half_lanes(shape, head):
    return (lax.broadcasted_iota(jnp.int32, shape, 1) < HEAD_DIM) == (head == 0)


def only_head(values, head):
    return jnp.where(half_lanes(values.shape, head), values, jnp.zeros_like(values))


def ones_lane(rows):
    first = lax.broadcasted_iota(jnp.int32, (rows, LANES), 1) == 0
    return jnp.where(first, 1.0, 0.0).astype(BF)


def attend_body(q_ref, k_ref, v_ref, mask_ref, o_ref, sum_ref, *, tile):
    keys = k_ref.shape[1]
    queries = q_ref.shape[1]
    ka = jnp.concatenate([k_ref[0], mask_ref[0]], axis=1)
    v_turned = jnp.transpose(v_ref[0])
    ones = jnp.ones((16, keys), BF)
    va = [
        jnp.concatenate([v_turned[:HEAD_DIM], ones], axis=0),
        jnp.concatenate([v_turned[HEAD_DIM:], ones], axis=0),
    ]
    one = ones_lane(tile)
    for start in range(0, queries, tile):
        q = q_ref[0, start : start + tile, :]
        parts = []
        for head in range(2):
            qa = jnp.concatenate([only_head(q, head), one], axis=1)
            s = dot(ka, qa, NT)
            top = jnp.max(s, axis=0, keepdims=True)
            p = jnp.exp2(s - top).astype(BF)
            mix = dot(va[head], p)
            total = mix[HEAD_DIM : HEAD_DIM + 1]
            parts.append(mix[:HEAD_DIM] / total)
            sum_ref[0, head : head + 1, start : start + tile] = top + jnp.log2(total)
        o_ref[0, start : start + tile, :] = jnp.transpose(jnp.concatenate(parts, axis=0))


def attend(merged, key_merged, key_base, mask, first=0, count=PAIRS):
    clips, queries, _ = merged.shape
    keys = key_merged.shape[1]
    tile = row_tile(queries)
    lanes = lambda rows, base: pl.BlockSpec((1, rows, LANES), lambda c, h: (c, 0, base + h))
    return pl.pallas_call(
        partial(attend_body, tile=tile),
        grid=(clips, count),
        in_specs=[
            lanes(queries, first),
            lanes(keys, key_base + first),
            lanes(keys, key_base + PAIRS + first),
            pl.BlockSpec((1, keys, LANES), lambda c, h: (c, 0, 0)),
        ],
        out_specs=[
            lanes(queries, 0),
            pl.BlockSpec((1, ROW_GROUP, queries), lambda c, h: (c, h, 0)),
        ],
        out_shape=[
            jax.ShapeDtypeStruct((clips, queries, count * LANES), F32),
            jax.ShapeDtypeStruct((clips, count * ROW_GROUP, queries), F32),
        ],
        compiler_params=params(2),
        cost_estimate=cost(
            clips * count * queries * keys * 2 * 4 * 256,
            clips * count * LANES * (2 * queries + 4 * keys + 4 * queries),
            clips * count * queries * keys * 2,
        ),
        name="attend",
    )(merged, key_merged, key_merged, mask)


def attend_back_body(
    q_ref, k_ref, v_ref, do_ref, mask_ref, sum_ref, delta_ref, *rest, tile
):
    dk_acc, dv_acc = rest[-2:]
    if len(rest) == 3:
        dq_ref, dk_ref, dv_ref = (rest[0].at[0, k] for k in range(3))
    else:
        dq_ref, dk_ref, dv_ref = (ref.at[0] for ref in rest[:3])
    queries = q_ref.shape[1]
    k = k_ref[0]
    v = v_ref[0]
    ka = jnp.concatenate([k, mask_ref[0]], axis=1)
    k_turned = jnp.transpose(k)
    one = ones_lane(tile)
    for start in range(0, queries, tile):
        rows = slice(start, start + tile)
        q = q_ref[0, rows, :]
        do = do_ref[0, rows, :]
        q_parts, do_parts, p_parts, ds_parts, dq_parts = [], [], [], [], []
        for head in range(2):
            qm = only_head(q, head)
            dom = only_head(do, head)
            s = dot(ka, jnp.concatenate([qm, one], axis=1), NT)
            p = jnp.exp2(s - sum_ref[0, head : head + 1, rows])
            dp = dot(v, dom, NT)
            ds = (p * (dp - delta_ref[0, head : head + 1, rows])).astype(BF)
            q_parts.append(qm)
            do_parts.append(dom)
            p_parts.append(p.astype(BF))
            ds_parts.append(ds)
            dq_parts.append(dot(k_turned[head * HEAD_DIM : (head + 1) * HEAD_DIM], ds))
        dq = jnp.transpose(jnp.concatenate(dq_parts, axis=0)) * (HEAD_DIM**-0.5)
        dq_ref[rows, :] = dq.astype(BF)
        dk = dot(jnp.concatenate(ds_parts, axis=1), jnp.concatenate(q_parts, axis=0))
        dv = dot(jnp.concatenate(p_parts, axis=1), jnp.concatenate(do_parts, axis=0))
        if start == 0:
            dk_acc[...] = dk
            dv_acc[...] = dv
        else:
            dk_acc[...] += dk
            dv_acc[...] += dv
    dk_ref[...] = (dk_acc[...] * (1.0 / LOG2E)).astype(BF)
    dv_ref[...] = dv_acc[...].astype(BF)


def attend_back(merged, key_merged, key_base, grad_out, mask, sums, delta, first=0, count=PAIRS):
    clips, queries, _ = merged.shape
    keys = key_merged.shape[1]
    tile = row_tile(queries)
    lanes = lambda rows, base: pl.BlockSpec((1, rows, LANES), lambda c, h: (c, 0, base + h))
    stat = lambda base: pl.BlockSpec((1, ROW_GROUP, queries), lambda c, h: (c, base + h, 0))
    columns = count * LANES
    if queries == keys:
        out_specs = [pl.BlockSpec((1, 3, keys, LANES), lambda c, h: (c, 0, 0, h))]
        out_shape = [jax.ShapeDtypeStruct((clips, 3, keys, columns), BF)]
    else:
        out_specs = [lanes(queries, 0), lanes(keys, 0), lanes(keys, 0)]
        out_shape = [
            jax.ShapeDtypeStruct((clips, queries, columns), BF),
            jax.ShapeDtypeStruct((clips, keys, columns), BF),
            jax.ShapeDtypeStruct((clips, keys, columns), BF),
        ]
    return pl.pallas_call(
        partial(attend_back_body, tile=tile),
        grid=(clips, count),
        in_specs=[
            lanes(queries, first),
            lanes(keys, key_base + first),
            lanes(keys, key_base + PAIRS + first),
            lanes(queries, first),
            pl.BlockSpec((1, keys, LANES), lambda c, h: (c, 0, 0)),
            stat(first),
            stat(first),
        ],
        out_specs=out_specs,
        out_shape=out_shape,
        scratch_shapes=[pltpu.VMEM((keys, LANES), F32), pltpu.VMEM((keys, LANES), F32)],
        compiler_params=params(2),
        cost_estimate=cost(
            clips * count * queries * keys * 2 * 9 * 256,
            clips * count * LANES * 2 * (3 * queries + 4 * keys),
            clips * count * queries * keys * 2,
        ),
        name="attend_back",
    )(merged, key_merged, key_merged, grad_out, mask, sums, delta)


ERF = (0.254829592, -0.284496736, 1.421413741, -1.453152027, 1.061405429)
ERF_P = 0.3275911


def gelu_both(u):
    bell = jnp.exp2(u * u * (-0.5 * LOG2E))
    t = 1.0 / (1.0 + (ERF_P * 0.5**0.5) * jnp.abs(u))
    series = ERF[4] * 0.5
    for term in ERF[3::-1]:
        series = series * t + term * 0.5
    tail = series * t * bell
    chance = jnp.where(u >= 0, 1.0 - tail, tail)
    return u * chance, chance + u * bell * 0.3989422804014327


def feed_body(*refs, chunk, mixes, wide, tall):
    x_ref, g_ref = refs[:2]
    o_refs = refs[2 : 2 + mixes]
    at = 2 + mixes
    wide_refs = refs[at : at + wide.count]
    at += wide.count
    tall_refs = refs[at : at + tall.count]
    at += tall.count
    (
        vecs_ref, be_ref, sel_ref,
        result_ref, h_ref, right_ref, gm_ref, left_ref, ga_ref, delta_ref, vec_ref,
        ebg_ref, wide_w, tall_w, wide_sems, tall_sems,
    ) = refs[at:]
    width = x_ref.shape[1]
    hidden_width = be_ref.shape[1]
    all_output = slice(hidden_width, hidden_width + width)

    @pl.when(pl.program_id(0) == 0)
    def _():
        wide.start(wide_refs, wide_w, wide_sems)
        tall.start(tall_refs, tall_w, tall_sems)
        vec_ref[...] = jnp.zeros_like(vec_ref)
        ebg_ref[...] = jnp.zeros_like(ebg_ref)
        wide.wait(wide_refs, wide_w, wide_sems)
        tall.wait(tall_refs, tall_w, tall_sems)

    o = jnp.concatenate([ref[...] for ref in o_refs], axis=1)
    att = o.astype(BF)
    left_ref[1] = jnp.transpose(att)
    middle = x_ref[...].astype(F32) + dot(att, wide.columns(wide_w, all_output)) + vecs_ref[4:5, :]
    z, scale = normed(middle)
    gain = vecs_ref[5:6, :]
    fi = (z * gain + vecs_ref[6:7, :]).astype(BF)
    left_ref[0] = jnp.transpose(fi)
    g = g_ref[...]
    out = middle + vecs_ref[7:8, :]
    u = jnp.zeros_like(middle)
    for start in range(0, hidden_width, chunk):
        cols = slice(start, start + chunk)
        we = wide.columns(wide_w, cols)
        ws = tall.rows(tall_w, cols)
        pre = dot(fi, we) + be_ref[:, cols]
        gh = dot(g, ws, NT)
        act, slope = gelu_both(pre)
        act = act.astype(BF)
        gp = (gh * slope).astype(BF)
        h_ref[:, cols] = act
        right_ref[:, cols] = gp
        ebg_ref[:, cols] += fold_rows(gp.astype(F32))
        out += dot(act, ws)
        u += dot(gp, we, NT)
    result_ref[...] = out.astype(BF)
    gf = g.astype(F32)
    gm = gf + norm_back(u, gain, z, scale)
    gm_ref[...] = gm
    gb = gm.astype(BF)
    right_ref[:, hidden_width:] = gb
    ga = dot(gb, wide.columns(wide_w, all_output), NT).astype(BF)
    ga_ref[...] = ga
    prod = ga.astype(F32) * o
    high = prod.astype(BF)
    low = (prod - high.astype(F32)).astype(BF)
    sel = sel_ref[...]
    delta_ref[...] = dot(sel, high, NT) + dot(sel, low, NT)
    vec_ref[:, :width] += fold_rows(u * z)
    vec_ref[:, width : 2 * width] += fold_rows(u)
    vec_ref[:, 2 * width : 3 * width] += fold_rows(gb.astype(F32))
    vec_ref[:, 3 * width :] += fold_rows(gf)


def feed(x, g, mixtures, wide, tall, vecs, be):
    rows, width = x.shape
    hidden_width = be.shape[1]
    tile = row_tile(rows)
    lane_head = jnp.arange(width)[None, :] // HEAD_DIM
    stat_row = jnp.arange(PAIRS * ROW_GROUP)[:, None]
    chosen = (stat_row // ROW_GROUP * 2 + stat_row % ROW_GROUP == lane_head) & (
        stat_row % ROW_GROUP < 2
    )
    select = chosen.astype(BF)
    row = lambda cols: pl.BlockSpec((tile, cols), lambda i: (i, 0))
    keep = lambda cols: pl.BlockSpec((ROW_GROUP, cols), lambda i: (0, 0))
    shape = jax.ShapeDtypeStruct
    return pl.pallas_call(
        partial(feed_body, chunk=768, mixes=len(mixtures), wide=wide, tall=tall),
        grid=(rows // tile,),
        in_specs=[
            row(width), row(width), *[row(mixture.shape[1]) for mixture in mixtures],
            *[ANYWHERE] * (wide.count + tall.count),
            whole(vecs.shape), whole((1, hidden_width)), whole(select.shape),
        ],
        out_specs=[
            row(width), row(hidden_width), row(hidden_width + width), row(width),
            pl.BlockSpec((2, width, tile), lambda i: (0, 0, i)), row(width),
            pl.BlockSpec((PAIRS * ROW_GROUP, tile), lambda i: (0, i)),
            keep(4 * width), keep(hidden_width),
        ],
        out_shape=[
            shape((rows, width), BF), shape((rows, hidden_width), BF),
            shape((rows, hidden_width + width), BF), shape((rows, width), F32),
            shape((2, width, rows), BF), shape((rows, width), BF),
            shape((PAIRS * ROW_GROUP, rows), F32),
            shape((ROW_GROUP, 4 * width), F32), shape((ROW_GROUP, hidden_width), F32),
        ],
        scratch_shapes=[
            pltpu.VMEM(wide.shape, BF), pltpu.VMEM(tall.shape, BF),
            pltpu.SemaphoreType.DMA((4,)), pltpu.SemaphoreType.DMA((4,)),
        ],
        compiler_params=params(1),
        cost_estimate=cost(
            rows * width * (4 * width + 8 * hidden_width),
            rows * (width * 20 + hidden_width * 4) + 2 * width * (width + 2 * hidden_width),
            rows * hidden_width * 2,
        ),
        name="feed",
    )(x, g, *mixtures, *wide.arrays, *tall.arrays, vecs, be, select)


def lay_out(value_ref, value_cols, outs, out_cols, rows, bits):
    if bits is None:
        outs[0][:, out_cols] = value_ref[:, value_cols].astype(BF)
        return
    keep_ref, send_ref = outs
    chip = lax.axis_index("dp")
    core = lax.axis_index("blk")
    for slot in range(keep_ref.shape[0]):
        owner = lax.bitwise_xor(chip, jnp.int32(relative(slot, bits)))
        for ref, which in ((keep_ref, core), (send_ref, 1 - core)):
            first = pl.multiple_of((owner * 2 + which) * rows, 8)
            ref[slot, :, out_cols] = value_ref[pl.ds(first, rows), value_cols].astype(BF)


def laid_out(few, columns, rows, bits):
    if bits is None:
        shapes = [(few, columns)]
    else:
        shapes = [(few // (2 * rows), rows, columns)] * 2
    return (
        [whole(shape) for shape in shapes],
        [jax.ShapeDtypeStruct(shape, BF) for shape in shapes],
    )


def outer_tall_body(left_ref, right_ref, *outs, rows, blocks, bits):
    value = dot(left_ref[...], right_ref[...], TN)
    if bits is None:
        outs[0][...] = value.astype(BF)
        return
    keep_ref, send_ref, value_ref = outs
    value_ref[...] = value
    chip = lax.axis_index("dp")
    core = lax.axis_index("blk")
    few = value.shape[1]
    chips = value.shape[0] // (2 * blocks * rows)
    for index in range(chips):
        owner = pl.program_id(0) * chips + index
        slot = slot_of(lax.bitwise_xor(chip, owner), bits)
        for ref, which in ((keep_ref, core), (send_ref, 1 - core)):
            for k in range(blocks):
                first = pl.multiple_of(((index * 2 + which) * blocks + k) * rows, 8)
                ref[slot, :, k * few : (k + 1) * few] = value_ref[pl.ds(first, rows), :].astype(BF)


def outer_tall(left, right, rows, blocks, bits):
    length, many = left.shape
    few = right.shape[1]
    chunk = 768
    if bits is None:
        out_specs = [pl.BlockSpec((chunk, few), lambda i: (i, 0))]
        out_shape = [jax.ShapeDtypeStruct((many, few), BF)]
        scratch = []
    else:
        shape = (many // (2 * blocks * rows), rows, blocks * few)
        out_specs = [whole(shape)] * 2
        out_shape = [jax.ShapeDtypeStruct(shape, BF)] * 2
        scratch = [pltpu.VMEM((chunk, few), F32)]
    return pl.pallas_call(
        partial(outer_tall_body, rows=rows, blocks=blocks, bits=bits),
        grid=(many // chunk,),
        in_specs=[pl.BlockSpec((length, chunk), lambda i: (0, i)), whole((length, few))],
        out_specs=out_specs,
        out_shape=out_shape,
        scratch_shapes=scratch,
        compiler_params=params(1),
        cost_estimate=cost(2 * length * many * few, 2 * length * (many + few) + 2 * many * few),
        name="outer_tall",
    )(left, right)


def outer_wide_body(left_ref, right_ref, vec_ref, col_ref, *outs, rows, bits):
    value_ref = outs[-1]
    outs = outs[:-1]
    step = pl.program_id(0)
    width = right_ref.shape[1]
    value_ref[...] = dot(left_ref[0], right_ref[...])
    cols = pl.ds(pl.multiple_of(step * width, 128), width)
    lay_out(value_ref, slice(None), outs, cols, rows, bits)

    @pl.when(step == pl.num_programs(0) - 1)
    def _():
        sums = [
            jnp.sum(vec_ref[:, k * width : (k + 1) * width], axis=0, keepdims=True)
            for k in range(4)
        ]
        table = jnp.concatenate(sums + [jnp.zeros((124, width), F32)], axis=0)
        value_ref[:, :128] = jnp.transpose(table) + col_ref[...]
        lay_out(value_ref, slice(0, 128), outs, slice(5 * width, 5 * width + 128), rows, bits)


def outer_wide(left, right, vec, cols, rows, bits):
    _, few, length = left.shape
    columns = right.shape[1]
    steps = columns // few
    out_specs, out_shape = laid_out(few, columns + 128, rows, bits)
    return pl.pallas_call(
        partial(outer_wide_body, rows=rows, bits=bits),
        grid=(steps,),
        in_specs=[
            pl.BlockSpec((1, few, length), lambda i: (i // (steps - 1), 0, 0)),
            pl.BlockSpec((length, few), lambda i: (0, i)),
            whole(vec.shape),
            whole(cols.shape),
        ],
        out_specs=out_specs,
        out_shape=out_shape,
        scratch_shapes=[pltpu.VMEM((few, few), F32)],
        compiler_params=params(1),
        cost_estimate=cost(
            2 * length * few * columns, 2 * length * (2 * few + columns) + 2 * few * columns
        ),
        name="outer_wide",
    )(left, right, vec, cols)


def outer_merged_body(left_ref, w_ref, extra_ref, *refs, pieces, rows, bits):
    right_refs = refs[:pieces]
    outs = refs[pieces:-2]
    value_ref, side_ref = refs[-2:]
    step = pl.program_id(0)
    width = left_ref.shape[0]
    rights = [ref[0] for ref in right_refs]
    right = rights[0] if pieces == 1 else jnp.concatenate(rights, axis=1)
    z_grad = dot(left_ref[...], right)
    total = jnp.sum(fold_rows(right.astype(F32)), axis=0, keepdims=True)
    gain = extra_ref[:, 0:1].astype(F32)
    shift = extra_ref[:, 1:2].astype(F32)
    value_ref[...] = gain * z_grad + shift * total
    cols = pl.ds(pl.multiple_of(step * width, 128), width)
    lay_out(value_ref, slice(None), outs, cols, rows, bits)
    w = w_ref[...].astype(F32)
    gain_grad = jnp.sum(w * z_grad, axis=1, keepdims=True)
    shift_grad = jnp.sum(w * total, axis=1, keepdims=True)
    turned = jnp.transpose(
        jnp.concatenate([total, jnp.zeros((127, width), F32)], axis=0)
    )[:, :1]
    lane = lax.broadcasted_iota(jnp.int32, (width, 128), 1)
    zero = jnp.zeros((), F32)
    bias_lane = jnp.where(step == 0, 2, jnp.where(step == 1, 4, 3))
    side = (
        jnp.where(lane == 0, gain_grad, zero)
        + jnp.where(lane == 1, shift_grad, zero)
        + jnp.where(lane == bias_lane, turned, zero)
    )

    @pl.when(step == 0)
    def _():
        side_ref[...] = side

    @pl.when(step > 0)
    def _():
        side_ref[...] += side

    @pl.when(step == 2)
    def _():
        lay_out(side_ref, slice(None), outs, slice(3 * width, 3 * width + 128), rows, bits)


def outer_merged(left, weight, grads, rows, bits):
    few, length = left.shape
    out_specs, out_shape = laid_out(few, 3 * few + 128, rows, bits)
    return pl.pallas_call(
        partial(outer_merged_body, pieces=len(grads), rows=rows, bits=bits),
        grid=(3,),
        in_specs=[
            whole(left.shape),
            pl.BlockSpec((few, few), lambda i: (0, i)),
            pl.BlockSpec((few, 128), lambda i: (0, 3 * few // 128)),
        ]
        + [pl.BlockSpec((1, length, grad.shape[2]), lambda i: (i, 0, 0)) for grad in grads],
        out_specs=out_specs,
        out_shape=out_shape,
        scratch_shapes=[pltpu.VMEM((few, few), F32), pltpu.VMEM((few, 128), F32)],
        compiler_params=params(1),
        cost_estimate=cost(6 * length * few * few, 8 * length * few + 12 * few * few),
        name="outer_merged",
    )(left, weight, weight, *grads)


def added(left, right):
    return (left.astype(F32) + right.astype(F32)).astype(BF)


def collect_plain(grads):
    total = lax.psum_scatter(grads, ("dp", "blk"), scatter_dimension=0, tiled=True)
    return total.astype(F32)


def halved(held):
    half = held.shape[0] // 2
    return held[:half], held[half:]


def shrink(held, bit):
    half = held.shape[0] // 2
    return held[:half], swap_bit(held[half:], bit)


def unproject_body(*refs, pieces):
    part_refs = refs[:pieces]
    w_ref, x_ref, vecs_ref, gm_ref, tg_ref = refs[pieces:]
    width = x_ref.shape[1]
    grads = [ref[k] for k in range(3) for ref in part_refs]
    u = dot(jnp.concatenate(grads, axis=1), w_ref[:, : 3 * width], NT)
    z, scale = normed(x_ref[...].astype(F32))
    back = norm_back(u, vecs_ref[0:1, :], z, scale)
    tg_ref[...] = (gm_ref[...] + back).astype(BF)


def unproject(grads, weight, x, vecs, gm):
    rows, width = x.shape
    tile = row_tile(rows)
    row = lambda cols: pl.BlockSpec((tile, cols), lambda i: (i, 0))
    return pl.pallas_call(
        partial(unproject_body, pieces=len(grads)),
        grid=(rows // tile,),
        in_specs=[pl.BlockSpec((3, tile, grad.shape[2]), lambda i: (0, i, 0)) for grad in grads]
        + [whole(weight.shape), row(width), whole(vecs.shape), row(width)],
        out_specs=row(width),
        out_shape=jax.ShapeDtypeStruct((rows, width), BF),
        compiler_params=params(1),
        cost_estimate=cost(6 * rows * width * width, 2 * rows * width * 8 + 6 * width * width),
        name="unproject",
    )(*grads, weight, x, vecs, gm)


def pad_rows(values, rows):
    return jnp.pad(values, ((0, 0), (0, rows - values.shape[1]), (0, 0)))


def trade_clips(values):
    if lax.axis_size("blk") != 2:
        return lax.all_to_all(values, "blk", 0, 1, tiled=True)
    clips, rows, width = values.shape
    core = lax.axis_index("blk")
    pairs = values.reshape(2, clips // 2, rows, width)
    low, high = pairs[0], pairs[1]
    mine = jnp.where(core == 0, low, high)
    other = sibling(jnp.where(core == 0, high, low))
    return jnp.concatenate(
        [jnp.where(core == 0, mine, other), jnp.where(core == 0, other, mine)], axis=1
    )


def trade_back(values):
    if lax.axis_size("blk") != 2:
        return lax.all_to_all(values, "blk", 1, 0, tiled=True)
    clips, rows, width = values.shape
    core = lax.axis_index("blk")
    low, high = values[:, : rows // 2], values[:, rows // 2 :]
    mine = jnp.where(core == 0, low, high)
    other = sibling(jnp.where(core == 0, high, low))
    return jnp.concatenate(
        [jnp.where(core == 0, mine, other), jnp.where(core == 0, other, mine)], axis=0
    )


def key_mask(counts, cycle, rows_dev, rows_pad):
    position = jnp.arange(cycle * rows_pad, dtype=jnp.int32)
    block = position // rows_pad
    offset = position % rows_pad
    column = block * ((rows_dev - 2) // FREQ) + (offset - 2) // FREQ
    seen = jnp.where(
        (offset < 2)[None, :], (block == 0)[None, :], column[None, :] < counts[:, None]
    ) & (offset < rows_dev)[None, :]
    lane = jnp.arange(LANES, dtype=jnp.int32)
    return jnp.where(seen[:, :, None] | (lane > 0)[None, None, :], 0.0, NEGATIVE).astype(BF)


GROUPS = ((0, 1), (1, 3), (4, 2))


def local(
    tokens, counts, attend_gain, attend_shift, merged_weight, query_bias, value_bias,
    output_weight, output_bias, feed_gain, feed_shift, expand_weight, expand_bias,
    shrink_weight, shrink_bias, cotangent,
):
    clips, rows_dev, width = tokens.shape
    chips, cycle = lax.axis_size("dp"), lax.axis_size("blk")
    quick = quick_mesh({"dp": chips, "blk": cycle})
    rows_pad = -(-rows_dev // 16) * 16
    traded = clips % cycle == 0
    weight_rows = merged_weight.shape[0]
    tall_rows = shrink_weight.shape[0]
    hidden_width = expand_weight.shape[1]
    devices = chips * cycle
    core = lax.axis_index("blk")
    bias_cols = expand_bias.reshape(weight_rows, -1)
    vec_rows = jnp.stack(
        [
            attend_gain, attend_shift, query_bias, value_bias,
            output_bias, feed_gain, feed_shift, shrink_bias,
        ]
    )
    extra = jnp.concatenate([vec_rows.T, bias_cols], axis=1)
    extra = jnp.pad(extra, ((0, 0), (0, VEC_COLS - extra.shape[1])))
    first_pack = jnp.concatenate([merged_weight, extra], axis=1)
    wide_pack = jnp.concatenate([expand_weight, output_weight], axis=1)
    if quick:
        blocks = tall_rows // weight_rows
        rest = jnp.concatenate(
            [wide_pack]
            + [shrink_weight[k * weight_rows : (k + 1) * weight_rows] for k in range(blocks)],
            axis=1,
        )
        held_first = grow(first_pack[None], 3)
        held_first = grow(held_first, 2)
        rest = lax.all_gather(after(rest, held_first), ("dp", "blk"), axis=0)
        wide_cols = wide_pack.shape[1]
        wide = Gathered(
            [rest],
            (devices, weight_rows, wide_cols),
            True,
            lambda refs, target: [(refs[0].at[:, :, :wide_cols], target)],
        )
        tall = Gathered(
            [rest],
            (devices, blocks, weight_rows, width),
            True,
            lambda refs, target: [
                (refs[0].at[:, :, pl.ds(wide_cols + k * width, width)], target.at[:, k])
                for k in range(blocks)
            ],
        )
        cut = first_pack.shape[1] // 2
        one = grow(held_first[:, :, :cut], 0)
        two = grow(held_first[:, :, cut:], 1)
    else:
        gather = lambda block: plain(lax.all_gather(block, ("dp", "blk"), axis=0, tiled=True))
        merged_full = gather(first_pack)
        wide = gather(wide_pack)
        tall = gather(shrink_weight)
    if quick:
        x = trade_clips(pad_rows(tokens, rows_pad))
        one = grow(one, 1, x)
        two = grow(two, 0, x)
        g = trade_clips(pad_rows(after(cotangent, one, two), rows_pad))
        merged_full = gathered_first(one, two, weight_rows)
    else:
        x = pad_rows(tokens, rows_pad)
        g = pad_rows(cotangent, rows_pad)
        if traded:
            x = trade_clips(x)
            g = trade_clips(g)
    held = clips // cycle if traded else clips
    own_counts = lax.dynamic_slice_in_dim(counts, core * held, held) if traded else counts
    queries = x.shape[1]
    total = held * queries
    x = x.reshape(total, width)
    g = g.reshape(total, width)
    mask = key_mask(own_counts, cycle, rows_dev, rows_pad)

    z_turned, merged, weight_flat, vecs = project(x, merged_full)
    weight_flat = weight_flat.reshape(devices * weight_rows, -1)
    bias_row = vecs[8 : 8 + bias_cols.shape[1]].T.reshape(1, hidden_width)
    merged = merged.reshape(held, queries, 3 * width)
    if traded:
        keys, key_base = merged, PAIRS
    else:
        keys = lax.all_gather(merged[:, :, width:], "blk", axis=1, tiled=True)
        key_base = 0
    mixture, sums = attend(merged, keys, key_base, mask)
    mixtures = [mixture.reshape(total, width)]
    (
        result, hidden, rights, grad_middle, lefts, grad_attended, delta, feed_vec, expand_vec,
    ) = feed(x, g, mixtures, wide, tall, vecs, bias_row)

    bits = BITS_FIRST if quick else None
    cols = jnp.pad(jnp.sum(expand_vec, axis=0).reshape(width, -1), ((0, 0), (4, 120)))
    wide_grad = outer_wide(lefts, rights, feed_vec, cols, weight_rows, bits)
    delta = delta.reshape(PAIRS * ROW_GROUP, held, queries).transpose(1, 0, 2)
    grad_heads = grad_attended.reshape(held, queries, width)
    blocks = tall_rows // weight_rows
    back = partial(attend_back, merged, keys, key_base)
    if quick:
        wide_keep, wide_send = wide_grad
        (wide_came,), (tall_keep, tall_send) = beside(
            [(wide_send, sibling)],
            lambda rows: outer_tall(rows, g, weight_rows, blocks, BITS_SECOND),
            hidden,
        )
        wide_held = added(wide_keep, wide_came)

        def back_group(index):
            first, count = GROUPS[index]
            return lambda rows: back(rows, mask, sums, delta, first, count)

        grads = []
        (tall_came,), part = beside(
            [(tall_send, sibling)], back_group(0), after(grad_heads, wide_held)
        )
        grads += part
        tall_held = added(tall_keep, tall_came)
        for index, bit in ((1, 1), (2, 0)):
            wide_kept, wide_away = halved(wide_held)
            tall_kept, tall_away = halved(tall_held)
            (wide_came, tall_came), part = beside(
                [(wide_away, over(bit)), (tall_away, over(1 - bit))],
                back_group(index),
                after(grad_heads, grads[-1]),
            )
            grads += part
            wide_held = added(wide_kept, wide_came)
            tall_held = added(tall_kept, tall_came)
        grads = [
            part.transpose(1, 0, 2, 3).reshape(3, total, part.shape[3]) for part in grads
        ]
        wide_kept, wide_away = halved(wide_held)
        tall_kept, tall_away = halved(tall_held)
        (wide_came, tall_came), (merged_keep, merged_send) = beside(
            [(wide_away, over(2)), (tall_away, over(2))],
            lambda rows: outer_merged(rows, weight_flat, grads, weight_rows, bits),
            z_turned,
        )
        merged_came = sibling(merged_send)
        wide_kept, wide_away = halved(added(wide_kept, wide_came))
        tall_kept, tall_away = halved(added(tall_kept, tall_came))
        merged_held = added(merged_keep, merged_came).reshape(
            2, 2, chips // 4, weight_rows, merged_keep.shape[2]
        )
        cut = merged_held.shape[-1] // 256 * 128
        one, two = merged_held[..., :cut], merged_held[..., cut:]
        (one_came, two_came, wide_came, tall_came), (tokens_grad,) = beside(
            [
                (one[1], over(1)), (two[:, 1], over(0)),
                (wide_away, over(3)), (tall_away, over(3)),
            ],
            lambda rows: [unproject(grads, weight_flat, rows, vecs, grad_middle)],
            x,
        )
        one = added(one[0], one_came)
        two = added(two[:, 0], two_came)
        one_came = swap_bit(one[1], 0)
        two_came = swap_bit(two[1], 1)
        one = added(one[0], one_came)
        two = added(two[0], two_came)
        merged_held = jnp.concatenate([one, two], axis=-1)
        merged_held = added(*shrink(merged_held, 2))
        full = lambda kept, came: (kept.astype(F32) + came.astype(F32))[0]
        merged_grad = full(*shrink(merged_held, 3))
        wide_grad = full(wide_kept, wide_came)
        tall_grad = full(tall_kept, tall_came)
        shrink_grad = jnp.concatenate(
            [tall_grad[:, k * width : (k + 1) * width] for k in range(blocks)], axis=0
        )
    else:
        shrink_grad = collect_plain(outer_tall(hidden, g, weight_rows, blocks, None)[0])
        columns = []
        for first, count in GROUPS:
            parts = back(grad_heads, mask, sums, delta, first, count)
            if traded:
                parts = [parts[0][:, k] for k in range(3)]
            else:
                scatter = partial(
                    lax.psum_scatter, axis_name="blk", scatter_dimension=1, tiled=True
                )
                parts = [parts[0], scatter(parts[1]), scatter(parts[2])]
            columns.append(jnp.stack(parts))
        grads = [jnp.concatenate(columns, axis=3).reshape(3, total, width)]
        merged_grad = outer_merged(z_turned, weight_flat, grads, weight_rows, None)
        tokens_grad = unproject(grads, weight_flat, x, vecs, grad_middle)
        merged_grad = collect_plain(merged_grad[0])
        wide_grad = collect_plain(wide_grad[0])
    vec_wide = wide_grad[:, 5 * width :]
    vec_merged = merged_grad[:, 3 * width :]

    def home(values):
        values = values.reshape(held, queries, width)
        if traded:
            values = trade_back(values)
        return values[:, :rows_dev]

    return (
        home(result),
        home(tokens_grad),
        vec_merged[:, 0],
        vec_merged[:, 1],
        merged_grad[:, : 3 * width],
        vec_merged[:, 2],
        vec_merged[:, 3],
        wide_grad[:, hidden_width : hidden_width + width],
        vec_wide[:, 2],
        vec_wide[:, 0],
        vec_wide[:, 1],
        wide_grad[:, :hidden_width],
        vec_wide[:, 4:8].reshape(-1),
        shrink_grad,
        vec_wide[:, 3],
    )


def solution(mesh):
    rows = P("dp", "blk", None)
    vector = P(("dp", "blk"))
    matrix = P(("dp", "blk"), None)
    in_specs = (
        rows, P("dp"), vector, vector, matrix, vector, vector, matrix, vector, vector, vector,
        matrix, vector, matrix, vector, rows,
    )
    out_specs = (
        rows, rows, vector, vector, matrix, vector, vector, matrix, vector, vector, vector,
        matrix, vector, matrix, vector,
    )
    return jax.shard_map(local, mesh=mesh, in_specs=in_specs, out_specs=out_specs, check_vma=False)
```

```python
from functools import partial

import jax
import jax.numpy as jnp
from jax import lax
from jax.experimental import pallas as pl
from jax.experimental.pallas import tpu as pltpu
from jax.sharding import PartitionSpec as P

HEADS = 12
HEAD_DIM = 64
FREQ = 12
EPSILON = 1e-06
NEGATIVE = -1e30
LOG2E = 1.4426950408889634
PAIRS = HEADS // 2
LANES = 2 * HEAD_DIM
ROW_GROUP = 8
VMEM_BYTES = 60 * 1024 * 1024

BF = jnp.bfloat16
F32 = jnp.float32

NN = (((1,), (0,)), ((), ()))
NT = (((1,), (1,)), ((), ()))
TN = (((0,), (0,)), ((), ()))


def dot(left, right, dims=NN):
    return lax.dot_general(left, right, dims, preferred_element_type=F32)


def params(count):
    return pltpu.CompilerParams(
        dimension_semantics=("arbitrary",) * count, vmem_limit_bytes=VMEM_BYTES
    )


def whole(shape):
    return pl.BlockSpec(shape, lambda *_: (0,) * len(shape), pipeline_mode=pl.Buffered(1))


def cost(flops, bytes_accessed, transcendentals=0):
    return pl.CostEstimate(
        flops=int(flops), bytes_accessed=int(bytes_accessed), transcendentals=int(transcendentals)
    )


def normed(values):
    mean_row = jnp.mean(values, axis=-1, keepdims=True)
    centered = values - mean_row
    spread = jnp.mean(centered * centered, axis=-1, keepdims=True)
    scale = lax.rsqrt(spread + EPSILON)
    return centered * scale, scale


def norm_back(upstream, gain_row, z, scale):
    w = upstream * gain_row
    return scale * (
        w - jnp.mean(w, axis=-1, keepdims=True) - z * jnp.mean(w * z, axis=-1, keepdims=True)
    )


def fold_rows(values):
    rows, width = values.shape
    return jnp.sum(values.reshape(rows // ROW_GROUP, ROW_GROUP, width), axis=0)


def row_tile(rows):
    return 256 if rows % 256 == 0 else rows


BITS_FIRST = (3, 2, 0, 1)
BITS_SECOND = (3, 2, 1, 0)


def after(value, *others):
    return lax.optimization_barrier((value, *others))[0]


def quick_mesh(sizes):
    return sizes["dp"] == 16 and sizes["blk"] == 2


def swap_bit(block, bit):
    return lax.ppermute(block, "dp", [(i, i ^ (1 << bit)) for i in range(lax.axis_size("dp"))])


def sibling(block):
    return lax.ppermute(block, "blk", [(0, 1), (1, 0)])


def grow(held, bit, *others):
    return jnp.concatenate([held, after(swap_bit(held, bit), *others)], axis=0)


def relative(slot, bits):
    return sum(((slot >> k) & 1) << bit for k, bit in enumerate(bits))


def slot_of(offset, bits):
    return sum(((offset >> bit) & 1) << k for k, bit in enumerate(bits))


def beside(moves, kernel, operand):
    came = [route(array) for array, route in moves]
    results = kernel(after(operand, *[array for array, _ in moves]))
    joined = lax.optimization_barrier((*came, *results))
    return joined[: len(came)], joined[len(came) :]


def over(bit):
    return partial(swap_bit, bit=bit)


class Gathered:
    def __init__(self, arrays, shape, blocked, moves):
        self.arrays = arrays
        self.shape = shape
        self.blocked = blocked
        self.moves = moves

    @property
    def count(self):
        return len(self.arrays)

    def start(self, refs, target, sems):
        for index, (source, spot) in enumerate(self.moves(refs, target)):
            pltpu.make_async_copy(source, spot, sems.at[index]).start()

    def wait(self, refs, target, sems):
        for index, (source, spot) in enumerate(self.moves(refs, target)):
            pltpu.make_async_copy(source, spot, sems.at[index]).wait()

    def columns(self, ref, cols):
        if not self.blocked:
            return ref[:, cols]
        block = ref[:, :, cols]
        return block.reshape(block.shape[0] * block.shape[1], block.shape[2])

    def rows(self, ref, cols):
        if not self.blocked:
            return ref[cols, :]
        of_device = ref.shape[1] * ref.shape[2]
        block = ref[cols.start // of_device : cols.stop // of_device]
        return block.reshape(cols.stop - cols.start, block.shape[3])


def plain(array):
    return Gathered([array], array.shape, False, lambda refs, target: [(refs[0], target)])


def gathered_first(one, two, rows):
    slots, _, cols = one.shape
    arrays = [one, sibling(one), two, sibling(two)]

    def moves(refs, target):
        chip = lax.axis_index("dp")
        core = lax.axis_index("blk")
        pairs = []
        for index, ref in enumerate(refs):
            bits = BITS_FIRST if index < 2 else BITS_SECOND
            which = core if index % 2 == 0 else 1 - core
            place = pl.ds(index // 2 * cols, cols)
            for slot in range(slots):
                owner = lax.bitwise_xor(chip, jnp.int32(relative(slot, bits)))
                pairs.append((ref.at[slot], target.at[owner * 2 + which, :, place]))
        return pairs

    return Gathered(arrays, (2 * slots, rows, 2 * cols), True, moves)


ANYWHERE = pl.BlockSpec(memory_space=pl.ANY)


VEC_COLS = 256


def pack_body(merged_ref, expand_ref, output_ref, tall_ref, *refs):
    vec_refs, first_ref, rest_ref = refs[:-2], refs[-2], refs[-1]
    rows, width = output_ref.shape
    vectors = jnp.concatenate([ref[...].astype(F32) for ref in vec_refs], axis=0)
    empty = jnp.zeros((16 - vectors.shape[0], rows), F32)
    vectors = jnp.concatenate([vectors, empty], axis=0).astype(BF)
    column = lax.broadcasted_iota(jnp.int32, (16, VEC_COLS), 1)
    line = lax.broadcasted_iota(jnp.int32, (16, VEC_COLS), 0)
    spread = jnp.where(column == line, 1.0, 0.0).astype(BF)
    first_ref[:, : 3 * width] = merged_ref[...]
    first_ref[:, 3 * width :] = dot(vectors, spread, TN).astype(BF)
    hidden_width = expand_ref.shape[1]
    rest_ref[:, :hidden_width] = expand_ref[...]
    rest_ref[:, hidden_width : hidden_width + width] = output_ref[...]
    for k in range(tall_ref.shape[0]):
        start = hidden_width + (1 + k) * width
        rest_ref[:, start : start + width] = tall_ref[k]


def pack(merged, expand, output, tall, vectors):
    rows, width = output.shape
    blocks = tall.shape[0] // rows
    first_cols = merged.shape[1] + VEC_COLS
    rest_cols = expand.shape[1] + (1 + blocks) * width
    return pl.pallas_call(
        pack_body,
        out_shape=[
            jax.ShapeDtypeStruct((rows, first_cols), BF),
            jax.ShapeDtypeStruct((rows, rest_cols), BF),
        ],
        compiler_params=pltpu.CompilerParams(vmem_limit_bytes=VMEM_BYTES),
        name="pack",
    )(merged, expand, output, tall.reshape(blocks, rows, width), *vectors)


def project_body(*refs, weight):
    count = weight.count
    x_ref = refs[0]
    sources = refs[1 : 1 + count]
    zt_ref, m_ref, w_ref, vec_ref, sems = refs[1 + count :]
    width = x_ref.shape[1]
    first = pl.program_id(0) == 0

    @pl.when(first)
    def _():
        weight.start(sources, w_ref, sems)

    z, _ = normed(x_ref[...].astype(F32))
    zt_ref[...] = jnp.transpose(z.astype(BF))

    @pl.when(first)
    def _():
        weight.wait(sources, w_ref, sems)
        extra = weight.columns(w_ref, slice(3 * width, 3 * width + 128))
        turned = jnp.transpose(extra.astype(F32))
        vec_ref[...] = turned[:16]

    a = (z * vec_ref[0:1, :] + vec_ref[1:2, :]).astype(BF)
    merged = dot(a, weight.columns(w_ref, slice(0, 3 * width)))
    query = (merged[:, :width] + vec_ref[2:3, :]) * (LOG2E * HEAD_DIM**-0.5)
    m_ref[:, :width] = query.astype(BF)
    m_ref[:, width : 2 * width] = merged[:, width : 2 * width].astype(BF)
    m_ref[:, 2 * width :] = (merged[:, 2 * width :] + vec_ref[3:4, :]).astype(BF)


def project(x, weight):
    rows, width = x.shape
    tile = row_tile(rows)
    row = lambda cols: pl.BlockSpec((tile, cols), lambda i: (i, 0))
    return pl.pallas_call(
        partial(project_body, weight=weight),
        grid=(rows // tile,),
        in_specs=[row(width)] + [ANYWHERE] * weight.count,
        out_specs=[
            pl.BlockSpec((width, tile), lambda i: (0, i)),
            row(3 * width), whole(weight.shape), whole((16, width)),
        ],
        out_shape=[
            jax.ShapeDtypeStruct((width, rows), BF),
            jax.ShapeDtypeStruct((rows, 3 * width), BF),
            jax.ShapeDtypeStruct(weight.shape, BF),
            jax.ShapeDtypeStruct((16, width), F32),
        ],
        scratch_shapes=[pltpu.SemaphoreType.DMA((64,))],
        compiler_params=params(1),
        cost_estimate=cost(6 * rows * width * width, 2 * rows * width * 5 + 6 * width * width),
        name="project",
    )(x, *weight.arrays)


def half_lanes(shape, head):
    return (lax.broadcasted_iota(jnp.int32, shape, 1) < HEAD_DIM) == (head == 0)


def only_head(values, head):
    return jnp.where(half_lanes(values.shape, head), values, jnp.zeros_like(values))


def ones_lane(rows):
    first = lax.broadcasted_iota(jnp.int32, (rows, LANES), 1) == 0
    return jnp.where(first, 1.0, 0.0).astype(BF)


AHEAD = 3


def attend_body(q_ref, k_ref, v_ref, mask_ref, o_ref, sum_ref, *, tile):
    keys = k_ref.shape[1]
    queries = q_ref.shape[1]
    ka = jnp.concatenate([k_ref[0], mask_ref[0]], axis=1)
    v_turned = jnp.transpose(v_ref[0])
    ones = jnp.ones((16, keys), BF)
    va = [
        jnp.concatenate([v_turned[:HEAD_DIM], ones], axis=0),
        jnp.concatenate([v_turned[HEAD_DIM:], ones], axis=0),
    ]
    one = ones_lane(tile)
    units = [(start, head) for start in range(0, queries, tile) for head in range(2)]

    def score(unit):
        start, head = unit
        q = only_head(q_ref[0, start : start + tile, :], head)
        return dot(ka, jnp.concatenate([q, one], axis=1), NT)

    ahead = [score(unit) for unit in units[:AHEAD]]
    parts = []
    for index, (start, head) in enumerate(units):
        if index + AHEAD < len(units):
            ahead.append(score(units[index + AHEAD]))
        s = ahead[index]
        top = jnp.max(s, axis=0, keepdims=True)
        p = jnp.exp2(s - top).astype(BF)
        mix = dot(va[head], p)
        total = mix[HEAD_DIM : HEAD_DIM + 1]
        parts.append(mix[:HEAD_DIM] / total)
        sum_ref[0, head : head + 1, start : start + tile] = top + jnp.log2(total)
        if head == 1:
            mixed = jnp.concatenate(parts, axis=0)
            o_ref[0, start : start + tile, :] = jnp.transpose(mixed)
            parts = []


def attend(merged, key_merged, key_base, mask, first=0, count=PAIRS):
    clips, queries, _ = merged.shape
    keys = key_merged.shape[1]
    tile = row_tile(queries)
    lanes = lambda rows, base: pl.BlockSpec((1, rows, LANES), lambda c, h: (c, 0, base + h))
    return pl.pallas_call(
        partial(attend_body, tile=tile),
        grid=(clips, count),
        in_specs=[
            lanes(queries, first),
            lanes(keys, key_base + first),
            lanes(keys, key_base + PAIRS + first),
            pl.BlockSpec((1, keys, LANES), lambda c, h: (c, 0, 0)),
        ],
        out_specs=[
            lanes(queries, 0),
            pl.BlockSpec((1, ROW_GROUP, queries), lambda c, h: (c, h, 0)),
        ],
        out_shape=[
            jax.ShapeDtypeStruct((clips, queries, count * LANES), F32),
            jax.ShapeDtypeStruct((clips, count * ROW_GROUP, queries), F32),
        ],
        compiler_params=params(2),
        cost_estimate=cost(
            clips * count * queries * keys * 2 * 4 * 256,
            clips * count * LANES * (2 * queries + 4 * keys + 4 * queries),
            clips * count * queries * keys * 2,
        ),
        name="attend",
    )(merged, key_merged, key_merged, mask)


def attend_back_body(
    q_ref, k_ref, v_ref, do_ref, mask_ref, sum_ref, delta_ref, *rest, tile
):
    dk_acc, dv_acc = rest[-2:]
    if len(rest) == 3:
        dq_ref, dk_ref, dv_ref = (rest[0].at[0, k] for k in range(3))
    else:
        dq_ref, dk_ref, dv_ref = (ref.at[0] for ref in rest[:3])
    queries = q_ref.shape[1]
    k = k_ref[0]
    v = v_ref[0]
    ka = jnp.concatenate([k, mask_ref[0]], axis=1)
    k_turned = jnp.transpose(k)
    one = ones_lane(tile)
    units = [(start, head) for start in range(0, queries, tile) for head in range(2)]

    def first(unit):
        start, head = unit
        rows = slice(start, start + tile)
        qm = only_head(q_ref[0, rows, :], head)
        dom = only_head(do_ref[0, rows, :], head)
        return qm, dom, dot(ka, jnp.concatenate([qm, one], axis=1), NT), dot(v, dom, NT)

    ahead = first(units[0])
    held = []
    for index, (start, head) in enumerate(units):
        rows = slice(start, start + tile)
        qm, dom, s, dp = ahead
        if index + 1 < len(units):
            ahead = first(units[index + 1])
        p = jnp.exp2(s - sum_ref[0, head : head + 1, rows])
        ds = (p * (dp - delta_ref[0, head : head + 1, rows])).astype(BF)
        dq = dot(k_turned[head * HEAD_DIM : (head + 1) * HEAD_DIM], ds)
        held.append((qm, dom, p.astype(BF), ds, dq))
        if head == 0:
            continue
        q_parts, do_parts, p_parts, ds_parts, dq_parts = zip(*held)
        held = []
        dq = jnp.transpose(jnp.concatenate(dq_parts, axis=0)) * (HEAD_DIM**-0.5)
        dq_ref[rows, :] = dq.astype(BF)
        dk = dot(jnp.concatenate(ds_parts, axis=1), jnp.concatenate(q_parts, axis=0))
        dv = dot(jnp.concatenate(p_parts, axis=1), jnp.concatenate(do_parts, axis=0))
        if start == 0:
            dk_acc[...] = dk
            dv_acc[...] = dv
        else:
            dk_acc[...] += dk
            dv_acc[...] += dv
    dk_ref[...] = (dk_acc[...] * (1.0 / LOG2E)).astype(BF)
    dv_ref[...] = dv_acc[...].astype(BF)


def attend_back(merged, key_merged, key_base, grad_out, mask, sums, delta, first=0, count=PAIRS):
    clips, queries, _ = merged.shape
    keys = key_merged.shape[1]
    tile = row_tile(queries)
    lanes = lambda rows, base: pl.BlockSpec((1, rows, LANES), lambda c, h: (c, 0, base + h))
    stat = lambda base: pl.BlockSpec((1, ROW_GROUP, queries), lambda c, h: (c, base + h, 0))
    columns = count * LANES
    if queries == keys:
        out_specs = [pl.BlockSpec((1, 3, keys, LANES), lambda c, h: (c, 0, 0, h))]
        out_shape = [jax.ShapeDtypeStruct((clips, 3, keys, columns), BF)]
    else:
        out_specs = [lanes(queries, 0), lanes(keys, 0), lanes(keys, 0)]
        out_shape = [
            jax.ShapeDtypeStruct((clips, queries, columns), BF),
            jax.ShapeDtypeStruct((clips, keys, columns), BF),
            jax.ShapeDtypeStruct((clips, keys, columns), BF),
        ]
    return pl.pallas_call(
        partial(attend_back_body, tile=tile),
        grid=(clips, count),
        in_specs=[
            lanes(queries, first),
            lanes(keys, key_base + first),
            lanes(keys, key_base + PAIRS + first),
            lanes(queries, first),
            pl.BlockSpec((1, keys, LANES), lambda c, h: (c, 0, 0)),
            stat(first),
            stat(first),
        ],
        out_specs=out_specs,
        out_shape=out_shape,
        scratch_shapes=[pltpu.VMEM((keys, LANES), F32), pltpu.VMEM((keys, LANES), F32)],
        compiler_params=params(2),
        cost_estimate=cost(
            clips * count * queries * keys * 2 * 9 * 256,
            clips * count * LANES * 2 * (3 * queries + 4 * keys),
            clips * count * queries * keys * 2,
        ),
        name="attend_back",
    )(merged, key_merged, key_merged, grad_out, mask, sums, delta)


ERF = (0.254829592, -0.284496736, 1.421413741, -1.453152027, 1.061405429)
ERF_P = 0.3275911


def gelu_both(u):
    bell = jnp.exp2(u * u * (-0.5 * LOG2E))
    t = 1.0 / (1.0 + (ERF_P * 0.5**0.5) * jnp.abs(u))
    series = ERF[4] * 0.5
    for term in ERF[3::-1]:
        series = series * t + term * 0.5
    tail = series * t * bell
    chance = jnp.where(u >= 0, 1.0 - tail, tail)
    return u * chance, chance + u * bell * 0.3989422804014327


def feed_body(*refs, chunk, mixes, wide, tall):
    x_ref, g_ref = refs[:2]
    o_refs = refs[2 : 2 + mixes]
    at = 2 + mixes
    wide_refs = refs[at : at + wide.count]
    at += wide.count
    tall_refs = refs[at : at + tall.count]
    at += tall.count
    (
        vecs_ref, be_ref, sel_ref,
        result_ref, h_ref, right_ref, gm_ref, left_ref, ga_ref, delta_ref, vec_ref,
        ebg_ref, wide_w, tall_w, wide_sems, tall_sems,
    ) = refs[at:]
    width = x_ref.shape[1]
    hidden_width = be_ref.shape[1]
    all_output = slice(hidden_width, hidden_width + width)

    @pl.when(pl.program_id(0) == 0)
    def _():
        wide.start(wide_refs, wide_w, wide_sems)
        tall.start(tall_refs, tall_w, tall_sems)
        vec_ref[...] = jnp.zeros_like(vec_ref)
        ebg_ref[...] = jnp.zeros_like(ebg_ref)
        wide.wait(wide_refs, wide_w, wide_sems)
        tall.wait(tall_refs, tall_w, tall_sems)

    o = jnp.concatenate([ref[...] for ref in o_refs], axis=1)
    att = o.astype(BF)
    left_ref[1] = jnp.transpose(att)
    middle = x_ref[...].astype(F32) + dot(att, wide.columns(wide_w, all_output)) + vecs_ref[4:5, :]
    z, scale = normed(middle)
    gain = vecs_ref[5:6, :]
    fi = (z * gain + vecs_ref[6:7, :]).astype(BF)
    left_ref[0] = jnp.transpose(fi)
    g = g_ref[...]
    out = middle + vecs_ref[7:8, :]
    u = jnp.zeros_like(middle)
    starts = list(range(0, hidden_width, chunk))

    def first(start):
        cols = slice(start, start + chunk)
        we = wide.columns(wide_w, cols)
        ws = tall.rows(tall_w, cols)
        return dot(fi, we) + be_ref[:, cols], dot(g, ws, NT), we, ws

    ahead = [first(start) for start in starts[:2]]
    for index, start in enumerate(starts):
        cols = slice(start, start + chunk)
        if index + 2 < len(starts):
            ahead.append(first(starts[index + 2]))
        pre, gh, we, ws = ahead[index]
        act, slope = gelu_both(pre)
        act = act.astype(BF)
        gp = (gh * slope).astype(BF)
        h_ref[:, cols] = act
        right_ref[:, cols] = gp
        ebg_ref[:, cols] += fold_rows(gp.astype(F32))
        out += dot(act, ws)
        u += dot(gp, we, NT)
    result_ref[...] = out.astype(BF)
    gf = g.astype(F32)
    gm = gf + norm_back(u, gain, z, scale)
    gm_ref[...] = gm
    gb = gm.astype(BF)
    right_ref[:, hidden_width:] = gb
    ga = dot(gb, wide.columns(wide_w, all_output), NT).astype(BF)
    ga_ref[...] = ga
    prod = ga.astype(F32) * o
    high = prod.astype(BF)
    low = (prod - high.astype(F32)).astype(BF)
    sel = sel_ref[...]
    delta_ref[...] = dot(sel, high, NT) + dot(sel, low, NT)
    vec_ref[:, :width] += fold_rows(u * z)
    vec_ref[:, width : 2 * width] += fold_rows(u)
    vec_ref[:, 2 * width : 3 * width] += fold_rows(gb.astype(F32))
    vec_ref[:, 3 * width :] += fold_rows(gf)


def feed(x, g, mixtures, wide, tall, vecs, be):
    rows, width = x.shape
    hidden_width = be.shape[1]
    tile = row_tile(rows)
    lane_head = jnp.arange(width)[None, :] // HEAD_DIM
    stat_row = jnp.arange(PAIRS * ROW_GROUP)[:, None]
    chosen = (stat_row // ROW_GROUP * 2 + stat_row % ROW_GROUP == lane_head) & (
        stat_row % ROW_GROUP < 2
    )
    select = chosen.astype(BF)
    row = lambda cols: pl.BlockSpec((tile, cols), lambda i: (i, 0))
    keep = lambda cols: pl.BlockSpec((ROW_GROUP, cols), lambda i: (0, 0))
    shape = jax.ShapeDtypeStruct
    return pl.pallas_call(
        partial(feed_body, chunk=768, mixes=len(mixtures), wide=wide, tall=tall),
        grid=(rows // tile,),
        in_specs=[
            row(width), row(width), *[row(mixture.shape[1]) for mixture in mixtures],
            *[ANYWHERE] * (wide.count + tall.count),
            whole(vecs.shape), whole((1, hidden_width)), whole(select.shape),
        ],
        out_specs=[
            row(width), row(hidden_width), row(hidden_width + width), row(width),
            pl.BlockSpec((2, width, tile), lambda i: (0, 0, i)), row(width),
            pl.BlockSpec((PAIRS * ROW_GROUP, tile), lambda i: (0, i)),
            keep(4 * width), keep(hidden_width),
        ],
        out_shape=[
            shape((rows, width), BF), shape((rows, hidden_width), BF),
            shape((rows, hidden_width + width), BF), shape((rows, width), F32),
            shape((2, width, rows), BF), shape((rows, width), BF),
            shape((PAIRS * ROW_GROUP, rows), F32),
            shape((ROW_GROUP, 4 * width), F32), shape((ROW_GROUP, hidden_width), F32),
        ],
        scratch_shapes=[
            pltpu.VMEM(wide.shape, BF), pltpu.VMEM(tall.shape, BF),
            pltpu.SemaphoreType.DMA((4,)), pltpu.SemaphoreType.DMA((4,)),
        ],
        compiler_params=params(1),
        cost_estimate=cost(
            rows * width * (4 * width + 8 * hidden_width),
            rows * (width * 20 + hidden_width * 4) + 2 * width * (width + 2 * hidden_width),
            rows * hidden_width * 2,
        ),
        name="feed",
    )(x, g, *mixtures, *wide.arrays, *tall.arrays, vecs, be, select)


def lay_out(value_ref, value_cols, outs, out_cols, rows, bits):
    if bits is None:
        outs[0][:, out_cols] = value_ref[:, value_cols].astype(BF)
        return
    keep_ref, send_ref = outs
    chip = lax.axis_index("dp")
    core = lax.axis_index("blk")
    for slot in range(keep_ref.shape[0]):
        owner = lax.bitwise_xor(chip, jnp.int32(relative(slot, bits)))
        for ref, which in ((keep_ref, core), (send_ref, 1 - core)):
            first = pl.multiple_of((owner * 2 + which) * rows, 8)
            ref[slot, :, out_cols] = value_ref[pl.ds(first, rows), value_cols].astype(BF)


def laid_out(few, columns, rows, bits):
    if bits is None:
        shapes = [(few, columns)]
    else:
        shapes = [(few // (2 * rows), rows, columns)] * 2
    return (
        [whole(shape) for shape in shapes],
        [jax.ShapeDtypeStruct(shape, BF) for shape in shapes],
    )


def outer_tall_body(left_ref, right_ref, side_ref, *outs, rows, blocks, bits):
    value = dot(left_ref[...], right_ref[...], TN)
    chunk, few = value.shape
    side = jnp.sum(side_ref[...], axis=0, keepdims=True)
    side = jnp.transpose(jnp.concatenate([side, jnp.zeros((127, chunk), F32)], axis=0))
    if bits is None:
        outs[0][:, :few] = value.astype(BF)
        outs[0][:, few:] = side.astype(BF)
        return
    keep_ref, send_ref, value_ref, turned_ref = outs
    value_ref[...] = value
    turned_ref[...] = jnp.broadcast_to(side[:, :1], (chunk, 128))
    chip = lax.axis_index("dp")
    core = lax.axis_index("blk")
    lane = lax.broadcasted_iota(jnp.int32, (rows, 128), 1)
    chips = chunk // (2 * blocks * rows)
    for index in range(chips):
        owner = pl.program_id(0) * chips + index
        slot = slot_of(lax.bitwise_xor(chip, owner), bits)
        for ref, which in ((keep_ref, core), (send_ref, 1 - core)):
            extra = jnp.zeros((rows, 128), F32)
            for k in range(blocks):
                first = pl.multiple_of(((index * 2 + which) * blocks + k) * rows, 8)
                ref[slot, :, k * few : (k + 1) * few] = value_ref[pl.ds(first, rows), :].astype(BF)
                extra += jnp.where(lane == k, turned_ref[pl.ds(first, rows), :], 0.0)
            ref[slot, :, blocks * few :] = extra.astype(BF)


def outer_tall(left, right, side, rows, blocks, bits):
    length, many = left.shape
    few = right.shape[1]
    chunk = 768
    if bits is None:
        out_specs = [pl.BlockSpec((chunk, few + 128), lambda i: (i, 0))]
        out_shape = [jax.ShapeDtypeStruct((many, few + 128), BF)]
        scratch = []
    else:
        shape = (many // (2 * blocks * rows), rows, blocks * few + 128)
        out_specs = [whole(shape)] * 2
        out_shape = [jax.ShapeDtypeStruct(shape, BF)] * 2
        scratch = [pltpu.VMEM((chunk, few), F32), pltpu.VMEM((chunk, 128), F32)]
    return pl.pallas_call(
        partial(outer_tall_body, rows=rows, blocks=blocks, bits=bits),
        grid=(many // chunk,),
        in_specs=[
            pl.BlockSpec((length, chunk), lambda i: (0, i)),
            whole((length, few)),
            pl.BlockSpec((ROW_GROUP, chunk), lambda i: (0, i)),
        ],
        out_specs=out_specs,
        out_shape=out_shape,
        scratch_shapes=scratch,
        compiler_params=params(1),
        cost_estimate=cost(2 * length * many * few, 2 * length * (many + few) + 2 * many * few),
        name="outer_tall",
    )(left, right, side)


def outer_wide_body(left_ref, right_ref, vec_ref, *outs, rows, bits):
    value_ref = outs[-1]
    outs = outs[:-1]
    step = pl.program_id(0)
    width = right_ref.shape[1]
    value_ref[...] = dot(left_ref[0], right_ref[...])
    cols = pl.ds(pl.multiple_of(step * width, 128), width)
    lay_out(value_ref, slice(None), outs, cols, rows, bits)

    @pl.when(step == pl.num_programs(0) - 1)
    def _():
        sums = [
            jnp.sum(vec_ref[:, k * width : (k + 1) * width], axis=0, keepdims=True)
            for k in range(4)
        ]
        table = jnp.concatenate(sums + [jnp.zeros((124, width), F32)], axis=0)
        value_ref[:, :128] = jnp.transpose(table)
        lay_out(value_ref, slice(0, 128), outs, slice(5 * width, 5 * width + 128), rows, bits)


def outer_wide(left, right, vec, rows, bits):
    _, few, length = left.shape
    columns = right.shape[1]
    steps = columns // few
    out_specs, out_shape = laid_out(few, columns + 128, rows, bits)
    return pl.pallas_call(
        partial(outer_wide_body, rows=rows, bits=bits),
        grid=(steps,),
        in_specs=[
            pl.BlockSpec((1, few, length), lambda i: (i // (steps - 1), 0, 0)),
            pl.BlockSpec((length, few), lambda i: (0, i)),
            whole(vec.shape),
        ],
        out_specs=out_specs,
        out_shape=out_shape,
        scratch_shapes=[pltpu.VMEM((few, few), F32)],
        compiler_params=params(1),
        cost_estimate=cost(
            2 * length * few * columns, 2 * length * (2 * few + columns) + 2 * few * columns
        ),
        name="outer_wide",
    )(left, right, vec)


def outer_merged_body(left_ref, w_ref, extra_ref, *refs, pieces, rows, bits):
    right_refs = refs[:pieces]
    outs = refs[pieces:-2]
    value_ref, side_ref = refs[-2:]
    step = pl.program_id(0)
    width = left_ref.shape[0]
    rights = [ref[0] for ref in right_refs]
    right = rights[0] if pieces == 1 else jnp.concatenate(rights, axis=1)
    z_grad = dot(left_ref[...], right)
    total = jnp.sum(fold_rows(right.astype(F32)), axis=0, keepdims=True)
    gain = extra_ref[:, 0:1].astype(F32)
    shift = extra_ref[:, 1:2].astype(F32)
    value_ref[...] = gain * z_grad + shift * total
    cols = pl.ds(pl.multiple_of(step * width, 128), width)
    lay_out(value_ref, slice(None), outs, cols, rows, bits)
    w = w_ref[...].astype(F32)
    gain_grad = jnp.sum(w * z_grad, axis=1, keepdims=True)
    shift_grad = jnp.sum(w * total, axis=1, keepdims=True)
    turned = jnp.transpose(
        jnp.concatenate([total, jnp.zeros((127, width), F32)], axis=0)
    )[:, :1]
    lane = lax.broadcasted_iota(jnp.int32, (width, 128), 1)
    zero = jnp.zeros((), F32)
    bias_lane = jnp.where(step == 0, 2, jnp.where(step == 1, 4, 3))
    side = (
        jnp.where(lane == 0, gain_grad, zero)
        + jnp.where(lane == 1, shift_grad, zero)
        + jnp.where(lane == bias_lane, turned, zero)
    )

    @pl.when(step == 0)
    def _():
        side_ref[...] = side

    @pl.when(step > 0)
    def _():
        side_ref[...] += side

    @pl.when(step == 2)
    def _():
        lay_out(side_ref, slice(None), outs, slice(3 * width, 3 * width + 128), rows, bits)


def outer_merged(left, weight, grads, rows, bits):
    few, length = left.shape
    out_specs, out_shape = laid_out(few, 3 * few + 128, rows, bits)
    return pl.pallas_call(
        partial(outer_merged_body, pieces=len(grads), rows=rows, bits=bits),
        grid=(3,),
        in_specs=[
            whole(left.shape),
            pl.BlockSpec((few, few), lambda i: (0, i)),
            pl.BlockSpec((few, 128), lambda i: (0, 3 * few // 128)),
        ]
        + [pl.BlockSpec((1, length, grad.shape[2]), lambda i: (i, 0, 0)) for grad in grads],
        out_specs=out_specs,
        out_shape=out_shape,
        scratch_shapes=[pltpu.VMEM((few, few), F32), pltpu.VMEM((few, 128), F32)],
        compiler_params=params(1),
        cost_estimate=cost(6 * length * few * few, 8 * length * few + 12 * few * few),
        name="outer_merged",
    )(left, weight, weight, *grads)


def added(left, right):
    return (left.astype(F32) + right.astype(F32)).astype(BF)


def collect_plain(grads):
    total = lax.psum_scatter(grads, ("dp", "blk"), scatter_dimension=0, tiled=True)
    return total.astype(F32)


def halved(held, came):
    half = held.shape[0] // 2
    return added(held[:half], came[:half]), added(held[half:], came[half:])


def unproject_body(*refs, pieces):
    part_refs = refs[:pieces]
    w_ref, x_ref, vecs_ref, gm_ref, tg_ref = refs[pieces:]
    width = x_ref.shape[1]
    grads = [ref[k] for k in range(3) for ref in part_refs]
    u = dot(jnp.concatenate(grads, axis=1), w_ref[:, : 3 * width], NT)
    z, scale = normed(x_ref[...].astype(F32))
    back = norm_back(u, vecs_ref[0:1, :], z, scale)
    tg_ref[...] = (gm_ref[...] + back).astype(BF)


def unproject(grads, weight, x, vecs, gm):
    rows, width = x.shape
    tile = row_tile(rows)
    row = lambda cols: pl.BlockSpec((tile, cols), lambda i: (i, 0))
    return pl.pallas_call(
        partial(unproject_body, pieces=len(grads)),
        grid=(rows // tile,),
        in_specs=[pl.BlockSpec((3, tile, grad.shape[2]), lambda i: (0, i, 0)) for grad in grads]
        + [whole(weight.shape), row(width), whole(vecs.shape), row(width)],
        out_specs=row(width),
        out_shape=jax.ShapeDtypeStruct((rows, width), BF),
        compiler_params=params(1),
        cost_estimate=cost(6 * rows * width * width, 2 * rows * width * 8 + 6 * width * width),
        name="unproject",
    )(*grads, weight, x, vecs, gm)


def pad_rows(values, rows):
    return jnp.pad(values, ((0, 0), (0, rows - values.shape[1]), (0, 0)))


def trade_clips(values):
    if lax.axis_size("blk") != 2:
        return lax.all_to_all(values, "blk", 0, 1, tiled=True)
    clips, rows, width = values.shape
    core = lax.axis_index("blk")
    pairs = values.reshape(2, clips // 2, rows, width)
    low, high = pairs[0], pairs[1]
    mine = jnp.where(core == 0, low, high)
    other = sibling(jnp.where(core == 0, high, low))
    return jnp.concatenate(
        [jnp.where(core == 0, mine, other), jnp.where(core == 0, other, mine)], axis=1
    )


def trade_back(values):
    if lax.axis_size("blk") != 2:
        return lax.all_to_all(values, "blk", 1, 0, tiled=True)
    clips, rows, width = values.shape
    core = lax.axis_index("blk")
    low, high = values[:, : rows // 2], values[:, rows // 2 :]
    mine = jnp.where(core == 0, low, high)
    other = sibling(jnp.where(core == 0, high, low))
    return jnp.concatenate(
        [jnp.where(core == 0, mine, other), jnp.where(core == 0, other, mine)], axis=0
    )


def key_mask(counts, cycle, rows_dev, rows_pad):
    position = jnp.arange(cycle * rows_pad, dtype=jnp.int32)
    block = position // rows_pad
    offset = position % rows_pad
    column = block * ((rows_dev - 2) // FREQ) + (offset - 2) // FREQ
    seen = jnp.where(
        (offset < 2)[None, :], (block == 0)[None, :], column[None, :] < counts[:, None]
    ) & (offset < rows_dev)[None, :]
    lane = jnp.arange(LANES, dtype=jnp.int32)
    return jnp.where(seen[:, :, None] | (lane > 0)[None, None, :], 0.0, NEGATIVE).astype(BF)


GROUPS = ((0, 1), (1, 3), (4, 2))


def local(
    tokens, counts, attend_gain, attend_shift, merged_weight, query_bias, value_bias,
    output_weight, output_bias, feed_gain, feed_shift, expand_weight, expand_bias,
    shrink_weight, shrink_bias, cotangent,
):
    clips, rows_dev, width = tokens.shape
    chips, cycle = lax.axis_size("dp"), lax.axis_size("blk")
    quick = quick_mesh({"dp": chips, "blk": cycle})
    rows_pad = -(-rows_dev // 16) * 16
    traded = clips % cycle == 0
    weight_rows = merged_weight.shape[0]
    tall_rows = shrink_weight.shape[0]
    hidden_width = expand_weight.shape[1]
    devices = chips * cycle
    core = lax.axis_index("blk")
    blocks = tall_rows // weight_rows
    vectors = [
        vector.reshape(-1, weight_rows)
        for vector in (
            attend_gain, attend_shift, query_bias, value_bias,
            output_bias, feed_gain, feed_shift, shrink_bias, expand_bias,
        )
    ]
    wide_cols = hidden_width + width
    if quick:
        first_pack, rest = pack(
            merged_weight, expand_weight, output_weight, shrink_weight, vectors
        )
        held_first = grow(first_pack[None], 3)
        held_first = grow(held_first, 2)
        rest = lax.all_gather(rest, ("dp", "blk"), axis=0)
        wide = Gathered(
            [rest],
            (devices, weight_rows, wide_cols),
            True,
            lambda refs, target: [(refs[0].at[:, :, :wide_cols], target)],
        )
        tall = Gathered(
            [rest],
            (devices, blocks, weight_rows, width),
            True,
            lambda refs, target: [
                (refs[0].at[:, :, pl.ds(wide_cols + k * width, width)], target.at[:, k])
                for k in range(blocks)
            ],
        )
        cut = first_pack.shape[1] // 2
        one = grow(held_first[:, :, :cut], 0)
        two = grow(held_first[:, :, cut:], 1)
    else:
        gather = lambda block: plain(lax.all_gather(block, ("dp", "blk"), axis=0, tiled=True))
        vec_cols = jnp.concatenate(vectors).T
        vec_cols = jnp.pad(vec_cols, ((0, 0), (0, VEC_COLS - vec_cols.shape[1])))
        merged_full = gather(jnp.concatenate([merged_weight, vec_cols], axis=1))
        wide = gather(jnp.concatenate([expand_weight, output_weight], axis=1))
        tall = gather(shrink_weight)
    if quick:
        x = trade_clips(pad_rows(tokens, rows_pad))
        one = grow(one, 1, x)
        two = grow(two, 0, x)
        g = trade_clips(pad_rows(after(cotangent, one, two), rows_pad))
        merged_full = gathered_first(one, two, weight_rows)
    else:
        x = pad_rows(tokens, rows_pad)
        g = pad_rows(cotangent, rows_pad)
        if traded:
            x = trade_clips(x)
            g = trade_clips(g)
    held = clips // cycle if traded else clips
    own_counts = lax.dynamic_slice_in_dim(counts, core * held, held) if traded else counts
    queries = x.shape[1]
    total = held * queries
    x = x.reshape(total, width)
    g = g.reshape(total, width)
    mask = key_mask(own_counts, cycle, rows_dev, rows_pad)

    z_turned, merged, weight_flat, vecs = project(x, merged_full)
    weight_flat = weight_flat.reshape(devices * weight_rows, -1)
    bias_row = (
        vecs[8 : 8 + blocks].reshape(blocks, devices, weight_rows).transpose(1, 0, 2)
    ).reshape(1, hidden_width)
    merged = merged.reshape(held, queries, 3 * width)
    if traded:
        keys, key_base = merged, PAIRS
    else:
        keys = lax.all_gather(merged[:, :, width:], "blk", axis=1, tiled=True)
        key_base = 0
    mixture, sums = attend(merged, keys, key_base, mask)
    mixtures = [mixture.reshape(total, width)]
    (
        result, hidden, rights, grad_middle, lefts, grad_attended, delta, feed_vec, expand_vec,
    ) = feed(x, g, mixtures, wide, tall, vecs, bias_row)

    def home(values):
        values = values.reshape(held, queries, width)
        if traded:
            values = trade_back(values)
        return values[:, :rows_dev]

    bits = BITS_FIRST if quick else None
    wide_grad = outer_wide(lefts, rights, feed_vec, weight_rows, bits)
    delta = delta.reshape(PAIRS * ROW_GROUP, held, queries).transpose(1, 0, 2)
    grad_heads = grad_attended.reshape(held, queries, width)
    back = partial(attend_back, merged, keys, key_base)
    if quick:
        wide_keep, wide_send = wide_grad
        (wide_came,), (tall_keep, tall_send) = beside(
            [(wide_send, sibling)],
            lambda rows: outer_tall(rows, g, expand_vec, weight_rows, blocks, BITS_SECOND),
            hidden,
        )
        wide_kept, wide_away = halved(wide_keep, wide_came)

        def back_group(index):
            first, count = GROUPS[index]
            return lambda rows: back(rows, mask, sums, delta, first, count)

        grads = []
        (tall_came,), part = beside(
            [(tall_send, sibling)], back_group(0), after(grad_heads, wide_kept, wide_away)
        )
        grads += part
        tall_kept, tall_away = halved(tall_keep, tall_came)
        for index, bit in ((1, 1), (2, 0)):
            (wide_came, tall_came), part = beside(
                [(wide_away, over(bit)), (tall_away, over(1 - bit))],
                back_group(index),
                after(grad_heads, grads[-1]),
            )
            grads += part
            if index == 1:
                wide_kept, wide_away = halved(wide_kept, wide_came)
                tall_kept, tall_away = halved(tall_kept, tall_came)
        grads = [
            part.transpose(1, 0, 2, 3).reshape(3, total, part.shape[3]) for part in grads
        ]
        late_kept, late_away = (
            jnp.concatenate(pair, axis=2)
            for pair in zip(halved(wide_kept, wide_came), halved(tall_kept, tall_came))
        )
        (late_came,), (merged_keep, merged_send) = beside(
            [(late_away, over(2))],
            lambda rows: outer_merged(rows, weight_flat, grads, weight_rows, bits),
            z_turned,
        )
        merged_came = sibling(merged_send)
        late_kept, late_away = halved(late_kept, late_came)
        merged_keep = merged_keep.reshape(2, 2, chips // 4, weight_rows, -1)
        merged_came = merged_came.reshape(merged_keep.shape)
        cut = merged_keep.shape[-1] // 256 * 128
        one = [added(merged_keep[k, ..., :cut], merged_came[k, ..., :cut]) for k in range(2)]
        two = [added(merged_keep[:, k, ..., cut:], merged_came[:, k, ..., cut:]) for k in range(2)]
        late_came = swap_bit(late_away, 3)
        (one_came, two_came), (tokens_grad,) = beside(
            [(one[1], over(1)), (two[1], over(0))],
            lambda rows: [unproject(grads, weight_flat, rows, vecs, grad_middle)],
            after(x, late_away),
        )
        one = [added(one[0][k], one_came[k]) for k in range(2)]
        two = [added(two[0][k], two_came[k]) for k in range(2)]
        one_came = swap_bit(one[1], 0)
        two_came = swap_bit(two[1], 1)
        late_came = after(late_came, one_came, two_came)
        one = added(one[0], one_came)
        two = added(two[0], two_came)
        merged_held = jnp.concatenate([one, two], axis=-1)
        merged_kept, merged_away = merged_held[:2], merged_held[2:]
        tokens_home = home(tokens_grad)
        merged_came = after(swap_bit(merged_away, 2), tokens_home)
        merged_kept, merged_away = halved(merged_kept, merged_came)
        full = lambda kept, came: (kept.astype(F32) + came.astype(F32))[0]
        merged_grad = full(merged_kept, swap_bit(merged_away, 3))
        late_grad = full(late_kept, late_came)
        wide_cols = wide_keep.shape[2]
        wide_grad = late_grad[:, :wide_cols]
        tall_grad = late_grad[:, wide_cols:]
        shrink_grad = jnp.concatenate(
            [tall_grad[:, k * width : (k + 1) * width] for k in range(blocks)], axis=0
        )
        expand_bias_grad = tall_grad[:, blocks * width : blocks * (width + 1)].T.reshape(-1)
    else:
        tall_grad = outer_tall(hidden, g, expand_vec, weight_rows, blocks, None)[0]
        tall_grad = collect_plain(tall_grad)
        shrink_grad = tall_grad[:, :width]
        expand_bias_grad = tall_grad[:, width]
        columns = []
        for first, count in GROUPS:
            parts = back(grad_heads, mask, sums, delta, first, count)
            if traded:
                parts = [parts[0][:, k] for k in range(3)]
            else:
                scatter = partial(
                    lax.psum_scatter, axis_name="blk", scatter_dimension=1, tiled=True
                )
                parts = [parts[0], scatter(parts[1]), scatter(parts[2])]
            columns.append(jnp.stack(parts))
        grads = [jnp.concatenate(columns, axis=3).reshape(3, total, width)]
        merged_grad = outer_merged(z_turned, weight_flat, grads, weight_rows, None)
        tokens_home = home(unproject(grads, weight_flat, x, vecs, grad_middle))
        merged_grad = collect_plain(merged_grad[0])
        wide_grad = collect_plain(wide_grad[0])
    vec_wide = wide_grad[:, 5 * width :]
    vec_merged = merged_grad[:, 3 * width :]

    return (
        home(result),
        tokens_home,
        vec_merged[:, 0],
        vec_merged[:, 1],
        merged_grad[:, : 3 * width],
        vec_merged[:, 2],
        vec_merged[:, 3],
        wide_grad[:, hidden_width : hidden_width + width],
        vec_wide[:, 2],
        vec_wide[:, 0],
        vec_wide[:, 1],
        wide_grad[:, :hidden_width],
        expand_bias_grad,
        shrink_grad,
        vec_wide[:, 3],
    )


def solution(mesh):
    rows = P("dp", "blk", None)
    vector = P(("dp", "blk"))
    matrix = P(("dp", "blk"), None)
    in_specs = (
        rows, P("dp"), vector, vector, matrix, vector, vector, matrix, vector, vector, vector,
        matrix, vector, matrix, vector, rows,
    )
    out_specs = (
        rows, rows, vector, vector, matrix, vector, vector, matrix, vector, vector, vector,
        matrix, vector, matrix, vector,
    )
    return jax.shard_map(local, mesh=mesh, in_specs=in_specs, out_specs=out_specs, check_vma=False)
```

```python
from functools import partial

import jax
import jax.numpy as jnp
from jax import lax
from jax.experimental import pallas as pl
from jax.experimental.pallas import tpu as pltpu
from jax.sharding import PartitionSpec as P

HEADS = 12
HEAD_DIM = 64
FREQ = 12
EPSILON = 1e-06
NEGATIVE = -1e30
LOG2E = 1.4426950408889634
PAIRS = HEADS // 2
LANES = 2 * HEAD_DIM
ROW_GROUP = 8
VMEM_BYTES = 60 * 1024 * 1024

BF = jnp.bfloat16
F32 = jnp.float32

NN = (((1,), (0,)), ((), ()))
NT = (((1,), (1,)), ((), ()))
TN = (((0,), (0,)), ((), ()))


def dot(left, right, dims=NN):
    return lax.dot_general(left, right, dims, preferred_element_type=F32)


def params(count):
    return pltpu.CompilerParams(
        dimension_semantics=("arbitrary",) * count, vmem_limit_bytes=VMEM_BYTES
    )


def whole(shape):
    return pl.BlockSpec(shape, lambda *_: (0,) * len(shape), pipeline_mode=pl.Buffered(1))


def cost(flops, bytes_accessed, transcendentals=0):
    return pl.CostEstimate(
        flops=int(flops), bytes_accessed=int(bytes_accessed), transcendentals=int(transcendentals)
    )


def normed(values):
    mean_row = jnp.mean(values, axis=-1, keepdims=True)
    centered = values - mean_row
    spread = jnp.mean(centered * centered, axis=-1, keepdims=True)
    scale = lax.rsqrt(spread + EPSILON)
    return centered * scale, scale


def norm_back(upstream, gain_row, z, scale):
    w = upstream * gain_row
    return scale * (
        w - jnp.mean(w, axis=-1, keepdims=True) - z * jnp.mean(w * z, axis=-1, keepdims=True)
    )


def fold_rows(values):
    rows, width = values.shape
    return jnp.sum(values.reshape(rows // ROW_GROUP, ROW_GROUP, width), axis=0)


def row_tile(rows):
    return 256 if rows % 256 == 0 else rows


BITS_FIRST = (3, 2, 0, 1)
BITS_SECOND = (3, 2, 1, 0)


def after(value, *others):
    return lax.optimization_barrier((value, *others))[0]


def quick_mesh(sizes):
    return sizes["dp"] == 16 and sizes["blk"] == 2


def swap_bit(block, bit):
    return lax.ppermute(block, "dp", [(i, i ^ (1 << bit)) for i in range(lax.axis_size("dp"))])


def sibling(block):
    return lax.ppermute(block, "blk", [(0, 1), (1, 0)])


def grow(held, bit, *others):
    return jnp.concatenate([held, after(swap_bit(held, bit), *others)], axis=0)


def relative(slot, bits):
    return sum(((slot >> k) & 1) << bit for k, bit in enumerate(bits))


def slot_of(offset, bits):
    return sum(((offset >> bit) & 1) << k for k, bit in enumerate(bits))


def beside(moves, kernel, operand):
    came = [route(array) for array, route in moves]
    results = kernel(after(operand, *[array for array, _ in moves]))
    joined = lax.optimization_barrier((*came, *results))
    return joined[: len(came)], joined[len(came) :]


def over(bit):
    return partial(swap_bit, bit=bit)


class Gathered:
    def __init__(self, arrays, shape, blocked, moves):
        self.arrays = arrays
        self.shape = shape
        self.blocked = blocked
        self.moves = moves

    @property
    def count(self):
        return len(self.arrays)

    def start(self, refs, target, sems):
        for index, (source, spot) in enumerate(self.moves(refs, target)):
            pltpu.make_async_copy(source, spot, sems.at[index]).start()

    def wait(self, refs, target, sems):
        for index, (source, spot) in enumerate(self.moves(refs, target)):
            pltpu.make_async_copy(source, spot, sems.at[index]).wait()

    def columns(self, ref, cols):
        if not self.blocked:
            return ref[:, cols]
        block = ref[:, :, cols]
        return block.reshape(block.shape[0] * block.shape[1], block.shape[2])

    def rows(self, ref, cols):
        if not self.blocked:
            return ref[cols, :]
        of_device = ref.shape[1] * ref.shape[2]
        block = ref[cols.start // of_device : cols.stop // of_device]
        return block.reshape(cols.stop - cols.start, block.shape[3])


def plain(array):
    return Gathered([array], array.shape, False, lambda refs, target: [(refs[0], target)])


def gathered_first(one, two, rows):
    slots, _, cols = one.shape
    arrays = [one, sibling(one), two, sibling(two)]

    def moves(refs, target):
        chip = lax.axis_index("dp")
        core = lax.axis_index("blk")
        pairs = []
        for index, ref in enumerate(refs):
            bits = BITS_FIRST if index < 2 else BITS_SECOND
            which = core if index % 2 == 0 else 1 - core
            place = pl.ds(index // 2 * cols, cols)
            for slot in range(slots):
                owner = lax.bitwise_xor(chip, jnp.int32(relative(slot, bits)))
                pairs.append((ref.at[slot], target.at[owner * 2 + which, :, place]))
        return pairs

    return Gathered(arrays, (2 * slots, rows, 2 * cols), True, moves)


ANYWHERE = pl.BlockSpec(memory_space=pl.ANY)


VEC_COLS = 256


def pack_body(merged_ref, expand_ref, output_ref, tall_ref, *refs):
    vec_refs, first_ref, rest_ref = refs[:-2], refs[-2], refs[-1]
    rows, width = output_ref.shape
    vectors = jnp.concatenate(
        [
            ref[:, start : start + rows].astype(F32)
            for ref in vec_refs
            for start in range(0, ref.shape[1], rows)
        ],
        axis=0,
    )
    empty = jnp.zeros((16 - vectors.shape[0], rows), F32)
    vectors = jnp.concatenate([vectors, empty], axis=0).astype(BF)
    column = lax.broadcasted_iota(jnp.int32, (16, VEC_COLS), 1)
    line = lax.broadcasted_iota(jnp.int32, (16, VEC_COLS), 0)
    spread = jnp.where(column == line, 1.0, 0.0).astype(BF)
    first_ref[:, : 3 * width] = merged_ref[...]
    first_ref[:, 3 * width :] = dot(vectors, spread, TN).astype(BF)
    hidden_width = expand_ref.shape[1]
    rest_ref[:, :hidden_width] = expand_ref[...]
    rest_ref[:, hidden_width : hidden_width + width] = output_ref[...]
    for k in range(tall_ref.shape[0]):
        start = hidden_width + (1 + k) * width
        rest_ref[:, start : start + width] = tall_ref[k]


def pack(merged, expand, output, tall, vectors):
    rows, width = output.shape
    blocks = tall.shape[0] // rows
    first_cols = merged.shape[1] + VEC_COLS
    rest_cols = expand.shape[1] + (1 + blocks) * width
    return pl.pallas_call(
        pack_body,
        out_shape=[
            jax.ShapeDtypeStruct((rows, first_cols), BF),
            jax.ShapeDtypeStruct((rows, rest_cols), BF),
        ],
        compiler_params=pltpu.CompilerParams(vmem_limit_bytes=VMEM_BYTES),
        name="pack",
    )(merged, expand, output, tall.reshape(blocks, rows, width), *vectors)


def project_body(*refs, weight):
    count = weight.count
    x_ref = refs[0]
    sources = refs[1 : 1 + count]
    zt_ref, m_ref, w_ref, vec_ref, sems = refs[1 + count :]
    width = x_ref.shape[1]
    first = pl.program_id(0) == 0

    @pl.when(first)
    def _():
        weight.start(sources, w_ref, sems)

    z, _ = normed(x_ref[...].astype(F32))
    zt_ref[...] = jnp.transpose(z.astype(BF))

    @pl.when(first)
    def _():
        weight.wait(sources, w_ref, sems)
        extra = weight.columns(w_ref, slice(3 * width, 3 * width + 128))
        turned = jnp.transpose(extra.astype(F32))
        vec_ref[...] = turned[:16]

    a = (z * vec_ref[0:1, :] + vec_ref[1:2, :]).astype(BF)
    merged = dot(a, weight.columns(w_ref, slice(0, 3 * width)))
    query = (merged[:, :width] + vec_ref[2:3, :]) * (LOG2E * HEAD_DIM**-0.5)
    m_ref[:, :width] = query.astype(BF)
    m_ref[:, width : 2 * width] = merged[:, width : 2 * width].astype(BF)
    m_ref[:, 2 * width :] = (merged[:, 2 * width :] + vec_ref[3:4, :]).astype(BF)


def project(x, weight):
    rows, width = x.shape
    tile = row_tile(rows)
    row = lambda cols: pl.BlockSpec((tile, cols), lambda i: (i, 0))
    return pl.pallas_call(
        partial(project_body, weight=weight),
        grid=(rows // tile,),
        in_specs=[row(width)] + [ANYWHERE] * weight.count,
        out_specs=[
            pl.BlockSpec((width, tile), lambda i: (0, i)),
            row(3 * width), whole(weight.shape), whole((16, width)),
        ],
        out_shape=[
            jax.ShapeDtypeStruct((width, rows), BF),
            jax.ShapeDtypeStruct((rows, 3 * width), BF),
            jax.ShapeDtypeStruct(weight.shape, BF),
            jax.ShapeDtypeStruct((16, width), F32),
        ],
        scratch_shapes=[pltpu.SemaphoreType.DMA((64,))],
        compiler_params=params(1),
        cost_estimate=cost(6 * rows * width * width, 2 * rows * width * 5 + 6 * width * width),
        name="project",
    )(x, *weight.arrays)


def half_lanes(shape, head):
    return (lax.broadcasted_iota(jnp.int32, shape, 1) < HEAD_DIM) == (head == 0)


def only_head(values, head):
    return jnp.where(half_lanes(values.shape, head), values, jnp.zeros_like(values))


def ones_lane(rows):
    first = lax.broadcasted_iota(jnp.int32, (rows, LANES), 1) == 0
    return jnp.where(first, 1.0, 0.0).astype(BF)


AHEAD = 3


def attend_body(q_ref, k_ref, v_ref, mask_ref, o_ref, sum_ref, *, tile):
    keys = k_ref.shape[1]
    queries = q_ref.shape[1]
    ka = jnp.concatenate([k_ref[0], mask_ref[0]], axis=1)
    v_turned = jnp.transpose(v_ref[0])
    ones = jnp.ones((16, keys), BF)
    va = [
        jnp.concatenate([v_turned[:HEAD_DIM], ones], axis=0),
        jnp.concatenate([v_turned[HEAD_DIM:], ones], axis=0),
    ]
    one = ones_lane(tile)
    units = [(start, head) for start in range(0, queries, tile) for head in range(2)]

    def score(unit):
        start, head = unit
        q = only_head(q_ref[0, start : start + tile, :], head)
        return dot(ka, jnp.concatenate([q, one], axis=1), NT)

    ahead = [score(unit) for unit in units[:AHEAD]]
    parts = []
    for index, (start, head) in enumerate(units):
        if index + AHEAD < len(units):
            ahead.append(score(units[index + AHEAD]))
        s = ahead[index]
        top = jnp.max(s, axis=0, keepdims=True)
        p = jnp.exp2(s - top).astype(BF)
        mix = dot(va[head], p)
        total = mix[HEAD_DIM : HEAD_DIM + 1]
        parts.append(mix[:HEAD_DIM] / total)
        sum_ref[0, head : head + 1, start : start + tile] = top + jnp.log2(total)
        if head == 1:
            mixed = jnp.concatenate(parts, axis=0)
            o_ref[0, start : start + tile, :] = jnp.transpose(mixed)
            parts = []


def attend(merged, key_merged, key_base, mask, first=0, count=PAIRS):
    clips, queries, _ = merged.shape
    keys = key_merged.shape[1]
    tile = row_tile(queries)
    lanes = lambda rows, base: pl.BlockSpec((1, rows, LANES), lambda c, h: (c, 0, base + h))
    return pl.pallas_call(
        partial(attend_body, tile=tile),
        grid=(clips, count),
        in_specs=[
            lanes(queries, first),
            lanes(keys, key_base + first),
            lanes(keys, key_base + PAIRS + first),
            pl.BlockSpec((1, keys, LANES), lambda c, h: (c, 0, 0)),
        ],
        out_specs=[
            lanes(queries, 0),
            pl.BlockSpec((1, ROW_GROUP, queries), lambda c, h: (c, h, 0)),
        ],
        out_shape=[
            jax.ShapeDtypeStruct((clips, queries, count * LANES), F32),
            jax.ShapeDtypeStruct((clips, count * ROW_GROUP, queries), F32),
        ],
        compiler_params=params(2),
        cost_estimate=cost(
            clips * count * queries * keys * 2 * 4 * 256,
            clips * count * LANES * (2 * queries + 4 * keys + 4 * queries),
            clips * count * queries * keys * 2,
        ),
        name="attend",
    )(merged, key_merged, key_merged, mask)


def attend_back_body(
    q_ref, k_ref, v_ref, do_ref, mask_ref, sum_ref, delta_ref, *rest, tile
):
    dk_acc, dv_acc = rest[-2:]
    if len(rest) == 3:
        dq_ref, dk_ref, dv_ref = (rest[0].at[0, k] for k in range(3))
    else:
        dq_ref, dk_ref, dv_ref = (ref.at[0] for ref in rest[:3])
    queries = q_ref.shape[1]
    k = k_ref[0]
    v = v_ref[0]
    ka = jnp.concatenate([k, mask_ref[0]], axis=1)
    k_turned = jnp.transpose(k)
    one = ones_lane(tile)
    units = [(start, head) for start in range(0, queries, tile) for head in range(2)]

    def first(unit):
        start, head = unit
        rows = slice(start, start + tile)
        qm = only_head(q_ref[0, rows, :], head)
        dom = only_head(do_ref[0, rows, :], head)
        return qm, dom, dot(ka, jnp.concatenate([qm, one], axis=1), NT), dot(v, dom, NT)

    ahead = first(units[0])
    held = []
    for index, (start, head) in enumerate(units):
        rows = slice(start, start + tile)
        qm, dom, s, dp = ahead
        if index + 1 < len(units):
            ahead = first(units[index + 1])
        p = jnp.exp2(s - sum_ref[0, head : head + 1, rows])
        ds = (p * (dp - delta_ref[0, head : head + 1, rows])).astype(BF)
        dq = dot(k_turned[head * HEAD_DIM : (head + 1) * HEAD_DIM], ds)
        held.append((qm, dom, p.astype(BF), ds, dq))
        if head == 0:
            continue
        q_parts, do_parts, p_parts, ds_parts, dq_parts = zip(*held)
        held = []
        dq = jnp.transpose(jnp.concatenate(dq_parts, axis=0)) * (HEAD_DIM**-0.5)
        dq_ref[rows, :] = dq.astype(BF)
        dk = dot(jnp.concatenate(ds_parts, axis=1), jnp.concatenate(q_parts, axis=0))
        dv = dot(jnp.concatenate(p_parts, axis=1), jnp.concatenate(do_parts, axis=0))
        if start == 0:
            dk_acc[...] = dk
            dv_acc[...] = dv
        else:
            dk_acc[...] += dk
            dv_acc[...] += dv
    dk_ref[...] = (dk_acc[...] * (1.0 / LOG2E)).astype(BF)
    dv_ref[...] = dv_acc[...].astype(BF)


def attend_back(merged, key_merged, key_base, grad_out, mask, sums, delta, first=0, count=PAIRS):
    clips, queries, _ = merged.shape
    keys = key_merged.shape[1]
    tile = row_tile(queries)
    lanes = lambda rows, base: pl.BlockSpec((1, rows, LANES), lambda c, h: (c, 0, base + h))
    stat = lambda base: pl.BlockSpec((1, ROW_GROUP, queries), lambda c, h: (c, base + h, 0))
    columns = count * LANES
    if queries == keys:
        out_specs = [pl.BlockSpec((1, 3, keys, LANES), lambda c, h: (c, 0, 0, h))]
        out_shape = [jax.ShapeDtypeStruct((clips, 3, keys, columns), BF)]
    else:
        out_specs = [lanes(queries, 0), lanes(keys, 0), lanes(keys, 0)]
        out_shape = [
            jax.ShapeDtypeStruct((clips, queries, columns), BF),
            jax.ShapeDtypeStruct((clips, keys, columns), BF),
            jax.ShapeDtypeStruct((clips, keys, columns), BF),
        ]
    return pl.pallas_call(
        partial(attend_back_body, tile=tile),
        grid=(clips, count),
        in_specs=[
            lanes(queries, first),
            lanes(keys, key_base + first),
            lanes(keys, key_base + PAIRS + first),
            lanes(queries, first),
            pl.BlockSpec((1, keys, LANES), lambda c, h: (c, 0, 0)),
            stat(first),
            stat(first),
        ],
        out_specs=out_specs,
        out_shape=out_shape,
        scratch_shapes=[pltpu.VMEM((keys, LANES), F32), pltpu.VMEM((keys, LANES), F32)],
        compiler_params=params(2),
        cost_estimate=cost(
            clips * count * queries * keys * 2 * 9 * 256,
            clips * count * LANES * 2 * (3 * queries + 4 * keys),
            clips * count * queries * keys * 2,
        ),
        name="attend_back",
    )(merged, key_merged, key_merged, grad_out, mask, sums, delta)


ERF = (0.254829592, -0.284496736, 1.421413741, -1.453152027, 1.061405429)
ERF_P = 0.3275911


def gelu_both(u):
    bell = jnp.exp2(u * u * (-0.5 * LOG2E))
    t = 1.0 / (1.0 + (ERF_P * 0.5**0.5) * jnp.abs(u))
    series = ERF[4] * 0.5
    for term in ERF[3::-1]:
        series = series * t + term * 0.5
    tail = series * t * bell
    chance = jnp.where(u >= 0, 1.0 - tail, tail)
    return u * chance, chance + u * bell * 0.3989422804014327


def feed_body(*refs, chunk, mixes, wide, tall):
    x_ref, g_ref = refs[:2]
    o_refs = refs[2 : 2 + mixes]
    at = 2 + mixes
    wide_refs = refs[at : at + wide.count]
    at += wide.count
    tall_refs = refs[at : at + tall.count]
    at += tall.count
    (
        vecs_ref, be_ref, sel_ref,
        result_ref, h_ref, right_ref, gm_ref, left_ref, ga_ref, delta_ref, vec_ref,
        ebg_ref, wide_w, tall_w, wide_sems, tall_sems,
    ) = refs[at:]
    width = x_ref.shape[1]
    hidden_width = be_ref.shape[1]
    all_output = slice(hidden_width, hidden_width + width)

    @pl.when(pl.program_id(0) == 0)
    def _():
        wide.start(wide_refs, wide_w, wide_sems)
        tall.start(tall_refs, tall_w, tall_sems)
        vec_ref[...] = jnp.zeros_like(vec_ref)
        ebg_ref[...] = jnp.zeros_like(ebg_ref)
        wide.wait(wide_refs, wide_w, wide_sems)
        tall.wait(tall_refs, tall_w, tall_sems)

    o = jnp.concatenate([ref[...] for ref in o_refs], axis=1)
    att = o.astype(BF)
    left_ref[1] = jnp.transpose(att)
    middle = x_ref[...].astype(F32) + dot(att, wide.columns(wide_w, all_output)) + vecs_ref[4:5, :]
    z, scale = normed(middle)
    gain = vecs_ref[5:6, :]
    fi = (z * gain + vecs_ref[6:7, :]).astype(BF)
    left_ref[0] = jnp.transpose(fi)
    g = g_ref[...]
    out = middle + vecs_ref[7:8, :]
    u = jnp.zeros_like(middle)
    starts = list(range(0, hidden_width, chunk))

    def first(start):
        cols = slice(start, start + chunk)
        we = wide.columns(wide_w, cols)
        ws = tall.rows(tall_w, cols)
        return dot(fi, we) + be_ref[:, cols], dot(g, ws, NT), we, ws

    ahead = [first(start) for start in starts[:2]]
    for index, start in enumerate(starts):
        cols = slice(start, start + chunk)
        if index + 2 < len(starts):
            ahead.append(first(starts[index + 2]))
        pre, gh, we, ws = ahead[index]
        act, slope = gelu_both(pre)
        act = act.astype(BF)
        gp = (gh * slope).astype(BF)
        h_ref[:, cols] = act
        right_ref[:, cols] = gp
        ebg_ref[:, cols] += fold_rows(gp.astype(F32))
        out += dot(act, ws)
        u += dot(gp, we, NT)
    result_ref[...] = out.astype(BF)
    gf = g.astype(F32)
    gm = gf + norm_back(u, gain, z, scale)
    gm_ref[...] = gm
    gb = gm.astype(BF)
    right_ref[:, hidden_width:] = gb
    ga = dot(gb, wide.columns(wide_w, all_output), NT).astype(BF)
    ga_ref[...] = ga
    prod = ga.astype(F32) * o
    high = prod.astype(BF)
    low = (prod - high.astype(F32)).astype(BF)
    sel = sel_ref[...]
    delta_ref[...] = dot(sel, high, NT) + dot(sel, low, NT)
    vec_ref[:, :width] += fold_rows(u * z)
    vec_ref[:, width : 2 * width] += fold_rows(u)
    vec_ref[:, 2 * width : 3 * width] += fold_rows(gb.astype(F32))
    vec_ref[:, 3 * width :] += fold_rows(gf)


def feed(x, g, mixtures, wide, tall, vecs, be):
    rows, width = x.shape
    hidden_width = be.shape[1]
    tile = row_tile(rows)
    lane_head = jnp.arange(width)[None, :] // HEAD_DIM
    stat_row = jnp.arange(PAIRS * ROW_GROUP)[:, None]
    chosen = (stat_row // ROW_GROUP * 2 + stat_row % ROW_GROUP == lane_head) & (
        stat_row % ROW_GROUP < 2
    )
    select = chosen.astype(BF)
    row = lambda cols: pl.BlockSpec((tile, cols), lambda i: (i, 0))
    keep = lambda cols: pl.BlockSpec((ROW_GROUP, cols), lambda i: (0, 0))
    shape = jax.ShapeDtypeStruct
    return pl.pallas_call(
        partial(feed_body, chunk=768, mixes=len(mixtures), wide=wide, tall=tall),
        grid=(rows // tile,),
        in_specs=[
            row(width), row(width), *[row(mixture.shape[1]) for mixture in mixtures],
            *[ANYWHERE] * (wide.count + tall.count),
            whole(vecs.shape), whole((1, hidden_width)), whole(select.shape),
        ],
        out_specs=[
            row(width), row(hidden_width), row(hidden_width + width), row(width),
            pl.BlockSpec((2, width, tile), lambda i: (0, 0, i)), row(width),
            pl.BlockSpec((PAIRS * ROW_GROUP, tile), lambda i: (0, i)),
            keep(4 * width), keep(hidden_width),
        ],
        out_shape=[
            shape((rows, width), BF), shape((rows, hidden_width), BF),
            shape((rows, hidden_width + width), BF), shape((rows, width), F32),
            shape((2, width, rows), BF), shape((rows, width), BF),
            shape((PAIRS * ROW_GROUP, rows), F32),
            shape((ROW_GROUP, 4 * width), F32), shape((ROW_GROUP, hidden_width), F32),
        ],
        scratch_shapes=[
            pltpu.VMEM(wide.shape, BF), pltpu.VMEM(tall.shape, BF),
            pltpu.SemaphoreType.DMA((4,)), pltpu.SemaphoreType.DMA((4,)),
        ],
        compiler_params=params(1),
        cost_estimate=cost(
            rows * width * (4 * width + 8 * hidden_width),
            rows * (width * 20 + hidden_width * 4) + 2 * width * (width + 2 * hidden_width),
            rows * hidden_width * 2,
        ),
        name="feed",
    )(x, g, *mixtures, *wide.arrays, *tall.arrays, vecs, be, select)


def lay_out(value, outs, cols, rows, bits):
    if bits is None:
        outs[0][:, cols] = value.astype(BF)
        return
    keep_ref, send_ref = outs
    chip = lax.axis_index("dp")
    low_core = lax.axis_index("blk") == 0
    for owner in range(keep_ref.shape[0]):
        slot = slot_of(lax.bitwise_xor(chip, jnp.int32(owner)), bits)
        low = value[2 * owner * rows : (2 * owner + 1) * rows]
        high = value[(2 * owner + 1) * rows : (2 * owner + 2) * rows]
        keep_ref[slot, :, cols] = jnp.where(low_core, low, high).astype(BF)
        send_ref[slot, :, cols] = jnp.where(low_core, high, low).astype(BF)


def laid_out(few, columns, rows, bits):
    if bits is None:
        shapes = [(few, columns)]
    else:
        shapes = [(few // (2 * rows), rows, columns)] * 2
    return (
        [whole(shape) for shape in shapes],
        [jax.ShapeDtypeStruct(shape, BF) for shape in shapes],
    )


def outer_tall_body(left_ref, right_ref, side_ref, vec_ref, *outs, rows, blocks, bits):
    value = dot(left_ref[...], right_ref[...], TN)
    chunk, few = value.shape
    side = jnp.sum(side_ref[...], axis=0, keepdims=True)
    side = jnp.transpose(jnp.concatenate([side, jnp.zeros((127, chunk), F32)], axis=0))
    if bits is None:
        outs[0][:, :few] = value.astype(BF)
        outs[0][:, few:] = side.astype(BF)
        return
    keep_ref, send_ref, turned_ref = outs

    @pl.when(pl.program_id(0) == 0)
    def _():
        sums = [
            jnp.sum(vec_ref[:, k * few : (k + 1) * few], axis=0, keepdims=True) for k in range(4)
        ]
        empty = lambda count: jnp.zeros((count, few), F32)
        table = jnp.concatenate([empty(blocks), *sums, empty(124 - blocks)], axis=0)
        turned_ref[...] = jnp.transpose(table)

    side = jnp.broadcast_to(side[:, :1], (chunk, 128))
    chip = lax.axis_index("dp")
    low_core = lax.axis_index("blk") == 0
    lane = lax.broadcasted_iota(jnp.int32, (rows, 128), 1)
    of_device = blocks * rows
    chips = chunk // (2 * of_device)
    for index in range(chips):
        owner = pl.program_id(0) * chips + index
        slot = slot_of(lax.bitwise_xor(chip, owner), bits)
        pair = []
        for which in range(2):
            start = (2 * index + which) * of_device
            parts = [value[start + k * rows : start + (k + 1) * rows] for k in range(blocks)]
            first = pl.multiple_of((owner * 2 + which) * rows, 8)
            extra = turned_ref[pl.ds(first, rows), :]
            for k in range(blocks):
                column = side[start + k * rows : start + (k + 1) * rows]
                extra += jnp.where(lane == k, column, 0.0)
            pair.append(parts + [extra])
        for k, (low, high) in enumerate(zip(*pair)):
            cols = slice(k * few, k * few + low.shape[1])
            keep_ref[slot, :, cols] = jnp.where(low_core, low, high).astype(BF)
            send_ref[slot, :, cols] = jnp.where(low_core, high, low).astype(BF)


def outer_tall(left, right, side, vec, rows, blocks, bits):
    length, many = left.shape
    few = right.shape[1]
    chunk = 768
    if bits is None:
        out_specs = [pl.BlockSpec((chunk, few + 128), lambda i: (i, 0))]
        out_shape = [jax.ShapeDtypeStruct((many, few + 128), BF)]
        scratch = []
    else:
        shape = (many // (2 * blocks * rows), rows, blocks * few + 128)
        out_specs = [whole(shape)] * 2
        out_shape = [jax.ShapeDtypeStruct(shape, BF)] * 2
        scratch = [pltpu.VMEM((few, 128), F32)]
    return pl.pallas_call(
        partial(outer_tall_body, rows=rows, blocks=blocks, bits=bits),
        grid=(many // chunk,),
        in_specs=[
            pl.BlockSpec((length, chunk), lambda i: (0, i)),
            whole((length, few)),
            pl.BlockSpec((ROW_GROUP, chunk), lambda i: (0, i)),
            whole(vec.shape),
        ],
        out_specs=out_specs,
        out_shape=out_shape,
        scratch_shapes=scratch,
        compiler_params=params(1),
        cost_estimate=cost(2 * length * many * few, 2 * length * (many + few) + 2 * many * few),
        name="outer_tall",
    )(left, right, side, vec)


def outer_wide_body(left_ref, right_ref, *outs, rows, bits):
    lay_out(dot(left_ref[0], right_ref[...]), outs, slice(None), rows, bits)


def outer_wide(left, right, rows, bits):
    _, few, length = left.shape
    columns = right.shape[1]
    steps = columns // few
    _, out_shape = laid_out(few, columns, rows, bits)
    if bits is None:
        out_specs = [pl.BlockSpec((few, few), lambda i: (0, i))]
    else:
        out_specs = [pl.BlockSpec((few // (2 * rows), rows, few), lambda i: (0, 0, i))] * 2
    return pl.pallas_call(
        partial(outer_wide_body, rows=rows, bits=bits),
        grid=(steps,),
        in_specs=[
            pl.BlockSpec((1, few, length), lambda i: (i // (steps - 1), 0, 0)),
            pl.BlockSpec((length, few), lambda i: (0, i)),
        ],
        out_specs=out_specs,
        out_shape=out_shape,
        compiler_params=params(1),
        cost_estimate=cost(
            2 * length * few * columns, 2 * length * (2 * few + columns) + 2 * few * columns
        ),
        name="outer_wide",
    )(left, right)


def outer_merged_body(left_ref, w_ref, extra_ref, *refs, pieces, rows, bits):
    right_refs = refs[:pieces]
    outs = refs[pieces:-1]
    side_ref = refs[-1]
    step = pl.program_id(0)
    width = left_ref.shape[0]
    rights = [ref[0] for ref in right_refs]
    right = rights[0] if pieces == 1 else jnp.concatenate(rights, axis=1)
    z_grad = dot(left_ref[...], right)
    total = jnp.sum(fold_rows(right.astype(F32)), axis=0, keepdims=True)
    gain = extra_ref[:, 0:1].astype(F32)
    shift = extra_ref[:, 1:2].astype(F32)
    cols = pl.ds(pl.multiple_of(step * width, 128), width)
    lay_out(gain * z_grad + shift * total, outs, cols, rows, bits)
    w = w_ref[...].astype(F32)
    gain_grad = jnp.sum(w * z_grad, axis=1, keepdims=True)
    shift_grad = jnp.sum(w * total, axis=1, keepdims=True)
    turned = jnp.transpose(
        jnp.concatenate([total, jnp.zeros((127, width), F32)], axis=0)
    )[:, :1]
    lane = lax.broadcasted_iota(jnp.int32, (width, 128), 1)
    zero = jnp.zeros((), F32)
    bias_lane = jnp.where(step == 0, 2, jnp.where(step == 1, 4, 3))
    side = (
        jnp.where(lane == 0, gain_grad, zero)
        + jnp.where(lane == 1, shift_grad, zero)
        + jnp.where(lane == bias_lane, turned, zero)
    )

    @pl.when(step == 0)
    def _():
        side_ref[...] = side

    @pl.when(step > 0)
    def _():
        side_ref[...] += side

    @pl.when(step == 2)
    def _():
        lay_out(side_ref[...], outs, slice(3 * width, 3 * width + 128), rows, bits)


def outer_merged(left, weight, grads, rows, bits):
    few, length = left.shape
    out_specs, out_shape = laid_out(few, 3 * few + 128, rows, bits)
    return pl.pallas_call(
        partial(outer_merged_body, pieces=len(grads), rows=rows, bits=bits),
        grid=(3,),
        in_specs=[
            whole(left.shape),
            pl.BlockSpec((few, few), lambda i: (0, i)),
            pl.BlockSpec((few, 128), lambda i: (0, 3 * few // 128)),
        ]
        + [pl.BlockSpec((1, length, grad.shape[2]), lambda i: (i, 0, 0)) for grad in grads],
        out_specs=out_specs,
        out_shape=out_shape,
        scratch_shapes=[pltpu.VMEM((few, 128), F32)],
        compiler_params=params(1),
        cost_estimate=cost(6 * length * few * few, 8 * length * few + 12 * few * few),
        name="outer_merged",
    )(left, weight, weight, *grads)


def added(left, right):
    return (left.astype(F32) + right.astype(F32)).astype(BF)


def collect_plain(grads):
    total = lax.psum_scatter(grads, ("dp", "blk"), scatter_dimension=0, tiled=True)
    return total.astype(F32)


def halved(held, came):
    half = held.shape[0] // 2
    return added(held[:half], came[:half]), added(held[half:], came[half:])


def unproject_body(*refs, pieces):
    part_refs = refs[:pieces]
    w_ref, x_ref, vecs_ref, gm_ref, tg_ref = refs[pieces:]
    width = x_ref.shape[1]
    grads = [ref[k] for k in range(3) for ref in part_refs]
    u = dot(jnp.concatenate(grads, axis=1), w_ref[:, : 3 * width], NT)
    z, scale = normed(x_ref[...].astype(F32))
    back = norm_back(u, vecs_ref[0:1, :], z, scale)
    tg_ref[...] = (gm_ref[...] + back).astype(BF)


def unproject(grads, weight, x, vecs, gm):
    rows, width = x.shape
    tile = row_tile(rows)
    row = lambda cols: pl.BlockSpec((tile, cols), lambda i: (i, 0))
    return pl.pallas_call(
        partial(unproject_body, pieces=len(grads)),
        grid=(rows // tile,),
        in_specs=[pl.BlockSpec((3, tile, grad.shape[2]), lambda i: (0, i, 0)) for grad in grads]
        + [whole(weight.shape), row(width), whole(vecs.shape), row(width)],
        out_specs=row(width),
        out_shape=jax.ShapeDtypeStruct((rows, width), BF),
        compiler_params=params(1),
        cost_estimate=cost(6 * rows * width * width, 2 * rows * width * 8 + 6 * width * width),
        name="unproject",
    )(*grads, weight, x, vecs, gm)


def pad_rows(values, rows):
    return jnp.pad(values, ((0, 0), (0, rows - values.shape[1]), (0, 0)))


def trade_clips(values):
    if lax.axis_size("blk") != 2:
        return lax.all_to_all(values, "blk", 0, 1, tiled=True)
    clips, rows, width = values.shape
    core = lax.axis_index("blk")
    pairs = values.reshape(2, clips // 2, rows, width)
    low, high = pairs[0], pairs[1]
    mine = jnp.where(core == 0, low, high)
    other = sibling(jnp.where(core == 0, high, low))
    return jnp.concatenate(
        [jnp.where(core == 0, mine, other), jnp.where(core == 0, other, mine)], axis=1
    )


def trade_away(values):
    core = lax.axis_index("blk")
    half = values.shape[1] // 2
    low, high = values[:, :half], values[:, half:]
    return jnp.where(core == 0, low, high), jnp.where(core == 0, high, low)


def trade_home(mine, other):
    core = lax.axis_index("blk")
    return jnp.concatenate(
        [jnp.where(core == 0, mine, other), jnp.where(core == 0, other, mine)], axis=0
    )


def trade_back(values):
    if lax.axis_size("blk") != 2:
        return lax.all_to_all(values, "blk", 1, 0, tiled=True)
    mine, away = trade_away(values)
    return trade_home(mine, sibling(away))


def key_mask(counts, cycle, rows_dev, rows_pad):
    position = jnp.arange(cycle * rows_pad, dtype=jnp.int32)
    block = position // rows_pad
    offset = position % rows_pad
    column = block * ((rows_dev - 2) // FREQ) + (offset - 2) // FREQ
    seen = jnp.where(
        (offset < 2)[None, :], (block == 0)[None, :], column[None, :] < counts[:, None]
    ) & (offset < rows_dev)[None, :]
    lane = jnp.arange(LANES, dtype=jnp.int32)
    return jnp.where(seen[:, :, None] | (lane > 0)[None, None, :], 0.0, NEGATIVE).astype(BF)


GROUPS = ((0, 1), (1, 3), (4, 2))


def local(
    tokens, counts, attend_gain, attend_shift, merged_weight, query_bias, value_bias,
    output_weight, output_bias, feed_gain, feed_shift, expand_weight, expand_bias,
    shrink_weight, shrink_bias, cotangent,
):
    clips, rows_dev, width = tokens.shape
    chips, cycle = lax.axis_size("dp"), lax.axis_size("blk")
    quick = quick_mesh({"dp": chips, "blk": cycle})
    rows_pad = -(-rows_dev // 16) * 16
    traded = clips % cycle == 0
    weight_rows = merged_weight.shape[0]
    tall_rows = shrink_weight.shape[0]
    hidden_width = expand_weight.shape[1]
    devices = chips * cycle
    core = lax.axis_index("blk")
    blocks = tall_rows // weight_rows
    vectors = [
        vector.reshape(1, -1)
        for vector in (
            attend_gain, attend_shift, query_bias, value_bias,
            output_bias, feed_gain, feed_shift, shrink_bias, expand_bias,
        )
    ]
    wide_cols = hidden_width + width
    if quick:
        first_pack, rest = pack(
            merged_weight, expand_weight, output_weight, shrink_weight, vectors
        )
        held_first = grow(first_pack[None], 3)
        held_first = grow(held_first, 2)
        rest = lax.all_gather(rest, ("dp", "blk"), axis=0)
        wide = Gathered(
            [rest],
            (devices, weight_rows, wide_cols),
            True,
            lambda refs, target: [(refs[0].at[:, :, :wide_cols], target)],
        )
        tall = Gathered(
            [rest],
            (devices, blocks, weight_rows, width),
            True,
            lambda refs, target: [
                (refs[0].at[:, :, pl.ds(wide_cols + k * width, width)], target.at[:, k])
                for k in range(blocks)
            ],
        )
        cut = first_pack.shape[1] // 2
        one = grow(held_first[:, :, :cut], 0)
        two = grow(held_first[:, :, cut:], 1)
    else:
        gather = lambda block: plain(lax.all_gather(block, ("dp", "blk"), axis=0, tiled=True))
        vec_cols = jnp.concatenate(vectors, axis=1).reshape(-1, weight_rows).T
        vec_cols = jnp.pad(vec_cols, ((0, 0), (0, VEC_COLS - vec_cols.shape[1])))
        merged_full = gather(jnp.concatenate([merged_weight, vec_cols], axis=1))
        wide = gather(jnp.concatenate([expand_weight, output_weight], axis=1))
        tall = gather(shrink_weight)
    if quick:
        x = trade_clips(pad_rows(tokens, rows_pad))
        one = grow(one, 1, x)
        two = grow(two, 0, x)
        g = trade_clips(pad_rows(after(cotangent, one, two), rows_pad))
        merged_full = gathered_first(one, two, weight_rows)
    else:
        x = pad_rows(tokens, rows_pad)
        g = pad_rows(cotangent, rows_pad)
        if traded:
            x = trade_clips(x)
            g = trade_clips(g)
    held = clips // cycle if traded else clips
    own_counts = lax.dynamic_slice_in_dim(counts, core * held, held) if traded else counts
    queries = x.shape[1]
    total = held * queries
    x = x.reshape(total, width)
    g = g.reshape(total, width)
    mask = key_mask(own_counts, cycle, rows_dev, rows_pad)

    z_turned, merged, weight_flat, vecs = project(x, merged_full)
    weight_flat = weight_flat.reshape(devices * weight_rows, -1)
    bias_row = (
        vecs[8 : 8 + blocks].reshape(blocks, devices, weight_rows).transpose(1, 0, 2)
    ).reshape(1, hidden_width)
    merged = merged.reshape(held, queries, 3 * width)
    if traded:
        keys, key_base = merged, PAIRS
    else:
        keys = lax.all_gather(merged[:, :, width:], "blk", axis=1, tiled=True)
        key_base = 0
    mixture, sums = attend(merged, keys, key_base, mask)
    mixtures = [mixture.reshape(total, width)]
    (
        result, hidden, rights, grad_middle, lefts, grad_attended, delta, feed_vec, expand_vec,
    ) = feed(x, g, mixtures, wide, tall, vecs, bias_row)

    def home(values):
        values = values.reshape(held, queries, width)
        if traded:
            values = trade_back(values)
        return values[:, :rows_dev]

    bits = BITS_FIRST if quick else None
    wide_grad = outer_wide(lefts, rights, weight_rows, bits)
    delta = delta.reshape(PAIRS * ROW_GROUP, held, queries).transpose(1, 0, 2)
    grad_heads = grad_attended.reshape(held, queries, width)
    back = partial(attend_back, merged, keys, key_base)
    if quick:
        wide_keep, wide_send = wide_grad
        (wide_came,), (tall_keep, tall_send) = beside(
            [(wide_send, sibling)],
            lambda rows: outer_tall(
                rows, g, expand_vec, feed_vec, weight_rows, blocks, BITS_SECOND
            ),
            hidden,
        )
        wide_kept, wide_away = halved(wide_keep, wide_came)

        def back_group(index):
            first, count = GROUPS[index]
            return lambda rows: back(rows, mask, sums, delta, first, count)

        grads = []
        (tall_came,), part = beside(
            [(tall_send, sibling)], back_group(0), after(grad_heads, wide_kept, wide_away)
        )
        grads += part
        tall_kept, tall_away = halved(tall_keep, tall_came)
        for index, bit in ((1, 1), (2, 0)):
            (wide_came, tall_came), part = beside(
                [(wide_away, over(bit)), (tall_away, over(1 - bit))],
                back_group(index),
                after(grad_heads, grads[-1]),
            )
            grads += part
            if index == 1:
                wide_kept, wide_away = halved(wide_kept, wide_came)
                tall_kept, tall_away = halved(tall_kept, tall_came)
        grads = [
            part.transpose(1, 0, 2, 3).reshape(3, total, part.shape[3]) for part in grads
        ]
        late_kept, late_away = (
            jnp.concatenate(pair, axis=2)
            for pair in zip(halved(wide_kept, wide_came), halved(tall_kept, tall_came))
        )
        (late_came,), (merged_keep, merged_send) = beside(
            [(late_away, over(2))],
            lambda rows: outer_merged(rows, weight_flat, grads, weight_rows, bits),
            z_turned,
        )
        result_rows = after(result, merged_send).reshape(held, queries, width)
        result_kept, result_away = trade_away(result_rows)
        result_came = sibling(result_away)
        late_kept, late_away = halved(late_kept, late_came)
        merged_came = after(sibling(merged_send), late_away)
        merged_keep = merged_keep.reshape(2, 2, chips // 4, weight_rows, -1)
        merged_came = merged_came.reshape(merged_keep.shape)
        cut = merged_keep.shape[-1] // 256 * 128
        one = [added(merged_keep[k, ..., :cut], merged_came[k, ..., :cut]) for k in range(2)]
        two = [added(merged_keep[:, k, ..., cut:], merged_came[:, k, ..., cut:]) for k in range(2)]
        late_came = swap_bit(late_away, 3)
        (one_came, two_came), (tokens_grad,) = beside(
            [(one[1], over(1)), (two[1], over(0))],
            lambda rows: [unproject(grads, weight_flat, rows, vecs, grad_middle)],
            after(x, late_away),
        )
        one = [added(one[0][k], one_came[k]) for k in range(2)]
        two = [added(two[0][k], two_came[k]) for k in range(2)]
        one_came = swap_bit(one[1], 0)
        two_came = swap_bit(two[1], 1)
        result_came = after(result_came, one[1], two[1])
        result_home = trade_home(result_kept, result_came)[:, :rows_dev]
        one = added(one[0], one_came)
        two = added(two[0], two_came)
        merged_held = jnp.concatenate([one, two], axis=-1)
        merged_kept, merged_away = merged_held[:2], merged_held[2:]
        late_came = after(late_came, merged_away)
        tokens_home = home(tokens_grad)
        merged_came = after(swap_bit(merged_away, 2), tokens_home)
        merged_kept, merged_away = halved(merged_kept, merged_came)
        full = lambda kept, came: (kept.astype(F32) + came.astype(F32))[0]
        merged_grad = full(merged_kept, swap_bit(merged_away, 3))
        late_grad = full(late_kept, late_came)
        wide_cols = wide_keep.shape[2]
        wide_grad = late_grad[:, :wide_cols]
        tall_grad = late_grad[:, wide_cols:]
        shrink_grad = jnp.concatenate(
            [tall_grad[:, k * width : (k + 1) * width] for k in range(blocks)], axis=0
        )
        extra = tall_grad[:, blocks * width :]
        expand_bias_grad = extra[:, :blocks].T.reshape(-1)
        vec_wide = extra[:, blocks : blocks + 4].T
    else:
        result_home = home(result)
        tall_grad = outer_tall(hidden, g, expand_vec, feed_vec, weight_rows, blocks, None)[0]
        tall_grad = collect_plain(tall_grad)
        shrink_grad = tall_grad[:, :width]
        expand_bias_grad = tall_grad[:, width]
        vec_wide = lax.psum_scatter(
            jnp.sum(feed_vec, axis=0).reshape(4, width), ("dp", "blk"), scatter_dimension=1,
            tiled=True,
        )
        columns = []
        for first, count in GROUPS:
            parts = back(grad_heads, mask, sums, delta, first, count)
            if traded:
                parts = [parts[0][:, k] for k in range(3)]
            else:
                scatter = partial(
                    lax.psum_scatter, axis_name="blk", scatter_dimension=1, tiled=True
                )
                parts = [parts[0], scatter(parts[1]), scatter(parts[2])]
            columns.append(jnp.stack(parts))
        grads = [jnp.concatenate(columns, axis=3).reshape(3, total, width)]
        merged_grad = outer_merged(z_turned, weight_flat, grads, weight_rows, None)
        tokens_home = home(unproject(grads, weight_flat, x, vecs, grad_middle))
        merged_grad = collect_plain(merged_grad[0])
        wide_grad = collect_plain(wide_grad[0])
    vec_merged = merged_grad[:, 3 * width :]

    return (
        result_home,
        tokens_home,
        vec_merged[:, 0],
        vec_merged[:, 1],
        merged_grad[:, : 3 * width],
        vec_merged[:, 2],
        vec_merged[:, 3],
        wide_grad[:, hidden_width : hidden_width + width],
        vec_wide[2],
        vec_wide[0],
        vec_wide[1],
        wide_grad[:, :hidden_width],
        expand_bias_grad,
        shrink_grad,
        vec_wide[3],
    )


def solution(mesh):
    rows = P("dp", "blk", None)
    vector = P(("dp", "blk"))
    matrix = P(("dp", "blk"), None)
    in_specs = (
        rows, P("dp"), vector, vector, matrix, vector, vector, matrix, vector, vector, vector,
        matrix, vector, matrix, vector, rows,
    )
    out_specs = (
        rows, rows, vector, vector, matrix, vector, vector, matrix, vector, vector, vector,
        matrix, vector, matrix, vector,
    )
    return jax.shard_map(local, mesh=mesh, in_specs=in_specs, out_specs=out_specs, check_vma=False)
```

```python
from functools import partial

import jax
import jax.numpy as jnp
from jax import lax
from jax.experimental import pallas as pl
from jax.experimental.pallas import tpu as pltpu
from jax.sharding import PartitionSpec as P

HEADS = 12
HEAD_DIM = 64
FREQ = 12
EPSILON = 1e-06
NEGATIVE = -1e30
LOG2E = 1.4426950408889634
PAIRS = HEADS // 2
LANES = 2 * HEAD_DIM
ROW_GROUP = 8
VMEM_BYTES = 60 * 1024 * 1024

BF = jnp.bfloat16
F32 = jnp.float32

NN = (((1,), (0,)), ((), ()))
NT = (((1,), (1,)), ((), ()))
TN = (((0,), (0,)), ((), ()))


def dot(left, right, dims=NN):
    return lax.dot_general(left, right, dims, preferred_element_type=F32)


def params(count):
    return pltpu.CompilerParams(
        dimension_semantics=("arbitrary",) * count, vmem_limit_bytes=VMEM_BYTES
    )


def whole(shape):
    return pl.BlockSpec(shape, lambda *_: (0,) * len(shape), pipeline_mode=pl.Buffered(1))


def cost(flops, bytes_accessed, transcendentals=0):
    return pl.CostEstimate(
        flops=int(flops), bytes_accessed=int(bytes_accessed), transcendentals=int(transcendentals)
    )


def normed(values):
    mean_row = jnp.mean(values, axis=-1, keepdims=True)
    centered = values - mean_row
    spread = jnp.mean(centered * centered, axis=-1, keepdims=True)
    scale = lax.rsqrt(spread + EPSILON)
    return centered * scale, scale


def norm_back(upstream, gain_row, z, scale):
    w = upstream * gain_row
    return scale * (
        w - jnp.mean(w, axis=-1, keepdims=True) - z * jnp.mean(w * z, axis=-1, keepdims=True)
    )


def fold_rows(values):
    rows, width = values.shape
    return jnp.sum(values.reshape(rows // ROW_GROUP, ROW_GROUP, width), axis=0)


def row_tile(rows):
    return 256 if rows % 256 == 0 else rows


def tiles_of(total, size):
    size = size if total % size == 0 else total
    return [slice(start, start + size) for start in range(0, total, size)]


BITS_FIRST = (3, 2, 0, 1)
BITS_SECOND = (3, 2, 1, 0)


def after(value, *others):
    return lax.optimization_barrier((value, *others))[0]


def quick_mesh(sizes):
    return sizes["dp"] == 16 and sizes["blk"] == 2


def swap_bit(block, bit):
    return lax.ppermute(block, "dp", [(i, i ^ (1 << bit)) for i in range(lax.axis_size("dp"))])


def sibling(block):
    return lax.ppermute(block, "blk", [(0, 1), (1, 0)])


def grow(held, bit, *others):
    return jnp.concatenate([held, after(swap_bit(held, bit), *others)], axis=0)


def relative(slot, bits):
    return sum(((slot >> k) & 1) << bit for k, bit in enumerate(bits))


def slot_of(offset, bits):
    return sum(((offset >> bit) & 1) << k for k, bit in enumerate(bits))


def beside(moves, kernel, operand):
    came = [route(array) for array, route in moves]
    results = kernel(after(operand, *[array for array, _ in moves]))
    joined = lax.optimization_barrier((*came, *results))
    return joined[: len(came)], joined[len(came) :]


def over(bit):
    return partial(swap_bit, bit=bit)


class Gathered:
    def __init__(self, arrays, shape, blocked, moves):
        self.arrays = arrays
        self.shape = shape
        self.blocked = blocked
        self.moves = moves

    @property
    def count(self):
        return len(self.arrays)

    def start(self, refs, target, sems):
        for index, (source, spot) in enumerate(self.moves(refs, target)):
            pltpu.make_async_copy(source, spot, sems.at[index]).start()

    def wait(self, refs, target, sems):
        for index, (source, spot) in enumerate(self.moves(refs, target)):
            pltpu.make_async_copy(source, spot, sems.at[index]).wait()

    def columns(self, ref, cols):
        if not self.blocked:
            return ref[:, cols]
        block = ref[:, :, cols]
        return block.reshape(block.shape[0] * block.shape[1], block.shape[2])

    def rows(self, ref, cols):
        if not self.blocked:
            return ref[cols, :]
        of_device = ref.shape[1] * ref.shape[2]
        block = ref[cols.start // of_device : cols.stop // of_device]
        return block.reshape(cols.stop - cols.start, block.shape[3])


def plain(array):
    return Gathered([array], array.shape, False, lambda refs, target: [(refs[0], target)])


def gathered_first(one, two, rows):
    slots, _, cols = one.shape
    arrays = [one, sibling(one), two, sibling(two)]

    def moves(refs, target):
        chip = lax.axis_index("dp")
        core = lax.axis_index("blk")
        pairs = []
        for index, ref in enumerate(refs):
            bits = BITS_FIRST if index < 2 else BITS_SECOND
            which = core if index % 2 == 0 else 1 - core
            place = pl.ds(index // 2 * cols, cols)
            for slot in range(slots):
                owner = lax.bitwise_xor(chip, jnp.int32(relative(slot, bits)))
                pairs.append((ref.at[slot], target.at[owner * 2 + which, :, place]))
        return pairs

    return Gathered(arrays, (2 * slots, rows, 2 * cols), True, moves)


ANYWHERE = pl.BlockSpec(memory_space=pl.ANY)


VEC_COLS = 256


def pack_body(merged_ref, expand_ref, output_ref, tall_ref, *refs):
    vec_refs, first_ref, rest_ref = refs[:-2], refs[-2], refs[-1]
    rows, width = output_ref.shape
    vectors = jnp.concatenate(
        [
            ref[:, start : start + rows].astype(F32)
            for ref in vec_refs
            for start in range(0, ref.shape[1], rows)
        ],
        axis=0,
    )
    empty = jnp.zeros((16 - vectors.shape[0], rows), F32)
    vectors = jnp.concatenate([vectors, empty], axis=0).astype(BF)
    column = lax.broadcasted_iota(jnp.int32, (16, VEC_COLS), 1)
    line = lax.broadcasted_iota(jnp.int32, (16, VEC_COLS), 0)
    spread = jnp.where(column == line, 1.0, 0.0).astype(BF)
    first_ref[:, : 3 * width] = merged_ref[...]
    first_ref[:, 3 * width :] = dot(vectors, spread, TN).astype(BF)
    hidden_width = expand_ref.shape[1]
    rest_ref[:, :hidden_width] = expand_ref[...]
    rest_ref[:, hidden_width : hidden_width + width] = output_ref[...]
    for k in range(tall_ref.shape[0]):
        start = hidden_width + (1 + k) * width
        rest_ref[:, start : start + width] = tall_ref[k]


def pack(merged, expand, output, tall, vectors):
    rows, width = output.shape
    blocks = tall.shape[0] // rows
    first_cols = merged.shape[1] + VEC_COLS
    rest_cols = expand.shape[1] + (1 + blocks) * width
    return pl.pallas_call(
        pack_body,
        out_shape=[
            jax.ShapeDtypeStruct((rows, first_cols), BF),
            jax.ShapeDtypeStruct((rows, rest_cols), BF),
        ],
        compiler_params=pltpu.CompilerParams(vmem_limit_bytes=VMEM_BYTES),
        name="pack",
    )(merged, expand, output, tall.reshape(blocks, rows, width), *vectors)


def project_body(*refs, weight):
    count = weight.count
    x_ref = refs[0]
    sources = refs[1 : 1 + count]
    zt_ref, m_ref, w_ref, vec_ref, sems = refs[1 + count :]
    width = x_ref.shape[1]
    first = pl.program_id(0) == 0

    @pl.when(first)
    def _():
        weight.start(sources, w_ref, sems)

    z, _ = normed(x_ref[...].astype(F32))
    zt_ref[...] = jnp.transpose(z.astype(BF))

    @pl.when(first)
    def _():
        weight.wait(sources, w_ref, sems)
        extra = weight.columns(w_ref, slice(3 * width, 3 * width + 128))
        turned = jnp.transpose(extra.astype(F32))
        vec_ref[...] = turned[:16]

    a = (z * vec_ref[0:1, :] + vec_ref[1:2, :]).astype(BF)
    merged = dot(a, weight.columns(w_ref, slice(0, 3 * width)))
    query = (merged[:, :width] + vec_ref[2:3, :]) * (LOG2E * HEAD_DIM**-0.5)
    m_ref[:, :width] = query.astype(BF)
    m_ref[:, width : 2 * width] = merged[:, width : 2 * width].astype(BF)
    m_ref[:, 2 * width :] = (merged[:, 2 * width :] + vec_ref[3:4, :]).astype(BF)


def project(x, weight):
    rows, width = x.shape
    tile = row_tile(rows)
    row = lambda cols: pl.BlockSpec((tile, cols), lambda i: (i, 0))
    return pl.pallas_call(
        partial(project_body, weight=weight),
        grid=(rows // tile,),
        in_specs=[row(width)] + [ANYWHERE] * weight.count,
        out_specs=[
            pl.BlockSpec((width, tile), lambda i: (0, i)),
            row(3 * width), whole(weight.shape), whole((16, width)),
        ],
        out_shape=[
            jax.ShapeDtypeStruct((width, rows), BF),
            jax.ShapeDtypeStruct((rows, 3 * width), BF),
            jax.ShapeDtypeStruct(weight.shape, BF),
            jax.ShapeDtypeStruct((16, width), F32),
        ],
        scratch_shapes=[pltpu.SemaphoreType.DMA((64,))],
        compiler_params=params(1),
        cost_estimate=cost(6 * rows * width * width, 2 * rows * width * 5 + 6 * width * width),
        name="project",
    )(x, *weight.arrays)


def half_lanes(shape, head):
    return (lax.broadcasted_iota(jnp.int32, shape, 1) < HEAD_DIM) == (head == 0)


def only_head(values, head):
    return jnp.where(half_lanes(values.shape, head), values, jnp.zeros_like(values))


def ones_lane(rows):
    first = lax.broadcasted_iota(jnp.int32, (rows, LANES), 1) == 0
    return jnp.where(first, 1.0, 0.0).astype(BF)


AHEAD = 3


def attend_body(q_ref, k_ref, v_ref, mask_ref, o_ref, sum_ref, *, tile):
    keys = k_ref.shape[1]
    queries = q_ref.shape[1]
    ka = jnp.concatenate([k_ref[0], mask_ref[0]], axis=1)
    v_turned = jnp.transpose(v_ref[0])
    ones = jnp.ones((16, keys), BF)
    va = [
        jnp.concatenate([v_turned[:HEAD_DIM], ones], axis=0),
        jnp.concatenate([v_turned[HEAD_DIM:], ones], axis=0),
    ]
    one = ones_lane(tile)
    units = [(start, head) for start in range(0, queries, tile) for head in range(2)]

    def score(unit):
        start, head = unit
        q = only_head(q_ref[0, start : start + tile, :], head)
        return dot(ka, jnp.concatenate([q, one], axis=1), NT)

    ahead = [score(unit) for unit in units[:AHEAD]]
    parts = []
    for index, (start, head) in enumerate(units):
        if index + AHEAD < len(units):
            ahead.append(score(units[index + AHEAD]))
        s = ahead[index]
        top = jnp.max(s, axis=0, keepdims=True)
        p = jnp.exp2(s - top).astype(BF)
        mix = dot(va[head], p)
        total = mix[HEAD_DIM : HEAD_DIM + 1]
        parts.append(mix[:HEAD_DIM] / total)
        sum_ref[0, head : head + 1, start : start + tile] = top + jnp.log2(total)
        if head == 1:
            mixed = jnp.concatenate(parts, axis=0)
            o_ref[0, start : start + tile, :] = jnp.transpose(mixed)
            parts = []


def attend(merged, key_merged, key_base, mask, first=0, count=PAIRS):
    clips, queries, _ = merged.shape
    keys = key_merged.shape[1]
    tile = row_tile(queries)
    lanes = lambda rows, base: pl.BlockSpec((1, rows, LANES), lambda c, h: (c, 0, base + h))
    return pl.pallas_call(
        partial(attend_body, tile=tile),
        grid=(clips, count),
        in_specs=[
            lanes(queries, first),
            lanes(keys, key_base + first),
            lanes(keys, key_base + PAIRS + first),
            pl.BlockSpec((1, keys, LANES), lambda c, h: (c, 0, 0)),
        ],
        out_specs=[
            lanes(queries, 0),
            pl.BlockSpec((1, ROW_GROUP, queries), lambda c, h: (c, h, 0)),
        ],
        out_shape=[
            jax.ShapeDtypeStruct((clips, queries, count * LANES), F32),
            jax.ShapeDtypeStruct((clips, count * ROW_GROUP, queries), F32),
        ],
        compiler_params=params(2),
        cost_estimate=cost(
            clips * count * queries * keys * 2 * 4 * 256,
            clips * count * LANES * (2 * queries + 4 * keys + 4 * queries),
            clips * count * queries * keys * 2,
        ),
        name="attend",
    )(merged, key_merged, key_merged, mask)


def attend_back_body(
    q_ref, k_ref, v_ref, do_ref, mask_ref, sum_ref, delta_ref, *rest, tile
):
    dk_acc, dv_acc = rest[-2:]
    if len(rest) == 3:
        dq_ref, dk_ref, dv_ref = (rest[0].at[0, k] for k in range(3))
    else:
        dq_ref, dk_ref, dv_ref = (ref.at[0] for ref in rest[:3])
    queries = q_ref.shape[1]
    k = k_ref[0]
    v = v_ref[0]
    ka = jnp.concatenate([k, mask_ref[0]], axis=1)
    k_turned = jnp.transpose(k)
    one = ones_lane(tile)
    units = [(start, head) for start in range(0, queries, tile) for head in range(2)]

    def first(unit):
        start, head = unit
        rows = slice(start, start + tile)
        qm = only_head(q_ref[0, rows, :], head)
        dom = only_head(do_ref[0, rows, :], head)
        return qm, dom, dot(ka, jnp.concatenate([qm, one], axis=1), NT), dot(v, dom, NT)

    ahead = first(units[0])
    held = []
    for index, (start, head) in enumerate(units):
        rows = slice(start, start + tile)
        qm, dom, s, dp = ahead
        if index + 1 < len(units):
            ahead = first(units[index + 1])
        p = jnp.exp2(s - sum_ref[0, head : head + 1, rows])
        ds = (p * (dp - delta_ref[0, head : head + 1, rows])).astype(BF)
        dq = dot(k_turned[head * HEAD_DIM : (head + 1) * HEAD_DIM], ds)
        held.append((qm, dom, p.astype(BF), ds, dq))
        if head == 0:
            continue
        q_parts, do_parts, p_parts, ds_parts, dq_parts = zip(*held)
        held = []
        dq = jnp.transpose(jnp.concatenate(dq_parts, axis=0)) * (HEAD_DIM**-0.5)
        dq_ref[rows, :] = dq.astype(BF)
        dk = dot(jnp.concatenate(ds_parts, axis=1), jnp.concatenate(q_parts, axis=0))
        dv = dot(jnp.concatenate(p_parts, axis=1), jnp.concatenate(do_parts, axis=0))
        if start == 0:
            dk_acc[...] = dk
            dv_acc[...] = dv
        else:
            dk_acc[...] += dk
            dv_acc[...] += dv
    dk_ref[...] = (dk_acc[...] * (1.0 / LOG2E)).astype(BF)
    dv_ref[...] = dv_acc[...].astype(BF)


def attend_back(merged, key_merged, key_base, grad_out, mask, sums, delta, first=0, count=PAIRS):
    clips, queries, _ = merged.shape
    keys = key_merged.shape[1]
    tile = row_tile(queries)
    lanes = lambda rows, base: pl.BlockSpec((1, rows, LANES), lambda c, h: (c, 0, base + h))
    stat = lambda base: pl.BlockSpec((1, ROW_GROUP, queries), lambda c, h: (c, base + h, 0))
    columns = count * LANES
    if queries == keys:
        out_specs = [pl.BlockSpec((1, 3, keys, LANES), lambda c, h: (c, 0, 0, h))]
        out_shape = [jax.ShapeDtypeStruct((clips, 3, keys, columns), BF)]
    else:
        out_specs = [lanes(queries, 0), lanes(keys, 0), lanes(keys, 0)]
        out_shape = [
            jax.ShapeDtypeStruct((clips, queries, columns), BF),
            jax.ShapeDtypeStruct((clips, keys, columns), BF),
            jax.ShapeDtypeStruct((clips, keys, columns), BF),
        ]
    return pl.pallas_call(
        partial(attend_back_body, tile=tile),
        grid=(clips, count),
        in_specs=[
            lanes(queries, first),
            lanes(keys, key_base + first),
            lanes(keys, key_base + PAIRS + first),
            lanes(queries, first),
            pl.BlockSpec((1, keys, LANES), lambda c, h: (c, 0, 0)),
            stat(first),
            stat(first),
        ],
        out_specs=out_specs,
        out_shape=out_shape,
        scratch_shapes=[pltpu.VMEM((keys, LANES), F32), pltpu.VMEM((keys, LANES), F32)],
        compiler_params=params(2),
        cost_estimate=cost(
            clips * count * queries * keys * 2 * 9 * 256,
            clips * count * LANES * 2 * (3 * queries + 4 * keys),
            clips * count * queries * keys * 2,
        ),
        name="attend_back",
    )(merged, key_merged, key_merged, grad_out, mask, sums, delta)


ERF = (0.254829592, -0.284496736, 1.421413741, -1.453152027, 1.061405429)
ERF_P = 0.3275911


def gelu_both(u):
    bell = jnp.exp2(u * u * (-0.5 * LOG2E))
    t = 1.0 / (1.0 + (ERF_P * 0.5**0.5) * jnp.abs(u))
    series = ERF[4] * 0.5
    for term in ERF[3::-1]:
        series = series * t + term * 0.5
    tail = series * t * bell
    chance = jnp.where(u >= 0, 1.0 - tail, tail)
    return u * chance, chance + u * bell * 0.3989422804014327


def feed_body(*refs, chunk, mixes, wide, tall):
    x_ref, g_ref = refs[:2]
    o_refs = refs[2 : 2 + mixes]
    at = 2 + mixes
    wide_refs = refs[at : at + wide.count]
    at += wide.count
    tall_refs = refs[at : at + tall.count]
    at += tall.count
    (
        vecs_ref, be_ref, sel_ref,
        result_ref, h_ref, right_ref, gm_ref, left_ref, ga_ref, delta_ref, vec_ref,
        ebg_ref, wide_w, tall_w, wide_sems, tall_sems,
    ) = refs[at:]
    width = x_ref.shape[1]
    hidden_width = be_ref.shape[1]
    all_output = slice(hidden_width, hidden_width + width)

    @pl.when(pl.program_id(0) == 0)
    def _():
        wide.start(wide_refs, wide_w, wide_sems)
        tall.start(tall_refs, tall_w, tall_sems)
        vec_ref[...] = jnp.zeros_like(vec_ref)
        ebg_ref[...] = jnp.zeros_like(ebg_ref)
        wide.wait(wide_refs, wide_w, wide_sems)
        tall.wait(tall_refs, tall_w, tall_sems)

    o = jnp.concatenate([ref[...] for ref in o_refs], axis=1)
    att = o.astype(BF)
    left_ref[1] = jnp.transpose(att)
    middle = x_ref[...].astype(F32) + dot(att, wide.columns(wide_w, all_output)) + vecs_ref[4:5, :]
    z, scale = normed(middle)
    gain = vecs_ref[5:6, :]
    fi = (z * gain + vecs_ref[6:7, :]).astype(BF)
    left_ref[0] = jnp.transpose(fi)
    g = g_ref[...]
    out = middle + vecs_ref[7:8, :]
    u = jnp.zeros_like(middle)
    starts = list(range(0, hidden_width, chunk))

    def first(start):
        cols = slice(start, start + chunk)
        we = wide.columns(wide_w, cols)
        ws = tall.rows(tall_w, cols)
        return dot(fi, we) + be_ref[:, cols], dot(g, ws, NT), we, ws

    ahead = [first(start) for start in starts[:3]]
    for index, start in enumerate(starts):
        cols = slice(start, start + chunk)
        if index + 3 < len(starts):
            ahead.append(first(starts[index + 3]))
        pre, gh, we, ws = ahead[index]
        act, slope = gelu_both(pre)
        act = act.astype(BF)
        gp = (gh * slope).astype(BF)
        h_ref[:, cols] = act
        right_ref[:, cols] = gp
        ebg_ref[:, cols] += fold_rows(gp.astype(F32))
        out += dot(act, ws)
        u += dot(gp, we, NT)
    result_ref[...] = out.astype(BF)
    gf = g.astype(F32)
    gm = gf + norm_back(u, gain, z, scale)
    gm_ref[...] = gm
    gb = gm.astype(BF)
    right_ref[:, hidden_width:] = gb
    ga = dot(gb, wide.columns(wide_w, all_output), NT).astype(BF)
    ga_ref[...] = ga
    prod = ga.astype(F32) * o
    high = prod.astype(BF)
    low = (prod - high.astype(F32)).astype(BF)
    sel = sel_ref[...]
    delta_ref[...] = dot(sel, high, NT) + dot(sel, low, NT)
    vec_ref[:, :width] += fold_rows(u * z)
    vec_ref[:, width : 2 * width] += fold_rows(u)
    vec_ref[:, 2 * width : 3 * width] += fold_rows(gb.astype(F32))
    vec_ref[:, 3 * width :] += fold_rows(gf)


def feed(x, g, mixtures, wide, tall, vecs, be):
    rows, width = x.shape
    hidden_width = be.shape[1]
    tile = row_tile(rows)
    lane_head = jnp.arange(width)[None, :] // HEAD_DIM
    stat_row = jnp.arange(PAIRS * ROW_GROUP)[:, None]
    chosen = (stat_row // ROW_GROUP * 2 + stat_row % ROW_GROUP == lane_head) & (
        stat_row % ROW_GROUP < 2
    )
    select = chosen.astype(BF)
    row = lambda cols: pl.BlockSpec((tile, cols), lambda i: (i, 0))
    keep = lambda cols: pl.BlockSpec((ROW_GROUP, cols), lambda i: (0, 0))
    shape = jax.ShapeDtypeStruct
    return pl.pallas_call(
        partial(feed_body, chunk=768, mixes=len(mixtures), wide=wide, tall=tall),
        grid=(rows // tile,),
        in_specs=[
            row(width), row(width), *[row(mixture.shape[1]) for mixture in mixtures],
            *[ANYWHERE] * (wide.count + tall.count),
            whole(vecs.shape), whole((1, hidden_width)), whole(select.shape),
        ],
        out_specs=[
            row(width), row(hidden_width), row(hidden_width + width), row(width),
            pl.BlockSpec((2, width, tile), lambda i: (0, 0, i)), row(width),
            pl.BlockSpec((PAIRS * ROW_GROUP, tile), lambda i: (0, i)),
            keep(4 * width), keep(hidden_width),
        ],
        out_shape=[
            shape((rows, width), BF), shape((rows, hidden_width), BF),
            shape((rows, hidden_width + width), BF), shape((rows, width), F32),
            shape((2, width, rows), BF), shape((rows, width), BF),
            shape((PAIRS * ROW_GROUP, rows), F32),
            shape((ROW_GROUP, 4 * width), F32), shape((ROW_GROUP, hidden_width), F32),
        ],
        scratch_shapes=[
            pltpu.VMEM(wide.shape, BF), pltpu.VMEM(tall.shape, BF),
            pltpu.SemaphoreType.DMA((4,)), pltpu.SemaphoreType.DMA((4,)),
        ],
        compiler_params=params(1),
        cost_estimate=cost(
            rows * width * (4 * width + 8 * hidden_width),
            rows * (width * 20 + hidden_width * 4) + 2 * width * (width + 2 * hidden_width),
            rows * hidden_width * 2,
        ),
        name="feed",
    )(x, g, *mixtures, *wide.arrays, *tall.arrays, vecs, be, select)


def lay_out(value, outs, cols, rows, bits):
    if bits is None:
        outs[0][:, cols] = value.astype(BF)
        return
    keep_ref, send_ref = outs
    chip = lax.axis_index("dp")
    low_core = lax.axis_index("blk") == 0
    for owner in range(keep_ref.shape[0]):
        slot = slot_of(lax.bitwise_xor(chip, jnp.int32(owner)), bits)
        low = value[2 * owner * rows : (2 * owner + 1) * rows]
        high = value[(2 * owner + 1) * rows : (2 * owner + 2) * rows]
        keep_ref[slot, :, cols] = jnp.where(low_core, low, high).astype(BF)
        send_ref[slot, :, cols] = jnp.where(low_core, high, low).astype(BF)


def laid_out(few, columns, rows, bits):
    if bits is None:
        shapes = [(few, columns)]
    else:
        shapes = [(few // (2 * rows), rows, columns)] * 2
    return (
        [whole(shape) for shape in shapes],
        [jax.ShapeDtypeStruct(shape, BF) for shape in shapes],
    )


def outer_tall_body(left_ref, right_ref, side_ref, vec_ref, *outs, rows, blocks, bits):
    value = dot(left_ref[...], right_ref[...], TN)
    chunk, few = value.shape
    side = jnp.sum(side_ref[...], axis=0, keepdims=True)
    side = jnp.transpose(jnp.concatenate([side, jnp.zeros((127, chunk), F32)], axis=0))
    if bits is None:
        outs[0][:, :few] = value.astype(BF)
        outs[0][:, few:] = side.astype(BF)
        return
    keep_ref, send_ref, turned_ref = outs

    @pl.when(pl.program_id(0) == 0)
    def _():
        sums = [
            jnp.sum(vec_ref[:, k * few : (k + 1) * few], axis=0, keepdims=True) for k in range(4)
        ]
        empty = lambda count: jnp.zeros((count, few), F32)
        table = jnp.concatenate([empty(blocks), *sums, empty(124 - blocks)], axis=0)
        turned_ref[...] = jnp.transpose(table)

    side = jnp.broadcast_to(side[:, :1], (chunk, 128))
    chip = lax.axis_index("dp")
    low_core = lax.axis_index("blk") == 0
    lane = lax.broadcasted_iota(jnp.int32, (rows, 128), 1)
    of_device = blocks * rows
    chips = chunk // (2 * of_device)
    for index in range(chips):
        owner = pl.program_id(0) * chips + index
        slot = slot_of(lax.bitwise_xor(chip, owner), bits)
        pair = []
        for which in range(2):
            start = (2 * index + which) * of_device
            parts = [value[start + k * rows : start + (k + 1) * rows] for k in range(blocks)]
            first = pl.multiple_of((owner * 2 + which) * rows, 8)
            extra = turned_ref[pl.ds(first, rows), :]
            for k in range(blocks):
                column = side[start + k * rows : start + (k + 1) * rows]
                extra += jnp.where(lane == k, column, 0.0)
            pair.append(parts + [extra])
        for k, (low, high) in enumerate(zip(*pair)):
            cols = slice(k * few, k * few + low.shape[1])
            keep_ref[slot, :, cols] = jnp.where(low_core, low, high).astype(BF)
            send_ref[slot, :, cols] = jnp.where(low_core, high, low).astype(BF)


def outer_tall(left, right, side, vec, rows, blocks, bits):
    length, many = left.shape
    few = right.shape[1]
    chunk = 768
    if bits is None:
        out_specs = [pl.BlockSpec((chunk, few + 128), lambda i: (i, 0))]
        out_shape = [jax.ShapeDtypeStruct((many, few + 128), BF)]
        scratch = []
    else:
        shape = (many // (2 * blocks * rows), rows, blocks * few + 128)
        out_specs = [whole(shape)] * 2
        out_shape = [jax.ShapeDtypeStruct(shape, BF)] * 2
        scratch = [pltpu.VMEM((few, 128), F32)]
    return pl.pallas_call(
        partial(outer_tall_body, rows=rows, blocks=blocks, bits=bits),
        grid=(many // chunk,),
        in_specs=[
            pl.BlockSpec((length, chunk), lambda i: (0, i)),
            whole((length, few)),
            pl.BlockSpec((ROW_GROUP, chunk), lambda i: (0, i)),
            whole(vec.shape),
        ],
        out_specs=out_specs,
        out_shape=out_shape,
        scratch_shapes=scratch,
        compiler_params=params(1),
        cost_estimate=cost(2 * length * many * few, 2 * length * (many + few) + 2 * many * few),
        name="outer_tall",
    )(left, right, side, vec)


def outer_wide_body(left_ref, right_ref, *outs, rows, bits):
    lay_out(dot(left_ref[0], right_ref[...]), outs, slice(None), rows, bits)


def outer_wide(left, right, rows, bits):
    _, few, length = left.shape
    columns = right.shape[1]
    steps = columns // few
    _, out_shape = laid_out(few, columns, rows, bits)
    if bits is None:
        out_specs = [pl.BlockSpec((few, few), lambda i: (0, i))]
    else:
        out_specs = [pl.BlockSpec((few // (2 * rows), rows, few), lambda i: (0, 0, i))] * 2
    return pl.pallas_call(
        partial(outer_wide_body, rows=rows, bits=bits),
        grid=(steps,),
        in_specs=[
            pl.BlockSpec((1, few, length), lambda i: (i // (steps - 1), 0, 0)),
            pl.BlockSpec((length, few), lambda i: (0, i)),
        ],
        out_specs=out_specs,
        out_shape=out_shape,
        compiler_params=params(1),
        cost_estimate=cost(
            2 * length * few * columns, 2 * length * (2 * few + columns) + 2 * few * columns
        ),
        name="outer_wide",
    )(left, right)


def outer_merged_body(left_ref, w_ref, extra_ref, *refs, pieces, rows, bits):
    right_refs = refs[:pieces]
    outs = refs[pieces:-1]
    side_ref = refs[-1]
    step = pl.program_id(0)
    width = left_ref.shape[0]
    rights = [ref[0] for ref in right_refs]
    right = rights[0] if pieces == 1 else jnp.concatenate(rights, axis=1)
    z_grad = dot(left_ref[...], right)
    total = jnp.sum(fold_rows(right.astype(F32)), axis=0, keepdims=True)
    gain = extra_ref[:, 0:1].astype(F32)
    shift = extra_ref[:, 1:2].astype(F32)
    cols = pl.ds(pl.multiple_of(step * width, 128), width)
    lay_out(gain * z_grad + shift * total, outs, cols, rows, bits)
    w = w_ref[...].astype(F32)
    gain_grad = jnp.sum(w * z_grad, axis=1, keepdims=True)
    shift_grad = jnp.sum(w * total, axis=1, keepdims=True)
    turned = jnp.transpose(
        jnp.concatenate([total, jnp.zeros((127, width), F32)], axis=0)
    )[:, :1]
    lane = lax.broadcasted_iota(jnp.int32, (width, 128), 1)
    zero = jnp.zeros((), F32)
    bias_lane = jnp.where(step == 0, 2, jnp.where(step == 1, 4, 3))
    side = (
        jnp.where(lane == 0, gain_grad, zero)
        + jnp.where(lane == 1, shift_grad, zero)
        + jnp.where(lane == bias_lane, turned, zero)
    )

    @pl.when(step == 0)
    def _():
        side_ref[...] = side

    @pl.when(step > 0)
    def _():
        side_ref[...] += side

    @pl.when(step == 2)
    def _():
        lay_out(side_ref[...], outs, slice(3 * width, 3 * width + 128), rows, bits)


def outer_merged(left, weight, grads, rows, bits):
    few, length = left.shape
    out_specs, out_shape = laid_out(few, 3 * few + 128, rows, bits)
    return pl.pallas_call(
        partial(outer_merged_body, pieces=len(grads), rows=rows, bits=bits),
        grid=(3,),
        in_specs=[
            whole(left.shape),
            pl.BlockSpec((few, few), lambda i: (0, i)),
            pl.BlockSpec((few, 128), lambda i: (0, 3 * few // 128)),
        ]
        + [pl.BlockSpec((1, length, grad.shape[2]), lambda i: (i, 0, 0)) for grad in grads],
        out_specs=out_specs,
        out_shape=out_shape,
        scratch_shapes=[pltpu.VMEM((few, 128), F32)],
        compiler_params=params(1),
        cost_estimate=cost(6 * length * few * few, 8 * length * few + 12 * few * few),
        name="outer_merged",
    )(left, weight, weight, *grads)


def added(left, right):
    return (left.astype(F32) + right.astype(F32)).astype(BF)


def collect_plain(grads):
    total = lax.psum_scatter(grads, ("dp", "blk"), scatter_dimension=0, tiled=True)
    return total.astype(F32)


def halved(held, came):
    half = held.shape[0] // 2
    return added(held[:half], came[:half]), added(held[half:], came[half:])


def unproject_body(*refs, pieces):
    part_refs = refs[:pieces]
    w_ref, x_ref, vecs_ref, gm_ref, tg_ref = refs[pieces:]
    width = x_ref.shape[1]

    def first(tile):
        grads = [ref[k, tile, :] for k in range(3) for ref in part_refs]
        return dot(jnp.concatenate(grads, axis=1), w_ref[:, : 3 * width], NT)

    tiles = tiles_of(x_ref.shape[0], 320)
    ahead = first(tiles[0])
    for index, tile in enumerate(tiles):
        u = ahead
        if index + 1 < len(tiles):
            ahead = first(tiles[index + 1])
        z, scale = normed(x_ref[tile, :].astype(F32))
        back = norm_back(u, vecs_ref[0:1, :], z, scale)
        tg_ref[tile, :] = (gm_ref[tile, :] + back).astype(BF)


def unproject(grads, weight, x, vecs, gm):
    rows, width = x.shape
    tile = 640 if rows % 640 == 0 else rows
    row = lambda cols: pl.BlockSpec((tile, cols), lambda i: (i, 0))
    return pl.pallas_call(
        partial(unproject_body, pieces=len(grads)),
        grid=(rows // tile,),
        in_specs=[pl.BlockSpec((3, tile, grad.shape[2]), lambda i: (0, i, 0)) for grad in grads]
        + [whole(weight.shape), row(width), whole(vecs.shape), row(width)],
        out_specs=row(width),
        out_shape=jax.ShapeDtypeStruct((rows, width), BF),
        compiler_params=params(1),
        cost_estimate=cost(6 * rows * width * width, 2 * rows * width * 8 + 6 * width * width),
        name="unproject",
    )(*grads, weight, x, vecs, gm)


def pad_rows(values, rows):
    return jnp.pad(values, ((0, 0), (0, rows - values.shape[1]), (0, 0)))


def trade_clips(values):
    if lax.axis_size("blk") != 2:
        return lax.all_to_all(values, "blk", 0, 1, tiled=True)
    clips, rows, width = values.shape
    core = lax.axis_index("blk")
    pairs = values.reshape(2, clips // 2, rows, width)
    low, high = pairs[0], pairs[1]
    mine = jnp.where(core == 0, low, high)
    other = sibling(jnp.where(core == 0, high, low))
    return jnp.concatenate(
        [jnp.where(core == 0, mine, other), jnp.where(core == 0, other, mine)], axis=1
    )


def trade_away(values):
    core = lax.axis_index("blk")
    half = values.shape[1] // 2
    low, high = values[:, :half], values[:, half:]
    return jnp.where(core == 0, low, high), jnp.where(core == 0, high, low)


def trade_home(mine, other):
    core = lax.axis_index("blk")
    return jnp.concatenate(
        [jnp.where(core == 0, mine, other), jnp.where(core == 0, other, mine)], axis=0
    )


def trade_back(values):
    if lax.axis_size("blk") != 2:
        return lax.all_to_all(values, "blk", 1, 0, tiled=True)
    mine, away = trade_away(values)
    return trade_home(mine, sibling(away))


def key_mask(counts, cycle, rows_dev, rows_pad):
    position = jnp.arange(cycle * rows_pad, dtype=jnp.int32)
    block = position // rows_pad
    offset = position % rows_pad
    column = block * ((rows_dev - 2) // FREQ) + (offset - 2) // FREQ
    seen = jnp.where(
        (offset < 2)[None, :], (block == 0)[None, :], column[None, :] < counts[:, None]
    ) & (offset < rows_dev)[None, :]
    lane = jnp.arange(LANES, dtype=jnp.int32)
    return jnp.where(seen[:, :, None] | (lane > 0)[None, None, :], 0.0, NEGATIVE).astype(BF)


GROUPS = ((0, 1), (1, 3), (4, 2))


def local(
    tokens, counts, attend_gain, attend_shift, merged_weight, query_bias, value_bias,
    output_weight, output_bias, feed_gain, feed_shift, expand_weight, expand_bias,
    shrink_weight, shrink_bias, cotangent,
):
    clips, rows_dev, width = tokens.shape
    chips, cycle = lax.axis_size("dp"), lax.axis_size("blk")
    quick = quick_mesh({"dp": chips, "blk": cycle})
    rows_pad = -(-rows_dev // 16) * 16
    traded = clips % cycle == 0
    weight_rows = merged_weight.shape[0]
    tall_rows = shrink_weight.shape[0]
    hidden_width = expand_weight.shape[1]
    devices = chips * cycle
    core = lax.axis_index("blk")
    blocks = tall_rows // weight_rows
    vectors = [
        vector.reshape(1, -1)
        for vector in (
            attend_gain, attend_shift, query_bias, value_bias,
            output_bias, feed_gain, feed_shift, shrink_bias, expand_bias,
        )
    ]
    wide_cols = hidden_width + width
    if quick:
        first_pack, rest = pack(
            merged_weight, expand_weight, output_weight, shrink_weight, vectors
        )
        held_first = grow(first_pack[None], 3)
        held_first = grow(held_first, 2)
        rest = lax.all_gather(rest, ("dp", "blk"), axis=0)
        wide = Gathered(
            [rest],
            (devices, weight_rows, wide_cols),
            True,
            lambda refs, target: [(refs[0].at[:, :, :wide_cols], target)],
        )
        tall = Gathered(
            [rest],
            (devices, blocks, weight_rows, width),
            True,
            lambda refs, target: [
                (refs[0].at[:, :, pl.ds(wide_cols + k * width, width)], target.at[:, k])
                for k in range(blocks)
            ],
        )
        cut = first_pack.shape[1] // 2
        one = grow(held_first[:, :, :cut], 0)
        two = grow(held_first[:, :, cut:], 1)
    else:
        gather = lambda block: plain(lax.all_gather(block, ("dp", "blk"), axis=0, tiled=True))
        vec_cols = jnp.concatenate(vectors, axis=1).reshape(-1, weight_rows).T
        vec_cols = jnp.pad(vec_cols, ((0, 0), (0, VEC_COLS - vec_cols.shape[1])))
        merged_full = gather(jnp.concatenate([merged_weight, vec_cols], axis=1))
        wide = gather(jnp.concatenate([expand_weight, output_weight], axis=1))
        tall = gather(shrink_weight)
    if quick:
        x = trade_clips(pad_rows(tokens, rows_pad))
        one = grow(one, 1, x)
        two = grow(two, 0, x)
        g = trade_clips(pad_rows(after(cotangent, one, two), rows_pad))
        merged_full = gathered_first(one, two, weight_rows)
    else:
        x = pad_rows(tokens, rows_pad)
        g = pad_rows(cotangent, rows_pad)
        if traded:
            x = trade_clips(x)
            g = trade_clips(g)
    held = clips // cycle if traded else clips
    own_counts = lax.dynamic_slice_in_dim(counts, core * held, held) if traded else counts
    queries = x.shape[1]
    total = held * queries
    x = x.reshape(total, width)
    g = g.reshape(total, width)
    mask = key_mask(own_counts, cycle, rows_dev, rows_pad)

    z_turned, merged, weight_flat, vecs = project(x, merged_full)
    weight_flat = weight_flat.reshape(devices * weight_rows, -1)
    bias_row = (
        vecs[8 : 8 + blocks].reshape(blocks, devices, weight_rows).transpose(1, 0, 2)
    ).reshape(1, hidden_width)
    merged = merged.reshape(held, queries, 3 * width)
    if traded:
        keys, key_base = merged, PAIRS
    else:
        keys = lax.all_gather(merged[:, :, width:], "blk", axis=1, tiled=True)
        key_base = 0
    mixture, sums = attend(merged, keys, key_base, mask)
    mixtures = [mixture.reshape(total, width)]
    (
        result, hidden, rights, grad_middle, lefts, grad_attended, delta, feed_vec, expand_vec,
    ) = feed(x, g, mixtures, wide, tall, vecs, bias_row)

    def home(values):
        values = values.reshape(held, queries, width)
        if traded:
            values = trade_back(values)
        return values[:, :rows_dev]

    bits = BITS_FIRST if quick else None
    wide_grad = outer_wide(lefts, rights, weight_rows, bits)
    delta = delta.reshape(PAIRS * ROW_GROUP, held, queries).transpose(1, 0, 2)
    grad_heads = grad_attended.reshape(held, queries, width)
    back = partial(attend_back, merged, keys, key_base)
    if quick:
        wide_keep, wide_send = wide_grad
        (wide_came,), (tall_keep, tall_send) = beside(
            [(wide_send, sibling)],
            lambda rows: outer_tall(
                rows, g, expand_vec, feed_vec, weight_rows, blocks, BITS_SECOND
            ),
            hidden,
        )
        wide_kept, wide_away = halved(wide_keep, wide_came)

        def back_group(index):
            first, count = GROUPS[index]
            return lambda rows: back(rows, mask, sums, delta, first, count)

        grads = []
        (tall_came,), part = beside(
            [(tall_send, sibling)], back_group(0), after(grad_heads, wide_kept, wide_away)
        )
        grads += part
        tall_kept, tall_away = halved(tall_keep, tall_came)
        for index, bit in ((1, 1), (2, 0)):
            (wide_came, tall_came), part = beside(
                [(wide_away, over(bit)), (tall_away, over(1 - bit))],
                back_group(index),
                after(grad_heads, grads[-1]),
            )
            grads += part
            if index == 1:
                wide_kept, wide_away = halved(wide_kept, wide_came)
                tall_kept, tall_away = halved(tall_kept, tall_came)
        grads = [
            part.transpose(1, 0, 2, 3).reshape(3, total, part.shape[3]) for part in grads
        ]
        late_kept, late_away = (
            jnp.concatenate(pair, axis=2)
            for pair in zip(halved(wide_kept, wide_came), halved(tall_kept, tall_came))
        )
        (late_came,), (merged_keep, merged_send) = beside(
            [(late_away, over(2))],
            lambda rows: outer_merged(rows, weight_flat, grads, weight_rows, bits),
            z_turned,
        )
        result_rows = after(result, merged_send).reshape(held, queries, width)
        result_kept, result_away = trade_away(result_rows)
        result_came = sibling(result_away)
        late_kept, late_away = halved(late_kept, late_came)
        merged_came = after(sibling(merged_send), late_away)
        merged_keep = merged_keep.reshape(2, 2, chips // 4, weight_rows, -1)
        merged_came = merged_came.reshape(merged_keep.shape)
        cut = merged_keep.shape[-1] // 256 * 128
        one = [added(merged_keep[k, ..., :cut], merged_came[k, ..., :cut]) for k in range(2)]
        two = [added(merged_keep[:, k, ..., cut:], merged_came[:, k, ..., cut:]) for k in range(2)]
        late_came = swap_bit(late_away, 3)
        (one_came, two_came), (tokens_grad,) = beside(
            [(one[1], over(1)), (two[1], over(0))],
            lambda rows: [unproject(grads, weight_flat, rows, vecs, grad_middle)],
            after(x, late_away),
        )
        one = [added(one[0][k], one_came[k]) for k in range(2)]
        two = [added(two[0][k], two_came[k]) for k in range(2)]
        one_came = swap_bit(one[1], 0)
        two_came = swap_bit(two[1], 1)
        result_came = after(result_came, one[1], two[1])
        result_home = trade_home(result_kept, result_came)[:, :rows_dev]
        one = added(one[0], one_came)
        two = added(two[0], two_came)
        merged_held = jnp.concatenate([one, two], axis=-1)
        merged_kept, merged_away = merged_held[:2], merged_held[2:]
        late_came = after(late_came, merged_away)
        tokens_home = home(tokens_grad)
        merged_came = after(swap_bit(merged_away, 2), tokens_home)
        merged_kept, merged_away = halved(merged_kept, merged_came)
        full = lambda kept, came: (kept.astype(F32) + came.astype(F32))[0]
        merged_grad = full(merged_kept, swap_bit(merged_away, 3))
        late_grad = full(late_kept, late_came)
        wide_cols = wide_keep.shape[2]
        wide_grad = late_grad[:, :wide_cols]
        tall_grad = late_grad[:, wide_cols:]
        shrink_grad = jnp.concatenate(
            [tall_grad[:, k * width : (k + 1) * width] for k in range(blocks)], axis=0
        )
        extra = tall_grad[:, blocks * width :]
        expand_bias_grad = extra[:, :blocks].T.reshape(-1)
        vec_wide = extra[:, blocks : blocks + 4].T
    else:
        result_home = home(result)
        tall_grad = outer_tall(hidden, g, expand_vec, feed_vec, weight_rows, blocks, None)[0]
        tall_grad = collect_plain(tall_grad)
        shrink_grad = tall_grad[:, :width]
        expand_bias_grad = tall_grad[:, width]
        vec_wide = lax.psum_scatter(
            jnp.sum(feed_vec, axis=0).reshape(4, width), ("dp", "blk"), scatter_dimension=1,
            tiled=True,
        )
        columns = []
        for first, count in GROUPS:
            parts = back(grad_heads, mask, sums, delta, first, count)
            if traded:
                parts = [parts[0][:, k] for k in range(3)]
            else:
                scatter = partial(
                    lax.psum_scatter, axis_name="blk", scatter_dimension=1, tiled=True
                )
                parts = [parts[0], scatter(parts[1]), scatter(parts[2])]
            columns.append(jnp.stack(parts))
        grads = [jnp.concatenate(columns, axis=3).reshape(3, total, width)]
        merged_grad = outer_merged(z_turned, weight_flat, grads, weight_rows, None)
        tokens_home = home(unproject(grads, weight_flat, x, vecs, grad_middle))
        merged_grad = collect_plain(merged_grad[0])
        wide_grad = collect_plain(wide_grad[0])
    vec_merged = merged_grad[:, 3 * width :]

    return (
        result_home,
        tokens_home,
        vec_merged[:, 0],
        vec_merged[:, 1],
        merged_grad[:, : 3 * width],
        vec_merged[:, 2],
        vec_merged[:, 3],
        wide_grad[:, hidden_width : hidden_width + width],
        vec_wide[2],
        vec_wide[0],
        vec_wide[1],
        wide_grad[:, :hidden_width],
        expand_bias_grad,
        shrink_grad,
        vec_wide[3],
    )


def solution(mesh):
    rows = P("dp", "blk", None)
    vector = P(("dp", "blk"))
    matrix = P(("dp", "blk"), None)
    in_specs = (
        rows, P("dp"), vector, vector, matrix, vector, vector, matrix, vector, vector, vector,
        matrix, vector, matrix, vector, rows,
    )
    out_specs = (
        rows, rows, vector, vector, matrix, vector, vector, matrix, vector, vector, vector,
        matrix, vector, matrix, vector,
    )
    return jax.shard_map(local, mesh=mesh, in_specs=in_specs, out_specs=out_specs, check_vma=False)
```

```python
from functools import partial

import jax
import jax.numpy as jnp
from jax import lax
from jax.experimental import pallas as pl
from jax.experimental.pallas import tpu as pltpu
from jax.sharding import PartitionSpec as P

HEADS = 12
HEAD_DIM = 64
FREQ = 12
EPSILON = 1e-06
NEGATIVE = -1e30
LOG2E = 1.4426950408889634
PAIRS = HEADS // 2
LANES = 2 * HEAD_DIM
ROW_GROUP = 8
VMEM_BYTES = 60 * 1024 * 1024

BF = jnp.bfloat16
F32 = jnp.float32

NN = (((1,), (0,)), ((), ()))
NT = (((1,), (1,)), ((), ()))
TN = (((0,), (0,)), ((), ()))


def dot(left, right, dims=NN):
    return lax.dot_general(left, right, dims, preferred_element_type=F32)


def params(count):
    return pltpu.CompilerParams(
        dimension_semantics=("arbitrary",) * count, vmem_limit_bytes=VMEM_BYTES
    )


def whole(shape):
    return pl.BlockSpec(shape, lambda *_: (0,) * len(shape), pipeline_mode=pl.Buffered(1))


def cost(flops, bytes_accessed, transcendentals=0):
    return pl.CostEstimate(
        flops=int(flops), bytes_accessed=int(bytes_accessed), transcendentals=int(transcendentals)
    )


def normed(values):
    mean_row = jnp.mean(values, axis=-1, keepdims=True)
    centered = values - mean_row
    spread = jnp.mean(centered * centered, axis=-1, keepdims=True)
    scale = lax.rsqrt(spread + EPSILON)
    return centered * scale, scale


def norm_back(upstream, gain_row, z, scale):
    w = upstream * gain_row
    return scale * (
        w - jnp.mean(w, axis=-1, keepdims=True) - z * jnp.mean(w * z, axis=-1, keepdims=True)
    )


def fold_rows(values):
    rows, width = values.shape
    return jnp.sum(values.reshape(rows // ROW_GROUP, ROW_GROUP, width), axis=0)


def row_tile(rows):
    return 256 if rows % 256 == 0 else rows


def tiles_of(total, size):
    size = size if total % size == 0 else total
    return [slice(start, start + size) for start in range(0, total, size)]


BITS_FIRST = (3, 2, 0, 1)
BITS_SECOND = (3, 2, 1, 0)


def after(value, *others):
    return lax.optimization_barrier((value, *others))[0]


def quick_mesh(sizes):
    return sizes["dp"] == 16 and sizes["blk"] == 2


def swap_bit(block, bit):
    return lax.ppermute(block, "dp", [(i, i ^ (1 << bit)) for i in range(lax.axis_size("dp"))])


def sibling(block):
    return lax.ppermute(block, "blk", [(0, 1), (1, 0)])


def grow(held, bit, *others):
    return jnp.concatenate([held, after(swap_bit(held, bit), *others)], axis=0)


def relative(slot, bits):
    return sum(((slot >> k) & 1) << bit for k, bit in enumerate(bits))


def slot_of(offset, bits):
    return sum(((offset >> bit) & 1) << k for k, bit in enumerate(bits))


def beside(moves, kernel, operand):
    came = [route(array) for array, route in moves]
    results = kernel(after(operand, *[array for array, _ in moves]))
    joined = lax.optimization_barrier((*came, *results))
    return joined[: len(came)], joined[len(came) :]


def over(bit):
    return partial(swap_bit, bit=bit)


class Gathered:
    def __init__(self, arrays, shape, blocked, moves):
        self.arrays = arrays
        self.shape = shape
        self.blocked = blocked
        self.moves = moves

    @property
    def count(self):
        return len(self.arrays)

    def start(self, refs, target, sems):
        for index, (source, spot) in enumerate(self.moves(refs, target)):
            pltpu.make_async_copy(source, spot, sems.at[index]).start()

    def wait(self, refs, target, sems):
        for index, (source, spot) in enumerate(self.moves(refs, target)):
            pltpu.make_async_copy(source, spot, sems.at[index]).wait()

    def columns(self, ref, cols):
        if not self.blocked:
            return ref[:, cols]
        block = ref[:, :, cols]
        return block.reshape(block.shape[0] * block.shape[1], block.shape[2])

    def rows(self, ref, cols):
        if not self.blocked:
            return ref[cols, :]
        of_device = ref.shape[1] * ref.shape[2]
        block = ref[cols.start // of_device : cols.stop // of_device]
        return block.reshape(cols.stop - cols.start, block.shape[3])


def plain(array):
    return Gathered([array], array.shape, False, lambda refs, target: [(refs[0], target)])


def gathered_first(one, two, rows):
    slots, _, cols = one.shape
    arrays = [one, sibling(one), two, sibling(two)]

    def moves(refs, target):
        chip = lax.axis_index("dp")
        core = lax.axis_index("blk")
        pairs = []
        for index, ref in enumerate(refs):
            bits = BITS_FIRST if index < 2 else BITS_SECOND
            which = core if index % 2 == 0 else 1 - core
            place = pl.ds(index // 2 * cols, ref.shape[2])
            for slot in range(slots):
                owner = lax.bitwise_xor(chip, jnp.int32(relative(slot, bits)))
                pairs.append((ref.at[slot], target.at[owner * 2 + which, :, place]))
        return pairs

    return Gathered(arrays, (2 * slots, rows, cols + two.shape[2]), True, moves)


ANYWHERE = pl.BlockSpec(memory_space=pl.ANY)


VEC_COLS = 128


def pack_body(merged_ref, expand_ref, output_ref, tall_ref, *refs):
    vec_refs, first_ref, rest_ref = refs[:-2], refs[-2], refs[-1]
    rows, width = output_ref.shape
    vectors = jnp.concatenate(
        [
            ref[:, start : start + rows].astype(F32)
            for ref in vec_refs
            for start in range(0, ref.shape[1], rows)
        ],
        axis=0,
    )
    empty = jnp.zeros((16 - vectors.shape[0], rows), F32)
    vectors = jnp.concatenate([vectors, empty], axis=0).astype(BF)
    column = lax.broadcasted_iota(jnp.int32, (16, VEC_COLS), 1)
    line = lax.broadcasted_iota(jnp.int32, (16, VEC_COLS), 0)
    spread = jnp.where(column == line, 1.0, 0.0).astype(BF)
    first_ref[:, : 3 * width] = merged_ref[...]
    first_ref[:, 3 * width :] = dot(vectors, spread, TN).astype(BF)
    hidden_width = expand_ref.shape[1]
    rest_ref[:, :hidden_width] = expand_ref[...]
    rest_ref[:, hidden_width : hidden_width + width] = output_ref[...]
    for k in range(tall_ref.shape[0]):
        start = hidden_width + (1 + k) * width
        rest_ref[:, start : start + width] = tall_ref[k]


def pack(merged, expand, output, tall, vectors):
    rows, width = output.shape
    blocks = tall.shape[0] // rows
    first_cols = merged.shape[1] + VEC_COLS
    rest_cols = expand.shape[1] + (1 + blocks) * width
    return pl.pallas_call(
        pack_body,
        out_shape=[
            jax.ShapeDtypeStruct((rows, first_cols), BF),
            jax.ShapeDtypeStruct((rows, rest_cols), BF),
        ],
        compiler_params=pltpu.CompilerParams(vmem_limit_bytes=VMEM_BYTES),
        name="pack",
    )(merged, expand, output, tall.reshape(blocks, rows, width), *vectors)


def project_body(*refs, weight):
    count = weight.count
    x_ref = refs[0]
    sources = refs[1 : 1 + count]
    zt_ref, m_ref, w_ref, vec_ref, sems = refs[1 + count :]
    width = x_ref.shape[1]
    first = pl.program_id(0) == 0

    @pl.when(first)
    def _():
        weight.start(sources, w_ref, sems)

    z, _ = normed(x_ref[...].astype(F32))
    zt_ref[...] = jnp.transpose(z.astype(BF))

    @pl.when(first)
    def _():
        weight.wait(sources, w_ref, sems)
        extra = weight.columns(w_ref, slice(3 * width, 3 * width + 128))
        turned = jnp.transpose(extra.astype(F32))
        vec_ref[...] = turned[:16]

    a = (z * vec_ref[0:1, :] + vec_ref[1:2, :]).astype(BF)
    merged = dot(a, weight.columns(w_ref, slice(0, 3 * width)))
    query = (merged[:, :width] + vec_ref[2:3, :]) * (LOG2E * HEAD_DIM**-0.5)
    m_ref[:, :width] = query.astype(BF)
    m_ref[:, width : 2 * width] = merged[:, width : 2 * width].astype(BF)
    m_ref[:, 2 * width :] = (merged[:, 2 * width :] + vec_ref[3:4, :]).astype(BF)


def project(x, weight):
    rows, width = x.shape
    tile = row_tile(rows)
    row = lambda cols: pl.BlockSpec((tile, cols), lambda i: (i, 0))
    return pl.pallas_call(
        partial(project_body, weight=weight),
        grid=(rows // tile,),
        in_specs=[row(width)] + [ANYWHERE] * weight.count,
        out_specs=[
            pl.BlockSpec((width, tile), lambda i: (0, i)),
            row(3 * width), whole(weight.shape), whole((16, width)),
        ],
        out_shape=[
            jax.ShapeDtypeStruct((width, rows), BF),
            jax.ShapeDtypeStruct((rows, 3 * width), BF),
            jax.ShapeDtypeStruct(weight.shape, BF),
            jax.ShapeDtypeStruct((16, width), F32),
        ],
        scratch_shapes=[pltpu.SemaphoreType.DMA((64,))],
        compiler_params=params(1),
        cost_estimate=cost(6 * rows * width * width, 2 * rows * width * 5 + 6 * width * width),
        name="project",
    )(x, *weight.arrays)


def half_lanes(shape, head):
    return (lax.broadcasted_iota(jnp.int32, shape, 1) < HEAD_DIM) == (head == 0)


def only_head(values, head):
    return jnp.where(half_lanes(values.shape, head), values, jnp.zeros_like(values))


def ones_lane(rows):
    first = lax.broadcasted_iota(jnp.int32, (rows, LANES), 1) == 0
    return jnp.where(first, 1.0, 0.0).astype(BF)


AHEAD = 3


def attend_body(q_ref, k_ref, v_ref, mask_ref, o_ref, sum_ref, *, tile):
    keys = k_ref.shape[1]
    queries = q_ref.shape[1]
    ka = jnp.concatenate([k_ref[0], mask_ref[0]], axis=1)
    v_turned = jnp.transpose(v_ref[0])
    ones = jnp.ones((16, keys), BF)
    va = [
        jnp.concatenate([v_turned[:HEAD_DIM], ones], axis=0),
        jnp.concatenate([v_turned[HEAD_DIM:], ones], axis=0),
    ]
    one = ones_lane(tile)
    units = [(start, head) for start in range(0, queries, tile) for head in range(2)]

    def score(unit):
        start, head = unit
        q = only_head(q_ref[0, start : start + tile, :], head)
        return dot(ka, jnp.concatenate([q, one], axis=1), NT)

    ahead = [score(unit) for unit in units[:AHEAD]]
    parts = []
    for index, (start, head) in enumerate(units):
        if index + AHEAD < len(units):
            ahead.append(score(units[index + AHEAD]))
        s = ahead[index]
        top = jnp.max(s, axis=0, keepdims=True)
        p = jnp.exp2(s - top).astype(BF)
        mix = dot(va[head], p)
        total = mix[HEAD_DIM : HEAD_DIM + 1]
        parts.append(mix[:HEAD_DIM] / total)
        sum_ref[0, head : head + 1, start : start + tile] = top + jnp.log2(total)
        if head == 1:
            mixed = jnp.concatenate(parts, axis=0)
            o_ref[0, start : start + tile, :] = jnp.transpose(mixed)
            parts = []


def attend(merged, key_merged, key_base, mask, first=0, count=PAIRS):
    clips, queries, _ = merged.shape
    keys = key_merged.shape[1]
    tile = row_tile(queries)
    lanes = lambda rows, base: pl.BlockSpec((1, rows, LANES), lambda c, h: (c, 0, base + h))
    return pl.pallas_call(
        partial(attend_body, tile=tile),
        grid=(clips, count),
        in_specs=[
            lanes(queries, first),
            lanes(keys, key_base + first),
            lanes(keys, key_base + PAIRS + first),
            pl.BlockSpec((1, keys, LANES), lambda c, h: (c, 0, 0)),
        ],
        out_specs=[
            lanes(queries, 0),
            pl.BlockSpec((1, ROW_GROUP, queries), lambda c, h: (c, h, 0)),
        ],
        out_shape=[
            jax.ShapeDtypeStruct((clips, queries, count * LANES), F32),
            jax.ShapeDtypeStruct((clips, count * ROW_GROUP, queries), F32),
        ],
        compiler_params=params(2),
        cost_estimate=cost(
            clips * count * queries * keys * 2 * 4 * 256,
            clips * count * LANES * (2 * queries + 4 * keys + 4 * queries),
            clips * count * queries * keys * 2,
        ),
        name="attend",
    )(merged, key_merged, key_merged, mask)


def attend_back_body(
    q_ref, k_ref, v_ref, do_ref, mask_ref, sum_ref, delta_ref, *rest, tile
):
    dk_acc, dv_acc = rest[-2:]
    if len(rest) == 3:
        dq_ref, dk_ref, dv_ref = (rest[0].at[0, k] for k in range(3))
    else:
        dq_ref, dk_ref, dv_ref = (ref.at[0] for ref in rest[:3])
    queries = q_ref.shape[1]
    k = k_ref[0]
    v = v_ref[0]
    ka = jnp.concatenate([k, mask_ref[0]], axis=1)
    k_turned = jnp.transpose(k)
    one = ones_lane(tile)
    units = [(start, head) for start in range(0, queries, tile) for head in range(2)]

    def first(unit):
        start, head = unit
        rows = slice(start, start + tile)
        qm = only_head(q_ref[0, rows, :], head)
        dom = only_head(do_ref[0, rows, :], head)
        return qm, dom, dot(ka, jnp.concatenate([qm, one], axis=1), NT), dot(v, dom, NT)

    ahead = first(units[0])
    held = []
    for index, (start, head) in enumerate(units):
        rows = slice(start, start + tile)
        qm, dom, s, dp = ahead
        if index + 1 < len(units):
            ahead = first(units[index + 1])
        p = jnp.exp2(s - sum_ref[0, head : head + 1, rows])
        ds = (p * (dp - delta_ref[0, head : head + 1, rows])).astype(BF)
        dq = dot(k_turned[head * HEAD_DIM : (head + 1) * HEAD_DIM], ds)
        held.append((qm, dom, p.astype(BF), ds, dq))
        if head == 0:
            continue
        q_parts, do_parts, p_parts, ds_parts, dq_parts = zip(*held)
        held = []
        dq = jnp.transpose(jnp.concatenate(dq_parts, axis=0)) * (HEAD_DIM**-0.5)
        dq_ref[rows, :] = dq.astype(BF)
        dk = dot(jnp.concatenate(ds_parts, axis=1), jnp.concatenate(q_parts, axis=0))
        dv = dot(jnp.concatenate(p_parts, axis=1), jnp.concatenate(do_parts, axis=0))
        if start == 0:
            dk_acc[...] = dk
            dv_acc[...] = dv
        else:
            dk_acc[...] += dk
            dv_acc[...] += dv
    dk_ref[...] = (dk_acc[...] * (1.0 / LOG2E)).astype(BF)
    dv_ref[...] = dv_acc[...].astype(BF)


def attend_back(merged, key_merged, key_base, grad_out, mask, sums, delta, first=0, count=PAIRS):
    clips, queries, _ = merged.shape
    keys = key_merged.shape[1]
    tile = row_tile(queries)
    lanes = lambda rows, base: pl.BlockSpec((1, rows, LANES), lambda c, h: (c, 0, base + h))
    stat = lambda base: pl.BlockSpec((1, ROW_GROUP, queries), lambda c, h: (c, base + h, 0))
    columns = count * LANES
    if queries == keys:
        out_specs = [pl.BlockSpec((1, 3, keys, LANES), lambda c, h: (c, 0, 0, h))]
        out_shape = [jax.ShapeDtypeStruct((clips, 3, keys, columns), BF)]
    else:
        out_specs = [lanes(queries, 0), lanes(keys, 0), lanes(keys, 0)]
        out_shape = [
            jax.ShapeDtypeStruct((clips, queries, columns), BF),
            jax.ShapeDtypeStruct((clips, keys, columns), BF),
            jax.ShapeDtypeStruct((clips, keys, columns), BF),
        ]
    return pl.pallas_call(
        partial(attend_back_body, tile=tile),
        grid=(clips, count),
        in_specs=[
            lanes(queries, first),
            lanes(keys, key_base + first),
            lanes(keys, key_base + PAIRS + first),
            lanes(queries, first),
            pl.BlockSpec((1, keys, LANES), lambda c, h: (c, 0, 0)),
            stat(first),
            stat(first),
        ],
        out_specs=out_specs,
        out_shape=out_shape,
        scratch_shapes=[pltpu.VMEM((keys, LANES), F32), pltpu.VMEM((keys, LANES), F32)],
        compiler_params=params(2),
        cost_estimate=cost(
            clips * count * queries * keys * 2 * 9 * 256,
            clips * count * LANES * 2 * (3 * queries + 4 * keys),
            clips * count * queries * keys * 2,
        ),
        name="attend_back",
    )(merged, key_merged, key_merged, grad_out, mask, sums, delta)


ERF = (0.254829592, -0.284496736, 1.421413741, -1.453152027, 1.061405429)
ERF_P = 0.3275911


def gelu_both(u):
    bell = jnp.exp2(u * u * (-0.5 * LOG2E))
    t = 1.0 / (1.0 + (ERF_P * 0.5**0.5) * jnp.abs(u))
    series = ERF[4] * 0.5
    for term in ERF[3::-1]:
        series = series * t + term * 0.5
    tail = series * t * bell
    chance = jnp.where(u >= 0, 1.0 - tail, tail)
    return u * chance, chance + u * bell * 0.3989422804014327


def feed_body(*refs, chunk, mixes, wide, tall):
    x_ref, g_ref = refs[:2]
    o_refs = refs[2 : 2 + mixes]
    at = 2 + mixes
    wide_refs = refs[at : at + wide.count]
    at += wide.count
    tall_refs = refs[at : at + tall.count]
    at += tall.count
    (
        vecs_ref, be_ref, sel_ref,
        result_ref, h_ref, right_ref, gm_ref, left_ref, ga_ref, delta_ref, vec_ref,
        ebg_ref, wide_w, tall_w, wide_sems, tall_sems,
    ) = refs[at:]
    width = x_ref.shape[1]
    hidden_width = be_ref.shape[1]
    all_output = slice(hidden_width, hidden_width + width)

    @pl.when(pl.program_id(0) == 0)
    def _():
        wide.start(wide_refs, wide_w, wide_sems)
        tall.start(tall_refs, tall_w, tall_sems)
        vec_ref[...] = jnp.zeros_like(vec_ref)
        ebg_ref[...] = jnp.zeros_like(ebg_ref)
        wide.wait(wide_refs, wide_w, wide_sems)
        tall.wait(tall_refs, tall_w, tall_sems)

    o = jnp.concatenate([ref[...] for ref in o_refs], axis=1)
    att = o.astype(BF)
    left_ref[1] = jnp.transpose(att)
    middle = x_ref[...].astype(F32) + dot(att, wide.columns(wide_w, all_output)) + vecs_ref[4:5, :]
    z, scale = normed(middle)
    gain = vecs_ref[5:6, :]
    fi = (z * gain + vecs_ref[6:7, :]).astype(BF)
    left_ref[0] = jnp.transpose(fi)
    g = g_ref[...]
    out = middle + vecs_ref[7:8, :]
    u = jnp.zeros_like(middle)
    starts = list(range(0, hidden_width, chunk))

    def first(start):
        cols = slice(start, start + chunk)
        we = wide.columns(wide_w, cols)
        ws = tall.rows(tall_w, cols)
        return dot(fi, we) + be_ref[:, cols], dot(g, ws, NT), we, ws

    ahead = [first(start) for start in starts[:3]]
    for index, start in enumerate(starts):
        cols = slice(start, start + chunk)
        if index + 3 < len(starts):
            ahead.append(first(starts[index + 3]))
        pre, gh, we, ws = ahead[index]
        act, slope = gelu_both(pre)
        act = act.astype(BF)
        gp = (gh * slope).astype(BF)
        h_ref[:, cols] = act
        right_ref[:, cols] = gp
        ebg_ref[:, cols] += fold_rows(gp.astype(F32))
        out += dot(act, ws)
        u += dot(gp, we, NT)
    result_ref[...] = out.astype(BF)
    gf = g.astype(F32)
    gm = gf + norm_back(u, gain, z, scale)
    gm_ref[...] = gm
    gb = gm.astype(BF)
    right_ref[:, hidden_width:] = gb
    ga = dot(gb, wide.columns(wide_w, all_output), NT).astype(BF)
    ga_ref[...] = ga
    prod = ga.astype(F32) * o
    high = prod.astype(BF)
    low = (prod - high.astype(F32)).astype(BF)
    sel = sel_ref[...]
    delta_ref[...] = dot(sel, high, NT) + dot(sel, low, NT)
    vec_ref[:, :width] += fold_rows(u * z)
    vec_ref[:, width : 2 * width] += fold_rows(u)
    vec_ref[:, 2 * width : 3 * width] += fold_rows(gb.astype(F32))
    vec_ref[:, 3 * width :] += fold_rows(gf)


def feed(x, g, mixtures, wide, tall, vecs, be):
    rows, width = x.shape
    hidden_width = be.shape[1]
    tile = row_tile(rows)
    lane_head = jnp.arange(width)[None, :] // HEAD_DIM
    stat_row = jnp.arange(PAIRS * ROW_GROUP)[:, None]
    chosen = (stat_row // ROW_GROUP * 2 + stat_row % ROW_GROUP == lane_head) & (
        stat_row % ROW_GROUP < 2
    )
    select = chosen.astype(BF)
    row = lambda cols: pl.BlockSpec((tile, cols), lambda i: (i, 0))
    keep = lambda cols: pl.BlockSpec((ROW_GROUP, cols), lambda i: (0, 0))
    shape = jax.ShapeDtypeStruct
    return pl.pallas_call(
        partial(feed_body, chunk=768, mixes=len(mixtures), wide=wide, tall=tall),
        grid=(rows // tile,),
        in_specs=[
            row(width), row(width), *[row(mixture.shape[1]) for mixture in mixtures],
            *[ANYWHERE] * (wide.count + tall.count),
            whole(vecs.shape), whole((1, hidden_width)), whole(select.shape),
        ],
        out_specs=[
            row(width), row(hidden_width), row(hidden_width + width), row(width),
            pl.BlockSpec((2, width, tile), lambda i: (0, 0, i)), row(width),
            pl.BlockSpec((PAIRS * ROW_GROUP, tile), lambda i: (0, i)),
            keep(4 * width), keep(hidden_width),
        ],
        out_shape=[
            shape((rows, width), BF), shape((rows, hidden_width), BF),
            shape((rows, hidden_width + width), BF), shape((rows, width), F32),
            shape((2, width, rows), BF), shape((rows, width), BF),
            shape((PAIRS * ROW_GROUP, rows), F32),
            shape((ROW_GROUP, 4 * width), F32), shape((ROW_GROUP, hidden_width), F32),
        ],
        scratch_shapes=[
            pltpu.VMEM(wide.shape, BF), pltpu.VMEM(tall.shape, BF),
            pltpu.SemaphoreType.DMA((4,)), pltpu.SemaphoreType.DMA((4,)),
        ],
        compiler_params=params(1),
        cost_estimate=cost(
            rows * width * (4 * width + 8 * hidden_width),
            rows * (width * 20 + hidden_width * 4) + 2 * width * (width + 2 * hidden_width),
            rows * hidden_width * 2,
        ),
        name="feed",
    )(x, g, *mixtures, *wide.arrays, *tall.arrays, vecs, be, select)


def lay_out(value, outs, cols, rows, bits):
    if bits is None:
        outs[0][:, cols] = value.astype(BF)
        return
    keep_ref, send_ref = outs
    chip = lax.axis_index("dp")
    low_core = lax.axis_index("blk") == 0
    for owner in range(keep_ref.shape[0]):
        slot = slot_of(lax.bitwise_xor(chip, jnp.int32(owner)), bits)
        low = value[2 * owner * rows : (2 * owner + 1) * rows]
        high = value[(2 * owner + 1) * rows : (2 * owner + 2) * rows]
        keep_ref[slot, :, cols] = jnp.where(low_core, low, high).astype(BF)
        send_ref[slot, :, cols] = jnp.where(low_core, high, low).astype(BF)


def laid_out(few, columns, rows, bits):
    if bits is None:
        shapes = [(few, columns)]
    else:
        shapes = [(few // (2 * rows), rows, columns)] * 2
    return (
        [whole(shape) for shape in shapes],
        [jax.ShapeDtypeStruct(shape, BF) for shape in shapes],
    )


def outer_tall_body(left_ref, right_ref, side_ref, vec_ref, *outs, rows, blocks, bits):
    value = dot(left_ref[...], right_ref[...], TN)
    chunk, few = value.shape
    side = jnp.sum(side_ref[...], axis=0, keepdims=True)
    side = jnp.transpose(jnp.concatenate([side, jnp.zeros((127, chunk), F32)], axis=0))
    if bits is None:
        outs[0][:, :few] = value.astype(BF)
        outs[0][:, few:] = side.astype(BF)
        return
    keep_ref, send_ref, turned_ref = outs

    @pl.when(pl.program_id(0) == 0)
    def _():
        sums = [
            jnp.sum(vec_ref[:, k * few : (k + 1) * few], axis=0, keepdims=True) for k in range(4)
        ]
        empty = lambda count: jnp.zeros((count, few), F32)
        table = jnp.concatenate([empty(blocks), *sums, empty(124 - blocks)], axis=0)
        turned_ref[...] = jnp.transpose(table)

    side = jnp.broadcast_to(side[:, :1], (chunk, 128))
    chip = lax.axis_index("dp")
    low_core = lax.axis_index("blk") == 0
    lane = lax.broadcasted_iota(jnp.int32, (rows, 128), 1)
    of_device = blocks * rows
    chips = chunk // (2 * of_device)
    for index in range(chips):
        owner = pl.program_id(0) * chips + index
        slot = slot_of(lax.bitwise_xor(chip, owner), bits)
        pair = []
        for which in range(2):
            start = (2 * index + which) * of_device
            parts = [value[start + k * rows : start + (k + 1) * rows] for k in range(blocks)]
            first = pl.multiple_of((owner * 2 + which) * rows, 8)
            extra = turned_ref[pl.ds(first, rows), :]
            for k in range(blocks):
                column = side[start + k * rows : start + (k + 1) * rows]
                extra += jnp.where(lane == k, column, 0.0)
            pair.append(parts + [extra])
        for k, (low, high) in enumerate(zip(*pair)):
            cols = slice(k * few, k * few + low.shape[1])
            keep_ref[slot, :, cols] = jnp.where(low_core, low, high).astype(BF)
            send_ref[slot, :, cols] = jnp.where(low_core, high, low).astype(BF)


def outer_tall(left, right, side, vec, rows, blocks, bits):
    length, many = left.shape
    few = right.shape[1]
    chunk = 768
    if bits is None:
        out_specs = [pl.BlockSpec((chunk, few + 128), lambda i: (i, 0))]
        out_shape = [jax.ShapeDtypeStruct((many, few + 128), BF)]
        scratch = []
    else:
        shape = (many // (2 * blocks * rows), rows, blocks * few + 128)
        out_specs = [whole(shape)] * 2
        out_shape = [jax.ShapeDtypeStruct(shape, BF)] * 2
        scratch = [pltpu.VMEM((few, 128), F32)]
    return pl.pallas_call(
        partial(outer_tall_body, rows=rows, blocks=blocks, bits=bits),
        grid=(many // chunk,),
        in_specs=[
            pl.BlockSpec((length, chunk), lambda i: (0, i)),
            whole((length, few)),
            pl.BlockSpec((ROW_GROUP, chunk), lambda i: (0, i)),
            whole(vec.shape),
        ],
        out_specs=out_specs,
        out_shape=out_shape,
        scratch_shapes=scratch,
        compiler_params=params(1),
        cost_estimate=cost(2 * length * many * few, 2 * length * (many + few) + 2 * many * few),
        name="outer_tall",
    )(left, right, side, vec)


def outer_wide_body(left_ref, right_ref, *outs, rows, bits):
    lay_out(dot(left_ref[0], right_ref[...]), outs, slice(None), rows, bits)


def outer_wide(left, right, rows, bits):
    _, few, length = left.shape
    columns = right.shape[1]
    steps = columns // few
    _, out_shape = laid_out(few, columns, rows, bits)
    if bits is None:
        out_specs = [pl.BlockSpec((few, few), lambda i: (0, i))]
    else:
        out_specs = [pl.BlockSpec((few // (2 * rows), rows, few), lambda i: (0, 0, i))] * 2
    return pl.pallas_call(
        partial(outer_wide_body, rows=rows, bits=bits),
        grid=(steps,),
        in_specs=[
            pl.BlockSpec((1, few, length), lambda i: (i // (steps - 1), 0, 0)),
            pl.BlockSpec((length, few), lambda i: (0, i)),
        ],
        out_specs=out_specs,
        out_shape=out_shape,
        compiler_params=params(1),
        cost_estimate=cost(
            2 * length * few * columns, 2 * length * (2 * few + columns) + 2 * few * columns
        ),
        name="outer_wide",
    )(left, right)


def outer_merged_body(left_ref, w_ref, extra_ref, *refs, pieces, rows, bits):
    right_refs = refs[:pieces]
    outs = refs[pieces:-1]
    side_ref = refs[-1]
    step = pl.program_id(0)
    width = left_ref.shape[0]
    rights = [ref[0] for ref in right_refs]
    right = rights[0] if pieces == 1 else jnp.concatenate(rights, axis=1)
    z_grad = dot(left_ref[...], right)
    total = jnp.sum(fold_rows(right.astype(F32)), axis=0, keepdims=True)
    gain = extra_ref[:, 0:1].astype(F32)
    shift = extra_ref[:, 1:2].astype(F32)
    cols = pl.ds(pl.multiple_of(step * width, 128), width)
    lay_out(gain * z_grad + shift * total, outs, cols, rows, bits)
    w = w_ref[...].astype(F32)
    gain_grad = jnp.sum(w * z_grad, axis=1, keepdims=True)
    shift_grad = jnp.sum(w * total, axis=1, keepdims=True)
    turned = jnp.transpose(
        jnp.concatenate([total, jnp.zeros((127, width), F32)], axis=0)
    )[:, :1]
    lane = lax.broadcasted_iota(jnp.int32, (width, 128), 1)
    zero = jnp.zeros((), F32)
    bias_lane = jnp.where(step == 0, 2, jnp.where(step == 1, 4, 3))
    side = (
        jnp.where(lane == 0, gain_grad, zero)
        + jnp.where(lane == 1, shift_grad, zero)
        + jnp.where(lane == bias_lane, turned, zero)
    )

    @pl.when(step == 0)
    def _():
        side_ref[...] = side

    @pl.when(step > 0)
    def _():
        side_ref[...] += side

    @pl.when(step == 2)
    def _():
        lay_out(side_ref[...], outs, slice(3 * width, 3 * width + 128), rows, bits)


def outer_merged(left, weight, grads, rows, bits):
    few, length = left.shape
    out_specs, out_shape = laid_out(few, 3 * few + 128, rows, bits)
    return pl.pallas_call(
        partial(outer_merged_body, pieces=len(grads), rows=rows, bits=bits),
        grid=(3,),
        in_specs=[
            whole(left.shape),
            pl.BlockSpec((few, few), lambda i: (0, i)),
            pl.BlockSpec((few, 128), lambda i: (0, 3 * few // 128)),
        ]
        + [pl.BlockSpec((1, length, grad.shape[2]), lambda i: (i, 0, 0)) for grad in grads],
        out_specs=out_specs,
        out_shape=out_shape,
        scratch_shapes=[pltpu.VMEM((few, 128), F32)],
        compiler_params=params(1),
        cost_estimate=cost(6 * length * few * few, 8 * length * few + 12 * few * few),
        name="outer_merged",
    )(left, weight, weight, *grads)


def added(left, right):
    return (left.astype(F32) + right.astype(F32)).astype(BF)


def collect_plain(grads):
    total = lax.psum_scatter(grads, ("dp", "blk"), scatter_dimension=0, tiled=True)
    return total.astype(F32)


def halved(held, came):
    half = held.shape[0] // 2
    return added(held[:half], came[:half]), added(held[half:], came[half:])


def unproject_body(*refs, pieces):
    part_refs = refs[:pieces]
    w_ref, x_ref, vecs_ref, gm_ref, tg_ref = refs[pieces:]
    width = x_ref.shape[1]

    def first(tile):
        grads = [ref[k, tile, :] for k in range(3) for ref in part_refs]
        return dot(jnp.concatenate(grads, axis=1), w_ref[:, : 3 * width], NT)

    tiles = tiles_of(x_ref.shape[0], 320)
    ahead = first(tiles[0])
    for index, tile in enumerate(tiles):
        u = ahead
        if index + 1 < len(tiles):
            ahead = first(tiles[index + 1])
        z, scale = normed(x_ref[tile, :].astype(F32))
        back = norm_back(u, vecs_ref[0:1, :], z, scale)
        tg_ref[tile, :] = (gm_ref[tile, :] + back).astype(BF)


def unproject(grads, weight, x, vecs, gm):
    rows, width = x.shape
    tile = 640 if rows % 640 == 0 else rows
    row = lambda cols: pl.BlockSpec((tile, cols), lambda i: (i, 0))
    return pl.pallas_call(
        partial(unproject_body, pieces=len(grads)),
        grid=(rows // tile,),
        in_specs=[pl.BlockSpec((3, tile, grad.shape[2]), lambda i: (0, i, 0)) for grad in grads]
        + [whole(weight.shape), row(width), whole(vecs.shape), row(width)],
        out_specs=row(width),
        out_shape=jax.ShapeDtypeStruct((rows, width), BF),
        compiler_params=params(1),
        cost_estimate=cost(6 * rows * width * width, 2 * rows * width * 8 + 6 * width * width),
        name="unproject",
    )(*grads, weight, x, vecs, gm)


def pad_rows(values, rows):
    return jnp.pad(values, ((0, 0), (0, rows - values.shape[1]), (0, 0)))


def trade_clips(values):
    if lax.axis_size("blk") != 2:
        return lax.all_to_all(values, "blk", 0, 1, tiled=True)
    clips, rows, width = values.shape
    core = lax.axis_index("blk")
    pairs = values.reshape(2, clips // 2, rows, width)
    low, high = pairs[0], pairs[1]
    mine = jnp.where(core == 0, low, high)
    other = sibling(jnp.where(core == 0, high, low))
    return jnp.concatenate(
        [jnp.where(core == 0, mine, other), jnp.where(core == 0, other, mine)], axis=1
    )


def trade_away(values):
    core = lax.axis_index("blk")
    half = values.shape[1] // 2
    low, high = values[:, :half], values[:, half:]
    return jnp.where(core == 0, low, high), jnp.where(core == 0, high, low)


def trade_home(mine, other):
    core = lax.axis_index("blk")
    return jnp.concatenate(
        [jnp.where(core == 0, mine, other), jnp.where(core == 0, other, mine)], axis=0
    )


def trade_back(values):
    if lax.axis_size("blk") != 2:
        return lax.all_to_all(values, "blk", 1, 0, tiled=True)
    mine, away = trade_away(values)
    return trade_home(mine, sibling(away))


def key_mask(counts, cycle, rows_dev, rows_pad):
    position = jnp.arange(cycle * rows_pad, dtype=jnp.int32)
    block = position // rows_pad
    offset = position % rows_pad
    column = block * ((rows_dev - 2) // FREQ) + (offset - 2) // FREQ
    seen = jnp.where(
        (offset < 2)[None, :], (block == 0)[None, :], column[None, :] < counts[:, None]
    ) & (offset < rows_dev)[None, :]
    lane = jnp.arange(LANES, dtype=jnp.int32)
    return jnp.where(seen[:, :, None] | (lane > 0)[None, None, :], 0.0, NEGATIVE).astype(BF)


GROUPS = ((0, 1), (1, 3), (4, 2))


def local(
    tokens, counts, attend_gain, attend_shift, merged_weight, query_bias, value_bias,
    output_weight, output_bias, feed_gain, feed_shift, expand_weight, expand_bias,
    shrink_weight, shrink_bias, cotangent,
):
    clips, rows_dev, width = tokens.shape
    chips, cycle = lax.axis_size("dp"), lax.axis_size("blk")
    quick = quick_mesh({"dp": chips, "blk": cycle})
    rows_pad = -(-rows_dev // 16) * 16
    traded = clips % cycle == 0
    weight_rows = merged_weight.shape[0]
    tall_rows = shrink_weight.shape[0]
    hidden_width = expand_weight.shape[1]
    devices = chips * cycle
    core = lax.axis_index("blk")
    blocks = tall_rows // weight_rows
    vectors = [
        vector.reshape(1, -1)
        for vector in (
            attend_gain, attend_shift, query_bias, value_bias,
            output_bias, feed_gain, feed_shift, shrink_bias, expand_bias,
        )
    ]
    wide_cols = hidden_width + width
    if quick:
        first_pack, rest = pack(
            merged_weight, expand_weight, output_weight, shrink_weight, vectors
        )
        held_first = grow(first_pack[None], 3)
        held_first = grow(held_first, 2)
        rest = lax.all_gather(rest, ("dp", "blk"), axis=0)
        wide = Gathered(
            [rest],
            (devices, weight_rows, wide_cols),
            True,
            lambda refs, target: [(refs[0].at[:, :, :wide_cols], target)],
        )
        tall = Gathered(
            [rest],
            (devices, blocks, weight_rows, width),
            True,
            lambda refs, target: [
                (refs[0].at[:, :, pl.ds(wide_cols + k * width, width)], target.at[:, k])
                for k in range(blocks)
            ],
        )
        cut = first_pack.shape[1] // 256 * 128
        one = grow(held_first[:, :, :cut], 0)
        two = grow(held_first[:, :, cut:], 1)
    else:
        gather = lambda block: plain(lax.all_gather(block, ("dp", "blk"), axis=0, tiled=True))
        vec_cols = jnp.concatenate(vectors, axis=1).reshape(-1, weight_rows).T
        vec_cols = jnp.pad(vec_cols, ((0, 0), (0, VEC_COLS - vec_cols.shape[1])))
        merged_full = gather(jnp.concatenate([merged_weight, vec_cols], axis=1))
        wide = gather(jnp.concatenate([expand_weight, output_weight], axis=1))
        tall = gather(shrink_weight)
    if quick:
        x = trade_clips(pad_rows(tokens, rows_pad))
        one = grow(one, 1, x)
        two = grow(two, 0, x)
        g = trade_clips(pad_rows(after(cotangent, one, two), rows_pad))
        merged_full = gathered_first(one, two, weight_rows)
    else:
        x = pad_rows(tokens, rows_pad)
        g = pad_rows(cotangent, rows_pad)
        if traded:
            x = trade_clips(x)
            g = trade_clips(g)
    held = clips // cycle if traded else clips
    own_counts = lax.dynamic_slice_in_dim(counts, core * held, held) if traded else counts
    queries = x.shape[1]
    total = held * queries
    x = x.reshape(total, width)
    g = g.reshape(total, width)
    mask = key_mask(own_counts, cycle, rows_dev, rows_pad)

    z_turned, merged, weight_flat, vecs = project(x, merged_full)
    weight_flat = weight_flat.reshape(devices * weight_rows, -1)
    bias_row = (
        vecs[8 : 8 + blocks].reshape(blocks, devices, weight_rows).transpose(1, 0, 2)
    ).reshape(1, hidden_width)
    merged = merged.reshape(held, queries, 3 * width)
    if traded:
        keys, key_base = merged, PAIRS
    else:
        keys = lax.all_gather(merged[:, :, width:], "blk", axis=1, tiled=True)
        key_base = 0
    mixture, sums = attend(merged, keys, key_base, mask)
    mixtures = [mixture.reshape(total, width)]
    (
        result, hidden, rights, grad_middle, lefts, grad_attended, delta, feed_vec, expand_vec,
    ) = feed(x, g, mixtures, wide, tall, vecs, bias_row)

    def home(values):
        values = values.reshape(held, queries, width)
        if traded:
            values = trade_back(values)
        return values[:, :rows_dev]

    bits = BITS_FIRST if quick else None
    wide_grad = outer_wide(lefts, rights, weight_rows, bits)
    delta = delta.reshape(PAIRS * ROW_GROUP, held, queries).transpose(1, 0, 2)
    grad_heads = grad_attended.reshape(held, queries, width)
    back = partial(attend_back, merged, keys, key_base)
    if quick:
        wide_keep, wide_send = wide_grad
        (wide_came,), (tall_keep, tall_send) = beside(
            [(wide_send, sibling)],
            lambda rows: outer_tall(
                rows, g, expand_vec, feed_vec, weight_rows, blocks, BITS_SECOND
            ),
            hidden,
        )
        wide_kept, wide_away = halved(wide_keep, wide_came)

        def back_group(index):
            first, count = GROUPS[index]
            return lambda rows: back(rows, mask, sums, delta, first, count)

        grads = []
        (tall_came,), part = beside(
            [(tall_send, sibling)], back_group(0), after(grad_heads, wide_kept, wide_away)
        )
        grads += part
        tall_kept, tall_away = halved(tall_keep, tall_came)
        for index, bit in ((1, 1), (2, 0)):
            (wide_came, tall_came), part = beside(
                [(wide_away, over(bit)), (tall_away, over(1 - bit))],
                back_group(index),
                after(grad_heads, grads[-1]),
            )
            grads += part
            if index == 1:
                wide_kept, wide_away = halved(wide_kept, wide_came)
                tall_kept, tall_away = halved(tall_kept, tall_came)
        grads = [
            part.transpose(1, 0, 2, 3).reshape(3, total, part.shape[3]) for part in grads
        ]
        late_kept, late_away = (
            jnp.concatenate(pair, axis=2)
            for pair in zip(halved(wide_kept, wide_came), halved(tall_kept, tall_came))
        )
        (late_came,), (merged_keep, merged_send) = beside(
            [(late_away, over(2))],
            lambda rows: outer_merged(rows, weight_flat, grads, weight_rows, bits),
            z_turned,
        )
        result_rows = after(result, merged_send).reshape(held, queries, width)
        result_kept, result_away = trade_away(result_rows)
        result_came = sibling(result_away)
        late_kept, late_away = halved(late_kept, late_came)
        merged_came = after(sibling(merged_send), late_away)
        merged_keep = merged_keep.reshape(2, 2, chips // 4, weight_rows, -1)
        merged_came = merged_came.reshape(merged_keep.shape)
        cut = merged_keep.shape[-1] // 256 * 128
        one = [added(merged_keep[k, ..., :cut], merged_came[k, ..., :cut]) for k in range(2)]
        two = [added(merged_keep[:, k, ..., cut:], merged_came[:, k, ..., cut:]) for k in range(2)]
        late_came = swap_bit(late_away, 3)
        (one_came, two_came), (tokens_grad,) = beside(
            [(one[1], over(1)), (two[1], over(0))],
            lambda rows: [unproject(grads, weight_flat, rows, vecs, grad_middle)],
            after(x, late_away),
        )
        one = [added(one[0][k], one_came[k]) for k in range(2)]
        two = [added(two[0][k], two_came[k]) for k in range(2)]
        one_came = swap_bit(one[1], 0)
        two_came = swap_bit(two[1], 1)
        result_came = after(result_came, one[1], two[1])
        result_home = trade_home(result_kept, result_came)[:, :rows_dev]
        one = added(one[0], one_came)
        two = added(two[0], two_came)
        merged_held = jnp.concatenate([one, two], axis=-1)
        merged_kept, merged_away = merged_held[:2], merged_held[2:]
        late_came = after(late_came, merged_away)
        tokens_home = home(tokens_grad)
        merged_came = after(swap_bit(merged_away, 2), tokens_home)
        merged_kept, merged_away = halved(merged_kept, merged_came)
        full = lambda kept, came: (kept.astype(F32) + came.astype(F32))[0]
        merged_grad = full(merged_kept, swap_bit(merged_away, 3))
        late_grad = full(late_kept, late_came)
        wide_cols = wide_keep.shape[2]
        wide_grad = late_grad[:, :wide_cols]
        tall_grad = late_grad[:, wide_cols:]
        shrink_grad = jnp.concatenate(
            [tall_grad[:, k * width : (k + 1) * width] for k in range(blocks)], axis=0
        )
        extra = tall_grad[:, blocks * width :]
        expand_bias_grad = extra[:, :blocks].T.reshape(-1)
        vec_wide = extra[:, blocks : blocks + 4].T
    else:
        result_home = home(result)
        tall_grad = outer_tall(hidden, g, expand_vec, feed_vec, weight_rows, blocks, None)[0]
        tall_grad = collect_plain(tall_grad)
        shrink_grad = tall_grad[:, :width]
        expand_bias_grad = tall_grad[:, width]
        vec_wide = lax.psum_scatter(
            jnp.sum(feed_vec, axis=0).reshape(4, width), ("dp", "blk"), scatter_dimension=1,
            tiled=True,
        )
        columns = []
        for first, count in GROUPS:
            parts = back(grad_heads, mask, sums, delta, first, count)
            if traded:
                parts = [parts[0][:, k] for k in range(3)]
            else:
                scatter = partial(
                    lax.psum_scatter, axis_name="blk", scatter_dimension=1, tiled=True
                )
                parts = [parts[0], scatter(parts[1]), scatter(parts[2])]
            columns.append(jnp.stack(parts))
        grads = [jnp.concatenate(columns, axis=3).reshape(3, total, width)]
        merged_grad = outer_merged(z_turned, weight_flat, grads, weight_rows, None)
        tokens_home = home(unproject(grads, weight_flat, x, vecs, grad_middle))
        merged_grad = collect_plain(merged_grad[0])
        wide_grad = collect_plain(wide_grad[0])
    vec_merged = merged_grad[:, 3 * width :]

    return (
        result_home,
        tokens_home,
        vec_merged[:, 0],
        vec_merged[:, 1],
        merged_grad[:, : 3 * width],
        vec_merged[:, 2],
        vec_merged[:, 3],
        wide_grad[:, hidden_width : hidden_width + width],
        vec_wide[2],
        vec_wide[0],
        vec_wide[1],
        wide_grad[:, :hidden_width],
        expand_bias_grad,
        shrink_grad,
        vec_wide[3],
    )


def solution(mesh):
    rows = P("dp", "blk", None)
    vector = P(("dp", "blk"))
    matrix = P(("dp", "blk"), None)
    in_specs = (
        rows, P("dp"), vector, vector, matrix, vector, vector, matrix, vector, vector, vector,
        matrix, vector, matrix, vector, rows,
    )
    out_specs = (
        rows, rows, vector, vector, matrix, vector, vector, matrix, vector, vector, vector,
        matrix, vector, matrix, vector,
    )
    return jax.shard_map(local, mesh=mesh, in_specs=in_specs, out_specs=out_specs, check_vma=False)
```
